32 devices in a mesh: seq: 4 (over y, core), chan: 8 (over z, x).
Axes of the slice: x: 2, y: 2, z: 4, core: 2. Of those that a mesh axis runs over, the one named last changes fastest.
Arguments:
- query_rows: bfloat16 [512, 8192], P('seq', 'chan'), may hold values from -6 to 6
- key_rows: bfloat16 [512, 8192], P('seq', 'chan'), may hold values from -6 to 6
- value_rows: bfloat16 [512, 8192], P('seq', 'chan'), may hold values from -6 to 6
- short_taps: float32 [3, 3, 8192], P(None, None, 'chan'), may hold values from -3.5 to 3.5
- long_filter: float32 [512, 128], P('seq'), may hold values from -1.1 to 1.1
- cotangent: bfloat16 [512, 8192], P('seq', 'chan'), may hold values from -6 to 6
Outputs:
- hyena_out: bfloat16 [512, 8192], P('seq', 'chan')
- grad_query: bfloat16 [512, 8192], P('seq', 'chan')
- grad_key: bfloat16 [512, 8192], P('seq', 'chan')
- grad_value: bfloat16 [512, 8192], P('seq', 'chan')
- grad_filter: float32 [512, 128], P('seq')
The draws below stay inside these ranges and needn't reach their ends.
All inputs are finite; a program needn't handle non-finite values.
Results may differ from the reference program's by a relative error of at most 0.001.
Values may be sent and summed in bfloat16 or wider, within the bound.
No kernel may reach another device: no remote copies, remote signals or barrier semaphores. Data moves between devices by JAX's collectives and lax.ppermute only.
A program may use at most 64 MiB of HBM per device.

```python
import math
import jax
import jax.numpy as jnp
from jax import lax

D = 8192
FILTER_GROUPS = 128
KS = 3
TOKEN_LENGTH = 512


def draw_long_filter(key, part):
    random_subkeys = jax.random.split(key, 5)
    position = jnp.arange(TOKEN_LENGTH, dtype=jnp.float32)[:, None]
    slow_share = 0.5
    slow_pick = jax.random.uniform(random_subkeys[0], (FILTER_GROUPS,)) < slow_share
    slow_scale = jnp.exp(jax.random.uniform(random_subkeys[1], (FILTER_GROUPS,), minval=math.log(0.5 * TOKEN_LENGTH), maxval=math.log(4.0 * TOKEN_LENGTH)))
    fast_scale = jax.random.uniform(random_subkeys[2], (FILTER_GROUPS,), minval=30.0, maxval=50.0)
    horizon = jnp.where(slow_pick, slow_scale, fast_scale)
    spike_position = jax.random.randint(random_subkeys[3], (4, FILTER_GROUPS), 0, TOKEN_LENGTH)
    steps_elapsed = jnp.arange(TOKEN_LENGTH, dtype=jnp.int32)[None, :, None] >= spike_position[:, None, :]
    spike_events = jnp.sum(steps_elapsed.astype(jnp.float32), axis=0)
    survival_fraction = jnp.exp(spike_events * math.log(0.6))
    jitter = jax.random.truncated_normal(random_subkeys[4], -4.0, 4.0, (TOKEN_LENGTH, FILTER_GROUPS))
    amplitude = 1.0 / jnp.sqrt(0.5 * jnp.minimum(horizon, float(TOKEN_LENGTH)))
    return (jitter * jnp.exp(-position / horizon) * survival_fraction * amplitude).astype(jnp.float32)


def steps_of(key, extent, cuts, smallest, high):
    gain, own = 1.0, jax.random.fold_in(key, 6)
    for dim, shards_of in cuts:
        draws = jnp.exp(jax.random.uniform(jax.random.fold_in(own, dim), (shards_of,), jnp.float32, smallest / len(cuts), high / len(cuts)))
        gain = gain * jnp.repeat(draws, extent[dim] // shards_of).reshape([-1 if axis == dim else 1 for axis in range(len(extent))])
    return gain


def bell_draw(own_key, dims, deviation, most, pieces=(), kind=jnp.bfloat16):
    entries = deviation * jax.random.normal(own_key, dims, jnp.float32)
    if pieces:
        entries = entries * steps_of(own_key, dims, pieces, -0.22, 0.18)
    return jnp.clip(entries, -most, most).astype(kind)


def setup_inputs(seed: int = 0) -> dict:
    splits = jax.random.split(jax.random.key(seed), 7)
    query_rows = bell_draw(splits[0], (TOKEN_LENGTH, D), 1.0, 6.0, ((0, 4), (1, 8)))
    key_rows = bell_draw(splits[1], (TOKEN_LENGTH, D), 1.0, 6.0, ((0, 4), (1, 8)))
    value_rows = bell_draw(splits[2], (TOKEN_LENGTH, D), 1.0, 6.0, ((0, 4), (1, 8)))
    short_taps = bell_draw(splits[3], (3, KS, D), KS ** -0.5, 3.5, ((2, 8),), jnp.float32)
    long_filter = draw_long_filter(jax.random.fold_in(splits[6], 71), 0)
    cotangent = bell_draw(splits[5], (TOKEN_LENGTH, D), 1.0, 6.0, ((0, 4), (1, 8)))
    return {"query_rows": query_rows, "key_rows": key_rows, "value_rows": value_rows, "short_taps": short_taps, "long_filter": long_filter, "cotangent": cotangent}


def causal_taps(signal, tap_weights):
    summed = tap_weights[0] * signal
    for shift_by in range(1, tap_weights.shape[0]):
        delayed = jnp.concatenate([jnp.zeros((shift_by, signal.shape[1]), signal.dtype), signal[:-shift_by]], axis=0)
        summed = summed + tap_weights[shift_by] * delayed
    return summed


def anticausal_taps(signal, tap_weights):
    summed = tap_weights[0] * signal
    for shift_by in range(1, tap_weights.shape[0]):
        advanced = jnp.concatenate([signal[shift_by:], jnp.zeros((shift_by, signal.shape[1]), signal.dtype)], axis=0)
        summed = summed + tap_weights[shift_by] * advanced
    return summed


def reference(query_rows, key_rows, value_rows, short_taps, long_filter, cotangent):
    width_block = math.gcd(D, FILTER_GROUPS * max(1, 1024 // FILTER_GROUPS))
    block_count = D // width_block
    padded_len = 2 * TOKEN_LENGTH

    def one_block(filter_sum, block_id):
        first_col = block_id * width_block

        def columns_of(source):
            return lax.dynamic_slice_in_dim(source, first_col, width_block, source.ndim - 1)

        taps_block = columns_of(short_taps)
        query_conv = causal_taps(columns_of(query_rows).astype(jnp.float32), taps_block[0])
        key_conv = causal_taps(columns_of(key_rows).astype(jnp.float32), taps_block[1])
        value_conv = causal_taps(columns_of(value_rows).astype(jnp.float32), taps_block[2])
        gated_rows = key_conv * value_conv
        filter_wide = jnp.tile(long_filter, (1, width_block // FILTER_GROUPS))
        gated_spec = jnp.fft.rfft(gated_rows, n=padded_len, axis=0)
        filter_spec = jnp.fft.rfft(filter_wide, n=padded_len, axis=0)
        long_conv = jnp.fft.irfft(gated_spec * filter_spec, n=padded_len, axis=0)[:TOKEN_LENGTH]
        hyena_out = (query_conv * long_conv).astype(jnp.bfloat16)
        incoming = columns_of(cotangent).astype(jnp.float32)
        conv_grad = incoming * query_conv
        query_grad = incoming * long_conv
        grad_spec = jnp.fft.rfft(conv_grad, n=padded_len, axis=0)
        gated_grad = jnp.fft.irfft(jnp.conj(filter_spec) * grad_spec, n=padded_len, axis=0)[:TOKEN_LENGTH]
        filter_grad = jnp.fft.irfft(jnp.conj(gated_spec) * grad_spec, n=padded_len, axis=0)[:TOKEN_LENGTH]
        filter_sum = filter_sum + filter_grad.reshape(TOKEN_LENGTH, width_block // FILTER_GROUPS, FILTER_GROUPS).sum(axis=1)
        grad_query = anticausal_taps(query_grad, taps_block[0]).astype(jnp.bfloat16)
        grad_key = anticausal_taps(gated_grad * value_conv, taps_block[1]).astype(jnp.bfloat16)
        grad_value = anticausal_taps(gated_grad * key_conv, taps_block[2]).astype(jnp.bfloat16)
        return filter_sum, (hyena_out, grad_query, grad_key, grad_value)

    initial = jnp.zeros((TOKEN_LENGTH, FILTER_GROUPS), jnp.float32)
    filter_total, stacked = lax.scan(one_block, initial, jnp.arange(block_count, dtype=jnp.int32))

    def unstack(blocks_out):
        return jnp.moveaxis(blocks_out, 0, 1).reshape(TOKEN_LENGTH, D)

    return (unstack(stacked[0]), unstack(stacked[1]), unstack(stacked[2]), unstack(stacked[3]), filter_total)
```

```python
import functools

import jax
import jax.numpy as jnp
import ml_dtypes
import numpy as np
from jax import lax
from jax.experimental import pallas as pl
from jax.experimental.pallas import tpu as pltpu
from jax.sharding import PartitionSpec as P

F32 = jnp.float32
BF16 = jnp.bfloat16
EDGE = 8
HALO = 16
VMEM = pl.BlockSpec(memory_space=pltpu.VMEM)


def split_table(table):
    high = table.astype(ml_dtypes.bfloat16)
    low = (table - high.astype(np.float64)).astype(ml_dtypes.bfloat16)
    return high, low


def dft_tables(length):
    frequency = np.pi * (2 * np.arange(length) + 1) / (2 * length)
    into = frequency[:, None] * np.arange(length)[None, :]
    high, low = split_table(np.concatenate([np.cos(into), -np.sin(into)], axis=0))
    forward = np.concatenate([high, high, low], axis=1)
    back = np.arange(length + EDGE)[:, None] * frequency[None, :]
    high, low = split_table(np.concatenate([np.cos(back), -np.sin(back)], axis=1) / length)
    inverse = np.concatenate([high, high, low], axis=1)
    return jnp.asarray(forward), jnp.asarray(inverse)


def halves(values):
    high = values.astype(BF16)
    return high, (values - high.astype(F32)).astype(BF16)


def table_dot(table, values):
    high, low = halves(values)
    return jnp.dot(
        table, jnp.concatenate([high, low, high], axis=0), preferred_element_type=F32
    )


def pack_kernel(bits, q_ref, k_ref, v_ref, c_ref, filter_ref, *unit_refs):
    length, width = q_ref.shape
    groups = filter_ref.shape[1]
    rows = length * groups // width
    me = lax.axis_index("seq")
    filter_high, filter_low = halves(filter_ref[...])
    for bit, unit in zip(bits, unit_refs):
        first = 2 * length
        for tile in range(width // groups):
            lanes = slice(tile * groups, (tile + 1) * groups)
            unit[first : first + rows, lanes] = filter_high[tile * rows : (tile + 1) * rows]
            unit[first + rows : first + 2 * rows, lanes] = filter_low[
                tile * rows : (tile + 1) * rows
            ]
        first += 2 * rows
        low_side = (me // bit) % 2 == 0

        @pl.when(low_side)
        def _():
            unit[0:length] = k_ref[...]
            unit[length : 2 * length] = v_ref[...]
            unit[first : first + HALO] = q_ref[length - HALO : length]

        @pl.when(jnp.logical_not(low_side))
        def _():
            unit[0:length] = q_ref[...]
            unit[length : 2 * length] = c_ref[...]
            unit[first : first + HALO] = jnp.concatenate(
                [k_ref[0:HALO].astype(F32)[0:EDGE], v_ref[0:HALO].astype(F32)[0:EDGE]], axis=0
            ).astype(BF16)


def taps_of(rows_ref, slot, count, weights, lanes_out=None):
    total = weights[0:1] * rows_ref[slot, EDGE : EDGE + count]
    for shift in range(1, weights.shape[0]):
        total = total + weights[shift : shift + 1] * rows_ref[
            slot, EDGE - shift : EDGE - shift + count
        ]
    return total


def main_kernel(
    blocks,
    tile_width,
    q_ref,
    k_ref,
    v_ref,
    c_ref,
    taps_ref,
    filter_ref,
    forward_ref,
    inverse_ref,
    *refs,
):
    units = refs[: blocks - 1]
    out_ref, gq_ref, gk_ref, gv_ref, gf_ref = refs[blocks - 1 : blocks + 4]
    first_rows, second_rows, spectra, filter_rows, cross, own_spec, acc, fix, grads = refs[
        blocks + 4 :
    ]
    length, width = q_ref.shape
    groups = filter_ref.shape[1]
    rows = length * groups // width
    me = lax.axis_index("seq")
    forward = forward_ref[...]
    sign = jnp.where(lax.broadcasted_iota(jnp.int32, (length, groups), 0) % 2 == 0, 1.0, -1.0)

    for edge in (0, 1, blocks + 2):
        filter_rows[edge] = jnp.zeros((length, groups), F32)
    filter_rows[me + 2] = filter_ref[...]
    for index, unit in enumerate(units):
        pieces = []
        for tile in range(width // groups):
            lanes = slice(tile * groups, (tile + 1) * groups)
            pieces.append(
                unit[2 * length : 2 * length + rows, lanes].astype(F32)
                + unit[2 * length + rows : 2 * length + 2 * rows, lanes].astype(F32)
            )
        filter_rows[(me ^ (index + 1)) + 2] = jnp.concatenate(pieces, axis=0)
    previous = None
    for distance in range(blocks):
        own = table_dot(forward, filter_rows[distance + 2])
        if previous is None:
            spectra[distance] = own
        else:
            spectra[distance, 0:length] = own[0:length] - sign * previous[length:]
            spectra[distance, length:] = own[length:] + sign * previous[0:length]
        previous = own
    cross[...] = jnp.zeros(cross.shape, F32)

    def wide(values):
        return jnp.concatenate([values] * (tile_width // groups), axis=1)

    def filter_row(block, row):
        return wide(filter_rows[block + 2, pl.ds(row, 1)])

    def one_tile(step, carry):
        lanes = pl.ds(pl.multiple_of(step * tile_width, tile_width), tile_width)
        weights = [taps_ref[p, :, lanes] for p in range(3)]
        zero_edge = jnp.zeros((EDGE, tile_width), F32)

        first_rows[0, 0:EDGE] = zero_edge
        second_rows[0, 0:EDGE] = zero_edge
        first_rows[me + 1, 0:EDGE] = zero_edge

        @pl.when(me == blocks - 1)
        def _():
            for slot in (me, me + 1):
                first_rows[slot, EDGE + length :] = zero_edge
                second_rows[slot, EDGE + length :] = zero_edge

        def place(slot, one, two):
            first_rows[slot, EDGE : EDGE + length] = one
            second_rows[slot, EDGE : EDGE + length] = two

        def own_pair(slot, one, two):
            place(slot, one[:, lanes].astype(F32), two[:, lanes].astype(F32))

        own_pair(me, k_ref, v_ref)
        own_pair(me + 1, q_ref, c_ref)

        first_rows[me + 2, 0:EDGE] = first_rows[me + 1, length : length + EDGE]
        for index, unit in enumerate(units):
            other = me ^ (index + 1)
            lower = other < me
            slot = jnp.where(lower, other, other + 1)
            one = unit[0:length, lanes].astype(F32)
            two = unit[length : 2 * length, lanes].astype(F32)
            place(slot, one, two)
            first_rows[slot + 1, 0:EDGE] = one[length - EDGE :]
            second_rows[slot + 1, 0:EDGE] = two[length - EDGE :]
            edge = unit[2 * length + 2 * rows :, lanes].astype(F32)

            @pl.when(other == me + 1)
            def _():
                first_rows[me, EDGE + length :] = edge[0:EDGE]
                second_rows[me, EDGE + length :] = edge[EDGE:]
                first_rows[me + 1, EDGE + length :] = one[0:EDGE]
                second_rows[me + 1, EDGE + length :] = two[0:EDGE]

        for index, unit in enumerate(units):
            other = me ^ (index + 1)

            @pl.when(other == me - 1)
            def _():
                edge = unit[2 * length + 2 * rows :, lanes].astype(F32)
                first_rows[me + 1, 0:EDGE] = edge[EDGE:]

        fix[...] = jnp.zeros(fix.shape, F32)

        def filter_spec(distance):
            return (
                wide(spectra[distance, 0:length]),
                wide(spectra[distance, length:]),
            )

        def add_lower(distance, signal, spec, fresh):
            re, im = spec[0:length], spec[length:]
            h_re, h_im = filter_spec(distance)
            new_re = h_re * re - h_im * im
            new_im = h_re * im + h_im * re
            if fresh:
                acc[0, 0:length] = new_re
                acc[0, length:] = new_im
            else:
                acc[0, 0:length] += new_re
                acc[0, length:] += new_im
            c_re, c_im = own_spec[0:length], own_spec[length:]
            cross_re = re * c_re + im * c_im
            cross_im = re * c_im - im * c_re
            for tile in range(tile_width // groups):
                part = slice(tile * groups, (tile + 1) * groups)
                cross[distance, 0:length] += cross_re[:, part]
                cross[distance, length:] += cross_im[:, part]
            near = filter_row(distance + 1, 0) + filter_row(distance - 1, 0)
            far = filter_row(distance + 1, 1) + filter_row(distance - 1, 1)
            fix[0:1] += signal[0:1] * near
            fix[1:2] += signal[0:1] * far + signal[1:2] * near

        def add_upper(distance, signal, spec, fresh):
            re, im = spec[0:length], spec[length:]
            h_re, h_im = filter_spec(distance)
            new_re = h_re * re + h_im * im
            new_im = h_re * im - h_im * re
            if fresh:
                acc[1, 0:length] = new_re
                acc[1, length:] = new_im
            else:
                acc[1, 0:length] += new_re
                acc[1, length:] += new_im
            fix[EDGE + 1 : EDGE + 2] += signal[0:1] * (
                filter_row(distance - 2, length - 1) + filter_row(distance, length - 1)
            )

        count = length + EDGE
        query_conv = taps_of(first_rows, me + 1, count, weights[0])
        incoming = second_rows[me + 1, EDGE : EDGE + count]
        conv_grad = (query_conv * incoming)[0:length]
        own_spec[...] = table_dot(forward, conv_grad)
        add_upper(0, conv_grad, own_spec[...], True)
        key_conv = taps_of(first_rows, me, count, weights[1])
        value_conv = taps_of(second_rows, me, count, weights[2])
        gated = key_conv * value_conv
        add_lower(0, gated[0:length], table_dot(forward, gated[0:length]), True)
        after = gated[length : length + 2]
        zero_lag, one_lag = filter_row(0, 0), filter_row(0, 1)
        fix[0:1] += after[0:1] * zero_lag
        fix[1:2] += after[1:2] * zero_lag + after[0:1] * one_lag

        for index in range(blocks - 1):
            other = me ^ (index + 1)

            @pl.when(other < me)
            def _():
                signal = taps_of(first_rows, other, length, weights[1]) * taps_of(
                    second_rows, other, length, weights[2]
                )
                add_lower(me - other, signal, table_dot(forward, signal), False)

            @pl.when(other > me)
            def _():
                signal = (
                    taps_of(first_rows, other + 1, length, weights[0])
                    * second_rows[other + 1, EDGE : EDGE + length]
                )
                add_upper(other - me, signal, table_dot(forward, signal), False)

        inverse = inverse_ref[...]
        long_conv = table_dot(inverse, acc[0])
        gated_grad = table_dot(inverse, acc[1])
        out_ref[:, lanes] = (query_conv[0:length] * long_conv[0:length]).astype(BF16)
        inside = jnp.where(me < blocks - 1, 1.0, 0.0)
        conv_edge = long_conv[length:] + fix[0:EDGE]
        grad_edge = (gated_grad[length:] + fix[EDGE:]) * inside
        grads[0, 0:length] = incoming[0:length] * long_conv[0:length]
        grads[0, length:] = incoming[length:] * conv_edge
        grads[1, 0:length] = gated_grad[0:length] * value_conv[0:length]
        grads[1, length:] = grad_edge * value_conv[length:]
        grads[2, 0:length] = gated_grad[0:length] * key_conv[0:length]
        grads[2, length:] = grad_edge * key_conv[length:]
        for p, ref in enumerate((gq_ref, gk_ref, gv_ref)):
            total = weights[p][0:1] * grads[p, 0:length]
            for shift in range(1, weights[p].shape[0]):
                total = total + weights[p][shift : shift + 1] * grads[p, shift : shift + length]
            ref[:, lanes] = total.astype(BF16)
        return carry

    lax.fori_loop(0, width // tile_width, one_tile, 0)

    inverse = inverse_ref[0:length]
    for block in range(blocks):
        re, im = cross[block, 0:length], cross[block, length:]
        if block + 1 < blocks:
            re = re + sign * cross[block + 1, length:]
            im = im - sign * cross[block + 1, 0:length]
        gf_ref[block] = table_dot(inverse, jnp.concatenate([re, im], axis=0))


def per_device(query_rows, key_rows, value_rows, short_taps, long_filter, cotangent):
    length, width = query_rows.shape
    groups = long_filter.shape[1]
    blocks = lax.axis_size("seq")
    chans = lax.axis_size("chan")
    bits = []
    while 1 << len(bits) < blocks:
        bits.append(1 << len(bits))
    bits.reverse()
    forward, inverse = dft_tables(length)

    unit_shape = jax.ShapeDtypeStruct(
        (2 * length + 2 * (length * groups // width) + HALO, width), BF16
    )
    own_units = pl.pallas_call(
        functools.partial(pack_kernel, bits),
        out_shape=[unit_shape] * len(bits),
        in_specs=[VMEM] * 5,
        out_specs=[VMEM] * len(bits),
    )(query_rows, key_rows, value_rows, cotangent, long_filter)

    def swap(block, bit):
        return lax.ppermute(block, "seq", [(i, i ^ bit) for i in range(blocks)])

    units = {}
    for bit, own in zip(bits, own_units):
        arrived = {bit: swap(own, bit)}
        for index, block in units.items():
            arrived[index ^ bit] = swap(block, bit)
        units.update(arrived)
    units = [units[index] for index in range(1, blocks)]

    tile_width = min(width, 256)
    rows_out = jax.ShapeDtypeStruct((length, width), BF16)
    hyena_out, grad_query, grad_key, grad_value, partial = pl.pallas_call(
        functools.partial(main_kernel, blocks, tile_width),
        out_shape=[rows_out] * 4 + [jax.ShapeDtypeStruct((blocks, length, groups), F32)],
        in_specs=[VMEM] * (8 + blocks - 1),
        out_specs=[VMEM] * 5,
        scratch_shapes=[
            pltpu.VMEM((blocks + 2, length + 2 * EDGE, tile_width), F32),
            pltpu.VMEM((blocks + 2, length + 2 * EDGE, tile_width), F32),
            pltpu.VMEM((blocks, 2 * length, groups), F32),
            pltpu.VMEM((blocks + 3, length, groups), F32),
            pltpu.VMEM((blocks, 2 * length, groups), F32),
            pltpu.VMEM((2 * length, tile_width), F32),
            pltpu.VMEM((2, 2 * length, tile_width), F32),
            pltpu.VMEM((2 * EDGE, tile_width), F32),
            pltpu.VMEM((3, length + EDGE, tile_width), F32),
        ],
        compiler_params=pltpu.CompilerParams(vmem_limit_bytes=48 * 1024 * 1024),
    )(
        query_rows,
        key_rows,
        value_rows,
        cotangent,
        short_taps,
        long_filter,
        forward,
        inverse,
        *units,
    )

    summed = lax.all_to_all(partial, "seq", 0, 0, tiled=True).sum(axis=0)
    shares = summed.reshape(chans, length // chans, groups)
    share = lax.all_to_all(shares, "chan", 0, 0, tiled=True).sum(axis=0)
    spread = jnp.broadcast_to(share, shares.shape)
    grad_filter = lax.all_to_all(spread, "chan", 0, 0, tiled=True).reshape(length, groups)
    return (hyena_out, grad_query, grad_key, grad_value, grad_filter)


def solution(mesh):
    in_specs = (
        P("seq", "chan"),
        P("seq", "chan"),
        P("seq", "chan"),
        P(None, None, "chan"),
        P("seq", None),
        P("seq", "chan"),
    )
    out_specs = (
        P("seq", "chan"),
        P("seq", "chan"),
        P("seq", "chan"),
        P("seq", "chan"),
        P("seq", None),
    )
    return jax.shard_map(
        per_device, mesh=mesh, in_specs=in_specs, out_specs=out_specs, check_vma=False
    )
```

```python
import functools

import jax
import jax.numpy as jnp
import ml_dtypes
import numpy as np
from jax import lax
from jax.experimental import pallas as pl
from jax.experimental.pallas import tpu as pltpu
from jax.sharding import PartitionSpec as P

F32 = jnp.float32
BF16 = jnp.bfloat16
EDGE = 8
HALO = 16
VMEM = pl.BlockSpec(memory_space=pltpu.VMEM)


def split_table(table):
    high = table.astype(ml_dtypes.bfloat16)
    low = (table - high.astype(np.float64)).astype(ml_dtypes.bfloat16)
    return high, low


def dft_tables(length):
    frequency = np.pi * (2 * np.arange(length) + 1) / (2 * length)
    into = frequency[:, None] * np.arange(length)[None, :]
    high, low = split_table(np.concatenate([np.cos(into), -np.sin(into)], axis=0))
    forward = np.concatenate([high, high, low], axis=1)
    back = np.arange(length + EDGE)[:, None] * frequency[None, :]
    high, low = split_table(np.concatenate([np.cos(back), -np.sin(back)], axis=1) / length)
    inverse = np.concatenate([high, high, low], axis=1)
    return jnp.asarray(forward), jnp.asarray(inverse)


def halves(values):
    high = values.astype(BF16)
    return high, (values - high.astype(F32)).astype(BF16)


def table_dot(table, values):
    high, low = halves(values)
    return jnp.dot(
        table, jnp.concatenate([high, low, high], axis=0), preferred_element_type=F32
    )


def pack_kernel(bits, q_ref, k_ref, v_ref, c_ref, filter_ref, *unit_refs):
    length, width = q_ref.shape
    groups = filter_ref.shape[1]
    rows = length * groups // width
    me = lax.axis_index("seq")
    filter_high, filter_low = halves(filter_ref[...])
    for bit, unit in zip(bits, unit_refs):
        first = 2 * length
        for tile in range(width // groups):
            lanes = slice(tile * groups, (tile + 1) * groups)
            unit[first : first + rows, lanes] = filter_high[tile * rows : (tile + 1) * rows]
            unit[first + rows : first + 2 * rows, lanes] = filter_low[
                tile * rows : (tile + 1) * rows
            ]
        first += 2 * rows
        low_side = (me // bit) % 2 == 0

        @pl.when(low_side)
        def _():
            unit[0:length] = k_ref[...]
            unit[length : 2 * length] = v_ref[...]
            unit[first : first + HALO] = q_ref[length - HALO : length]

        @pl.when(jnp.logical_not(low_side))
        def _():
            unit[0:length] = q_ref[...]
            unit[length : 2 * length] = c_ref[...]
            unit[first : first + HALO] = jnp.concatenate(
                [k_ref[0:HALO].astype(F32)[0:EDGE], v_ref[0:HALO].astype(F32)[0:EDGE]], axis=0
            ).astype(BF16)


def taps_of(rows_ref, slot, count, weights, lanes_out=None):
    total = weights[0:1] * rows_ref[slot, EDGE : EDGE + count]
    for shift in range(1, weights.shape[0]):
        total = total + weights[shift : shift + 1] * rows_ref[
            slot, EDGE - shift : EDGE - shift + count
        ]
    return total


def main_kernel(
    blocks,
    tile_width,
    q_ref,
    k_ref,
    v_ref,
    c_ref,
    taps_ref,
    filter_ref,
    forward_ref,
    inverse_ref,
    *refs,
):
    units = refs[: blocks - 1]
    out_ref, gq_ref, gk_ref, gv_ref = refs[blocks - 1 : blocks + 3]
    gf_refs = refs[blocks + 3 : -9]
    first_rows, second_rows, spectra, filter_rows, cross, own_spec, acc, fix, grads = refs[-9:]
    length, width = q_ref.shape
    groups = filter_ref.shape[1]
    rows = length * groups // width
    me = lax.axis_index("seq")
    forward = forward_ref[...]
    sign = jnp.where(lax.broadcasted_iota(jnp.int32, (length, groups), 0) % 2 == 0, 1.0, -1.0)

    for edge in (0, 1, blocks + 2):
        filter_rows[edge] = jnp.zeros((length, groups), F32)
    filter_rows[me + 2] = filter_ref[...]
    for index, unit in enumerate(units):
        pieces = []
        for tile in range(width // groups):
            lanes = slice(tile * groups, (tile + 1) * groups)
            pieces.append(
                unit[2 * length : 2 * length + rows, lanes].astype(F32)
                + unit[2 * length + rows : 2 * length + 2 * rows, lanes].astype(F32)
            )
        filter_rows[(me ^ (index + 1)) + 2] = jnp.concatenate(pieces, axis=0)
    previous = None
    for distance in range(blocks):
        own = table_dot(forward, filter_rows[distance + 2])
        if previous is None:
            spectra[distance] = own
        else:
            spectra[distance, 0:length] = own[0:length] - sign * previous[length:]
            spectra[distance, length:] = own[length:] + sign * previous[0:length]
        previous = own
    cross[...] = jnp.zeros(cross.shape, F32)

    def wide(values):
        return jnp.concatenate([values] * (tile_width // groups), axis=1)

    def filter_row(block, row):
        return wide(filter_rows[block + 2, pl.ds(row, 1)])

    def one_tile(step, carry):
        lanes = pl.ds(pl.multiple_of(step * tile_width, tile_width), tile_width)
        weights = [taps_ref[p, :, lanes] for p in range(3)]
        zero_edge = jnp.zeros((EDGE, tile_width), F32)

        first_rows[0, 0:EDGE] = zero_edge
        second_rows[0, 0:EDGE] = zero_edge
        first_rows[me + 1, 0:EDGE] = zero_edge

        @pl.when(me == blocks - 1)
        def _():
            for slot in (me, me + 1):
                first_rows[slot, EDGE + length :] = zero_edge
                second_rows[slot, EDGE + length :] = zero_edge

        def place(slot, one, two):
            first_rows[slot, EDGE : EDGE + length] = one
            second_rows[slot, EDGE : EDGE + length] = two

        def own_pair(slot, one, two):
            place(slot, one[:, lanes].astype(F32), two[:, lanes].astype(F32))

        own_pair(me, k_ref, v_ref)
        own_pair(me + 1, q_ref, c_ref)

        first_rows[me + 2, 0:EDGE] = first_rows[me + 1, length : length + EDGE]
        for index, unit in enumerate(units):
            other = me ^ (index + 1)
            lower = other < me
            slot = jnp.where(lower, other, other + 1)
            one = unit[0:length, lanes].astype(F32)
            two = unit[length : 2 * length, lanes].astype(F32)
            place(slot, one, two)
            first_rows[slot + 1, 0:EDGE] = one[length - EDGE :]
            second_rows[slot + 1, 0:EDGE] = two[length - EDGE :]
            edge = unit[2 * length + 2 * rows :, lanes].astype(F32)

            @pl.when(other == me + 1)
            def _():
                first_rows[me, EDGE + length :] = edge[0:EDGE]
                second_rows[me, EDGE + length :] = edge[EDGE:]
                first_rows[me + 1, EDGE + length :] = one[0:EDGE]
                second_rows[me + 1, EDGE + length :] = two[0:EDGE]

        for index, unit in enumerate(units):
            other = me ^ (index + 1)

            @pl.when(other == me - 1)
            def _():
                edge = unit[2 * length + 2 * rows :, lanes].astype(F32)
                first_rows[me + 1, 0:EDGE] = edge[EDGE:]

        fix[...] = jnp.zeros(fix.shape, F32)

        def filter_spec(distance):
            return (
                wide(spectra[distance, 0:length]),
                wide(spectra[distance, length:]),
            )

        def add_lower(distance, signal, spec, fresh):
            re, im = spec[0:length], spec[length:]
            h_re, h_im = filter_spec(distance)
            new_re = h_re * re - h_im * im
            new_im = h_re * im + h_im * re
            if fresh:
                acc[0, 0:length] = new_re
                acc[0, length:] = new_im
            else:
                acc[0, 0:length] += new_re
                acc[0, length:] += new_im
            c_re, c_im = own_spec[0:length], own_spec[length:]
            cross_re = re * c_re + im * c_im
            cross_im = re * c_im - im * c_re
            for tile in range(tile_width // groups):
                part = slice(tile * groups, (tile + 1) * groups)
                cross[distance, 0:length] += cross_re[:, part]
                cross[distance, length:] += cross_im[:, part]
            near = filter_row(distance + 1, 0) + filter_row(distance - 1, 0)
            far = filter_row(distance + 1, 1) + filter_row(distance - 1, 1)
            fix[0:1] += signal[0:1] * near
            fix[1:2] += signal[0:1] * far + signal[1:2] * near

        def add_upper(distance, signal, spec, fresh):
            re, im = spec[0:length], spec[length:]
            h_re, h_im = filter_spec(distance)
            new_re = h_re * re + h_im * im
            new_im = h_re * im - h_im * re
            if fresh:
                acc[1, 0:length] = new_re
                acc[1, length:] = new_im
            else:
                acc[1, 0:length] += new_re
                acc[1, length:] += new_im
            fix[EDGE + 1 : EDGE + 2] += signal[0:1] * (
                filter_row(distance - 2, length - 1) + filter_row(distance, length - 1)
            )

        count = length + EDGE
        query_conv = taps_of(first_rows, me + 1, count, weights[0])
        incoming = second_rows[me + 1, EDGE : EDGE + count]
        conv_grad = (query_conv * incoming)[0:length]
        own_spec[...] = table_dot(forward, conv_grad)
        add_upper(0, conv_grad, own_spec[...], True)
        key_conv = taps_of(first_rows, me, count, weights[1])
        value_conv = taps_of(second_rows, me, count, weights[2])
        gated = key_conv * value_conv
        add_lower(0, gated[0:length], table_dot(forward, gated[0:length]), True)
        after = gated[length : length + 2]
        zero_lag, one_lag = filter_row(0, 0), filter_row(0, 1)
        fix[0:1] += after[0:1] * zero_lag
        fix[1:2] += after[1:2] * zero_lag + after[0:1] * one_lag

        for index in range(blocks - 1):
            other = me ^ (index + 1)

            @pl.when(other < me)
            def _():
                signal = taps_of(first_rows, other, length, weights[1]) * taps_of(
                    second_rows, other, length, weights[2]
                )
                add_lower(me - other, signal, table_dot(forward, signal), False)

            @pl.when(other > me)
            def _():
                signal = (
                    taps_of(first_rows, other + 1, length, weights[0])
                    * second_rows[other + 1, EDGE : EDGE + length]
                )
                add_upper(other - me, signal, table_dot(forward, signal), False)

        inverse = inverse_ref[...]
        long_conv = table_dot(inverse, acc[0])
        gated_grad = table_dot(inverse, acc[1])
        out_ref[:, lanes] = (query_conv[0:length] * long_conv[0:length]).astype(BF16)
        inside = jnp.where(me < blocks - 1, 1.0, 0.0)
        conv_edge = long_conv[length:] + fix[0:EDGE]
        grad_edge = (gated_grad[length:] + fix[EDGE:]) * inside
        grads[0, 0:length] = incoming[0:length] * long_conv[0:length]
        grads[0, length:] = incoming[length:] * conv_edge
        grads[1, 0:length] = gated_grad[0:length] * value_conv[0:length]
        grads[1, length:] = grad_edge * value_conv[length:]
        grads[2, 0:length] = gated_grad[0:length] * key_conv[0:length]
        grads[2, length:] = grad_edge * key_conv[length:]
        for p, ref in enumerate((gq_ref, gk_ref, gv_ref)):
            total = weights[p][0:1] * grads[p, 0:length]
            for shift in range(1, weights[p].shape[0]):
                total = total + weights[p][shift : shift + 1] * grads[p, shift : shift + length]
            ref[:, lanes] = total.astype(BF16)
        return carry

    lax.fori_loop(0, width // tile_width, one_tile, 0)

    inverse = inverse_ref[0:length]
    for level, ref in enumerate(gf_refs):
        for place_in, index in enumerate(range(1 << level, blocks, 2 << level) or (0,)):
            block = me ^ index
            re = cross[block, 0:length] + sign * cross[block + 1, length:]
            im = cross[block, length:] - sign * cross[block + 1, 0:length]
            ref[place_in] = table_dot(inverse, jnp.concatenate([re, im], axis=0))


def per_device(query_rows, key_rows, value_rows, short_taps, long_filter, cotangent):
    length, width = query_rows.shape
    groups = long_filter.shape[1]
    blocks = lax.axis_size("seq")
    chans = lax.axis_size("chan")
    bits = []
    while 1 << len(bits) < blocks:
        bits.append(1 << len(bits))
    bits.reverse()
    forward, inverse = dft_tables(length)

    unit_shape = jax.ShapeDtypeStruct(
        (2 * length + 2 * (length * groups // width) + HALO, width), BF16
    )
    own_units = pl.pallas_call(
        functools.partial(pack_kernel, bits),
        out_shape=[unit_shape] * len(bits),
        in_specs=[VMEM] * 5,
        out_specs=[VMEM] * len(bits),
    )(query_rows, key_rows, value_rows, cotangent, long_filter)

    def swap(block, bit):
        return lax.ppermute(block, "seq", [(i, i ^ bit) for i in range(blocks)])

    units = {}
    for bit, own in zip(bits, own_units):
        arrived = {bit: swap(own, bit)}
        for index, block in units.items():
            arrived[index ^ bit] = swap(block, bit)
        units.update(arrived)
    units = [units[index] for index in range(1, blocks)]

    tile_width = min(width, 256)
    rows_out = jax.ShapeDtypeStruct((length, width), BF16)
    partial_shapes = [
        jax.ShapeDtypeStruct((max(1, blocks >> (level + 1)), length, groups), F32)
        for level in range(len(bits) + 1)
    ]
    hyena_out, grad_query, grad_key, grad_value, *partial = pl.pallas_call(
        functools.partial(main_kernel, blocks, tile_width),
        out_shape=[rows_out] * 4 + partial_shapes,
        in_specs=[VMEM] * (8 + blocks - 1),
        out_specs=[VMEM] * (4 + len(partial_shapes)),
        scratch_shapes=[
            pltpu.VMEM((blocks + 2, length + 2 * EDGE, tile_width), F32),
            pltpu.VMEM((blocks + 2, length + 2 * EDGE, tile_width), F32),
            pltpu.VMEM((blocks, 2 * length, groups), F32),
            pltpu.VMEM((blocks + 3, length, groups), F32),
            pltpu.VMEM((blocks + 1, 2 * length, groups), F32),
            pltpu.VMEM((2 * length, tile_width), F32),
            pltpu.VMEM((2, 2 * length, tile_width), F32),
            pltpu.VMEM((2 * EDGE, tile_width), F32),
            pltpu.VMEM((3, length + EDGE, tile_width), F32),
        ],
        compiler_params=pltpu.CompilerParams(vmem_limit_bytes=48 * 1024 * 1024),
    )(
        query_rows,
        key_rows,
        value_rows,
        cotangent,
        short_taps,
        long_filter,
        forward,
        inverse,
        *units,
    )

    kept = list(partial)
    for level in range(len(bits)):
        arrived = swap(kept[level], 1 << level)
        for later in range(level + 1, len(kept)):
            first = (1 << (later - level - 1)) % arrived.shape[0]
            kept[later] = kept[later] + arrived[first :: 1 << (later - level)]
    grad_filter = kept[-1][0]
    step = 1
    while step < chans:
        grad_filter = grad_filter + lax.ppermute(
            grad_filter, "chan", [(i, i ^ step) for i in range(chans)]
        )
        step *= 2
    return (hyena_out, grad_query, grad_key, grad_value, grad_filter)


def solution(mesh):
    in_specs = (
        P("seq", "chan"),
        P("seq", "chan"),
        P("seq", "chan"),
        P(None, None, "chan"),
        P("seq", None),
        P("seq", "chan"),
    )
    out_specs = (
        P("seq", "chan"),
        P("seq", "chan"),
        P("seq", "chan"),
        P("seq", "chan"),
        P("seq", None),
    )
    return jax.shard_map(
        per_device, mesh=mesh, in_specs=in_specs, out_specs=out_specs, check_vma=False
    )
```

```python
import functools

import jax
import jax.numpy as jnp
import ml_dtypes
import numpy as np
from jax import lax
from jax.experimental import pallas as pl
from jax.experimental.pallas import tpu as pltpu
from jax.sharding import PartitionSpec as P

F32 = jnp.float32
BF16 = jnp.bfloat16
EDGE = 8
HALO = 16
VMEM = pl.BlockSpec(memory_space=pltpu.VMEM)


def split_table(table):
    high = table.astype(ml_dtypes.bfloat16)
    low = (table - high.astype(np.float64)).astype(ml_dtypes.bfloat16)
    return high, low


def dft_tables(length):
    frequency = np.pi * (2 * np.arange(length) + 1) / (2 * length)
    into = frequency[:, None] * np.arange(length)[None, :]
    high, low = split_table(np.concatenate([np.cos(into), -np.sin(into)], axis=0))
    forward = np.concatenate([high, high, low], axis=1)
    back = np.arange(length + EDGE)[:, None] * frequency[None, :]
    high, low = split_table(np.concatenate([np.cos(back), -np.sin(back)], axis=1) / length)
    inverse = np.concatenate([high, high, low], axis=1)
    return jnp.asarray(forward), jnp.asarray(inverse)


def halves(values):
    high = values.astype(BF16)
    return high, (values - high.astype(F32)).astype(BF16)


def table_dot(table, values):
    high, low = halves(values)
    return jnp.dot(
        table, jnp.concatenate([high, low, high], axis=0), preferred_element_type=F32
    )


def tap_sum(rows_ref, first, count, weights):
    total = weights[0:1] * rows_ref[first : first + count]
    for shift in range(1, weights.shape[0]):
        total = total + weights[shift : shift + 1] * rows_ref[first - shift : first - shift + count]
    return total


def put_filter(unit, first, filter_high, filter_low):
    length, groups = filter_high.shape
    width = unit.shape[1]
    rows = length * groups // width
    for tile in range(width // groups):
        lanes = slice(tile * groups, (tile + 1) * groups)
        part = slice(tile * rows, (tile + 1) * rows)
        unit[first : first + rows, lanes] = filter_high[part]
        unit[first + rows : first + 2 * rows, lanes] = filter_low[part]


def get_filter(unit, first, length, groups):
    width = unit.shape[1]
    rows = length * groups // width
    pieces = []
    for tile in range(width // groups):
        lanes = slice(tile * groups, (tile + 1) * groups)
        pieces.append(
            unit[first : first + rows, lanes].astype(F32)
            + unit[first + rows : first + 2 * rows, lanes].astype(F32)
        )
    return jnp.concatenate(pieces, axis=0)


def own_kernel(
    bits,
    tile_width,
    q_ref,
    k_ref,
    v_ref,
    c_ref,
    taps_ref,
    filter_ref,
    tails_ref,
    pair_ref,
    conv_ref,
    edge_ref,
    *refs,
):
    unit_refs, rows_scratch = refs[:-1], refs[-1]
    length, width = q_ref.shape
    half = width // 2
    me = lax.axis_index("seq")
    margin = taps_ref.shape[1] - 1
    filter_high, filter_low = halves(filter_ref[...])
    put_filter(pair_ref, 4 * length, filter_high, filter_low)
    for later in unit_refs[1::2]:
        put_filter(later, 2 * length, filter_high, filter_low)
    for tile in range(width // tile_width):
        lanes = slice(tile * tile_width, (tile + 1) * tile_width)
        convs = []
        for p, ref in enumerate((q_ref, k_ref, v_ref)):
            rows_scratch[p, EDGE - margin : EDGE] = tails_ref[p * margin : (p + 1) * margin, lanes]
            rows_scratch[p, EDGE : EDGE + length] = ref[:, lanes].astype(F32)
            edge_ref[p, :, lanes] = rows_scratch[p, length : length + EDGE]
            conv = tap_sum(rows_scratch.at[p], EDGE, length, taps_ref[p, :, lanes])
            conv_ref[p, :, lanes] = conv
            convs.append(conv)
        incoming = c_ref[:, lanes].astype(F32)
        parts = [*halves(convs[1] * convs[2]), *halves(incoming * convs[0])]
        for index, part in enumerate(parts):
            pair_ref[index * length : (index + 1) * length, lanes] = part
        in_half = tile * tile_width // half
        lanes_half = slice(tile * tile_width % half, tile * tile_width % half + tile_width)
        for index, bit in enumerate(bits):
            low_side = (me // bit) % 2 == 0
            first, later = unit_refs[2 * index : 2 * index + 2]
            target_low, target_high = (first, later) if in_half == 0 else (later, first)

            @pl.when(low_side)
            def _():
                target_low[0:length, lanes_half] = parts[0]
                target_low[length : 2 * length, lanes_half] = parts[1]

            @pl.when(jnp.logical_not(low_side))
            def _():
                target_high[0:length, lanes_half] = parts[2]
                target_high[length : 2 * length, lanes_half] = parts[3]


def spectrum(forward, high, low):
    return jnp.dot(
        forward, jnp.concatenate([high, low, high], axis=0), preferred_element_type=F32
    )


def cross_add(cross, distance, early, late, groups):
    length = early.shape[0] // 2
    e_re, e_im = early[0:length], early[length:]
    l_re, l_im = late[0:length], late[length:]
    re = e_re * l_re + e_im * l_im
    im = e_re * l_im - e_im * l_re
    parts = range(early.shape[1] // groups)
    cross[distance, 0:length] += sum(re[:, p * groups : (p + 1) * groups] for p in parts)
    cross[distance, length:] += sum(im[:, p * groups : (p + 1) * groups] for p in parts)


def chip_kernel(tile_width, groups, own_ref, other_ref, forward_ref, spec_ref, cross_ref):
    length = forward_ref.shape[0] // 2
    width = own_ref.shape[1]
    core = lax.axis_index("seq") % 2
    forward = forward_ref[...]
    cross_ref[...] = jnp.zeros(cross_ref.shape, F32)

    def one_tile(step, carry):
        lanes = pl.ds(pl.multiple_of(step * tile_width, tile_width), tile_width)
        for ref, slot in ((own_ref, core), (other_ref, 1 - core)):
            for kind in range(2):
                first = 2 * kind * length
                spec_ref[2 * kind + slot, :, lanes] = spectrum(
                    forward,
                    ref[first : first + length, lanes],
                    ref[first + length : first + 2 * length, lanes],
                )
        cross_add(cross_ref, 0, spec_ref[core, :, lanes], spec_ref[2 + core, :, lanes], groups)

        @pl.when(2 * step * tile_width // width == core)
        def _():
            cross_add(cross_ref, 1, spec_ref[0, :, lanes], spec_ref[3, :, lanes], groups)

        return carry

    lax.fori_loop(0, width // tile_width, one_tile, 0)


def filter_grad_kernel(blocks, tile_width, spec_ref, near_ref, forward_ref, inverse_ref, *refs):
    chips = blocks // 2
    units = refs[: chips - 1]
    gf_refs, cross = refs[chips - 1 : -1], refs[-1]
    length = forward_ref.shape[0] // 2
    groups = near_ref.shape[2]
    half = spec_ref.shape[2] // 2
    me = lax.axis_index("seq")
    core, chip = me % 2, me // 2
    forward = forward_ref[...]
    cross[0:2] = near_ref[...]
    cross[2:] = jnp.zeros((blocks - 1, 2 * length, groups), F32)
    for index, unit in enumerate(units):
        other = chip ^ (index + 1)

        def one_tile(step, carry):
            start = pl.multiple_of(step * tile_width, tile_width)
            lanes = pl.ds(start, tile_width)
            spec = spectrum(forward, unit[0:length, lanes], unit[length : 2 * length, lanes])

            @pl.when(other < chip)
            def _():
                for slot in range(2):
                    distance = 2 * chip + slot - (2 * other + core)
                    cross_add(cross, distance, spec, spec_ref[2 + slot, :, lanes], groups)

            @pl.when(other > chip)
            def _():
                upper = pl.ds(pl.multiple_of(half + start, tile_width), tile_width)
                for slot in range(2):
                    distance = 2 * other + core - (2 * chip + slot)
                    cross_add(cross, distance, spec_ref[slot, :, upper], spec, groups)

            return carry

        lax.fori_loop(0, half // tile_width, one_tile, 0)

    inverse = inverse_ref[0:length]
    sign = signs(length, groups)
    for level, ref in enumerate(gf_refs):
        for place, index in enumerate(range(1 << level, blocks, 2 << level) or (0,)):
            block = me ^ index
            re = cross[block, 0:length] + sign * cross[block + 1, length:]
            im = cross[block, length:] - sign * cross[block + 1, 0:length]
            ref[place] = table_dot(inverse, jnp.concatenate([re, im], axis=0))


def signs(length, groups):
    row = lax.broadcasted_iota(jnp.int32, (length, groups), 0)
    return jnp.where(row % 2 == 0, 1.0, -1.0)


def result_kernel(
    blocks,
    tile_width,
    c_ref,
    taps_ref,
    filter_ref,
    heads_ref,
    conv_ref,
    edge_ref,
    own_ref,
    other_ref,
    spec_ref,
    forward_ref,
    inverse_ref,
    *refs,
):
    chips = blocks // 2
    count = 4 * (chips - 1)
    units = [refs[4 * index : 4 * index + 4] for index in range(chips - 1)]
    out_ref, gq_ref, gk_ref, gv_ref = refs[count : count + 4]
    window, spectra, filter_rows, acc, fix, grads = refs[count + 4 :]
    length, width = c_ref.shape
    groups = filter_ref.shape[1]
    half = width // 2
    margin = taps_ref.shape[1] - 1
    me = lax.axis_index("seq")
    core, chip = me % 2, me // 2
    forward = forward_ref[...]
    sign = signs(length, groups)

    for edge in (0, 1, blocks + 2):
        filter_rows[edge] = jnp.zeros((length, groups), F32)
    filter_rows[me + 2] = filter_ref[...]
    filter_rows[(me ^ 1) + 2] = get_filter(other_ref, 4 * length, length, groups)
    for index, unit in enumerate(units):
        block = me ^ (2 * (index + 1))
        filter_rows[block + 2] = get_filter(unit[1], 2 * length, length, groups)
        filter_rows[(block ^ 1) + 2] = get_filter(unit[3], 2 * length, length, groups)
    previous = None
    for distance in range(blocks):
        own = table_dot(forward, filter_rows[distance + 2])
        if previous is None:
            spectra[distance] = own
        else:
            spectra[distance, 0:length] = own[0:length] - sign * previous[length:]
            spectra[distance, length:] = own[length:] + sign * previous[0:length]
        previous = own

    def wide(values):
        return jnp.concatenate([values] * (tile_width // groups), axis=1)

    def filter_row(block, row):
        return wide(filter_rows[block + 2, pl.ds(row, 1)])

    def first_rows(ref, first, lanes):
        return (
            ref[first : first + HALO, lanes].astype(F32)
            + ref[first + length : first + length + HALO, lanes].astype(F32)
        )

    def add_lower(distance, signal, spec, fresh=False):
        re, im = spec[0:length], spec[length:]
        h_re, h_im = wide(spectra[distance, 0:length]), wide(spectra[distance, length:])
        new_re = h_re * re - h_im * im
        new_im = h_re * im + h_im * re
        acc[0, 0:length] = new_re if fresh else acc[0, 0:length] + new_re
        acc[0, length:] = new_im if fresh else acc[0, length:] + new_im
        near = filter_row(distance + 1, 0) + filter_row(distance - 1, 0)
        far = filter_row(distance + 1, 1) + filter_row(distance - 1, 1)
        fix[0:1] += signal[0:1] * near
        fix[1:2] += signal[0:1] * far + signal[1:2] * near

    def add_upper(distance, signal, spec, fresh=False):
        re, im = spec[0:length], spec[length:]
        h_re, h_im = wide(spectra[distance, 0:length]), wide(spectra[distance, length:])
        new_re = h_re * re + h_im * im
        new_im = h_re * im - h_im * re
        acc[1, 0:length] = new_re if fresh else acc[1, 0:length] + new_re
        acc[1, length:] = new_im if fresh else acc[1, length:] + new_im
        fix[EDGE + 1 : EDGE + 2] += signal[0:1] * (
            filter_row(distance - 2, length - 1) + filter_row(distance, length - 1)
        )

    def one_tile(tile, in_half):
        start = in_half * half + tile * tile_width
        lanes = pl.ds(pl.multiple_of(start, tile_width), tile_width)
        lanes_half = pl.ds(pl.multiple_of(tile * tile_width, tile_width), tile_width)
        weights = [taps_ref[p, :, lanes] for p in range(3)]
        fix[...] = jnp.zeros(fix.shape, F32)

        add_lower(0, first_rows(own_ref, 0, lanes), spec_ref[core, :, lanes], True)
        add_upper(0, first_rows(own_ref, 2 * length, lanes), spec_ref[2 + core, :, lanes], True)

        @pl.when(core == 1)
        def _():
            add_lower(1, first_rows(other_ref, 0, lanes), spec_ref[0, :, lanes])

        @pl.when(core == 0)
        def _():
            add_upper(1, first_rows(other_ref, 2 * length, lanes), spec_ref[3, :, lanes])

        for index, unit in enumerate(units):
            other = chip ^ (index + 1)
            for ref_low, ref_high, block in (
                (unit[in_half], unit[1 - in_half], 2 * other + core),
                (unit[2 + in_half], unit[3 - in_half], 2 * other + 1 - core),
            ):

                @pl.when(other < chip)
                def _():
                    high, low = ref_low[0:length, lanes_half], ref_low[length : 2 * length, lanes_half]
                    signal = first_rows(ref_low, 0, lanes_half)
                    add_lower(me - block, signal, spectrum(forward, high, low))

                @pl.when(other > chip)
                def _():
                    high, low = ref_high[0:length, lanes_half], ref_high[length : 2 * length, lanes_half]
                    signal = first_rows(ref_high, 0, lanes_half)
                    add_upper(block - me, signal, spectrum(forward, high, low))

        after = []
        for p in range(3):
            window[0:EDGE] = edge_ref[p, :, lanes]
            window[EDGE:] = jnp.zeros((EDGE, tile_width), F32)
            window[EDGE : EDGE + margin] = heads_ref[p * margin : (p + 1) * margin, lanes]
            after.append(tap_sum(window, EDGE, EDGE, weights[p]))
        window[EDGE:] = jnp.zeros((EDGE, tile_width), F32)
        window[EDGE : EDGE + margin] = heads_ref[3 * margin : 4 * margin, lanes]
        after_incoming = window[EDGE:]
        gated = after[1] * after[2]
        zero_lag, one_lag = filter_row(0, 0), filter_row(0, 1)
        fix[0:1] += gated[0:1] * zero_lag
        fix[1:2] += gated[1:2] * zero_lag + gated[0:1] * one_lag

        inverse = inverse_ref[...]
        long_conv = table_dot(inverse, acc[0])
        gated_grad = table_dot(inverse, acc[1])
        incoming = c_ref[:, lanes].astype(F32)
        out_ref[:, lanes] = (conv_ref[0, :, lanes] * long_conv[0:length]).astype(BF16)
        inside = jnp.where(me < blocks - 1, 1.0, 0.0)
        grad_edge = (gated_grad[length:] + fix[EDGE:]) * inside
        grads[0, 0:length] = incoming * long_conv[0:length]
        grads[0, length:] = after_incoming * (long_conv[length:] + fix[0:EDGE])
        grads[1, 0:length] = gated_grad[0:length] * conv_ref[2, :, lanes]
        grads[1, length:] = grad_edge * after[2]
        grads[2, 0:length] = gated_grad[0:length] * conv_ref[1, :, lanes]
        grads[2, length:] = grad_edge * after[1]
        for p, ref in enumerate((gq_ref, gk_ref, gv_ref)):
            total = weights[p][0:1] * grads[p, 0:length]
            for shift in range(1, margin + 1):
                total = total + weights[p][shift : shift + 1] * grads[p, shift : shift + length]
            ref[:, lanes] = total.astype(BF16)

    for in_half in range(2):
        lax.fori_loop(
            0, half // tile_width, lambda tile, carry: one_tile(tile, in_half), None
        )


def per_device(query_rows, key_rows, value_rows, short_taps, long_filter, cotangent):
    length, width = query_rows.shape
    groups = long_filter.shape[1]
    blocks = lax.axis_size("seq")
    chans = lax.axis_size("chan")
    chips, half = blocks // 2, width // 2
    margin = short_taps.shape[1] - 1
    tile_width = min(half, 256)
    bits = []
    while 2 << len(bits) < blocks:
        bits.append(2 << len(bits))
    bits.reverse()
    forward, inverse = dft_tables(length)
    shape = jax.ShapeDtypeStruct
    params = pltpu.CompilerParams(vmem_limit_bytes=40 * 1024 * 1024)

    def swap(block, bit):
        return lax.ppermute(block, "seq", [(i, i ^ bit) for i in range(blocks)])

    def call(kernel, outs, args, scratch, flops):
        return pl.pallas_call(
            kernel,
            out_shape=outs,
            in_specs=[VMEM] * len(args),
            out_specs=[VMEM] * len(outs),
            scratch_shapes=scratch,
            compiler_params=params,
            cost_estimate=pl.CostEstimate(
                flops=flops, bytes_accessed=4 * length * width, transcendentals=0
            ),
        )(*args)

    def edges(rows, *arrays):
        picked = jnp.concatenate([array[rows] for array in arrays], axis=0).astype(F32)
        return jnp.pad(picked, ((0, EDGE - picked.shape[0]), (0, 0)))

    tails = lax.ppermute(
        edges(slice(length - margin, length), query_rows, key_rows, value_rows),
        "seq",
        [(i, i + 1) for i in range(blocks - 1)],
    )
    heads = lax.ppermute(
        edges(slice(0, margin), query_rows, key_rows, value_rows, cotangent),
        "seq",
        [(i + 1, i) for i in range(blocks - 1)],
    )

    filter_rows = length * groups // width
    pair_shape = shape((4 * length + 2 * filter_rows, width), BF16)
    first_shape = shape((2 * length, half), BF16)
    later_shape = shape((2 * length + 4 * filter_rows, half), BF16)
    pair, conv, edge, *own_units = call(
        functools.partial(own_kernel, bits, tile_width),
        [pair_shape, shape((3, length, width), F32), shape((3, EDGE, width), F32)]
        + [first_shape, later_shape] * len(bits),
        [query_rows, key_rows, value_rows, cotangent, short_taps, long_filter, tails],
        [pltpu.VMEM((3, length + EDGE, tile_width), F32)],
        length * width * 64,
    )

    def gather(own):
        units = {}
        for bit, block in zip(bits, own):
            arrived = {bit // 2: swap(block, bit)}
            for index, unit in units.items():
                arrived[index ^ bit // 2] = swap(unit, bit)
            units.update(arrived)
        return [units[index] for index in range(1, chips)]

    firsts = gather(own_units[0::2])
    sibling = swap(pair, 1)
    laters = gather(own_units[1::2])
    spec, near = call(
        functools.partial(chip_kernel, tile_width, groups),
        [shape((4, 2 * length, width), F32), shape((2, 2 * length, groups), F32)],
        [pair, sibling, forward],
        [],
        4 * 6 * 2 * length * length * width,
    )
    kept = call(
        functools.partial(filter_grad_kernel, blocks, tile_width),
        [
            shape((max(1, blocks >> (level + 1)), length, groups), F32)
            for level in range(len(bits) + 2)
        ],
        [spec, near, forward, inverse, *firsts],
        [pltpu.VMEM((blocks + 1, 2 * length, groups), F32)],
        6 * 2 * length * length * width,
    )
    units = []
    for first, later in zip(firsts, laters):
        units += [first, later, swap(first, 1), swap(later, 1)]
    rows_out = shape((length, width), BF16)
    results = call(
        functools.partial(result_kernel, blocks, tile_width),
        [rows_out] * 4,
        [
            cotangent,
            short_taps,
            long_filter,
            heads,
            conv,
            edge,
            pair,
            sibling,
            spec,
            forward,
            inverse,
            *units,
        ],
        [
            pltpu.VMEM((2 * EDGE, tile_width), F32),
            pltpu.VMEM((blocks, 2 * length, groups), F32),
            pltpu.VMEM((blocks + 3, length, groups), F32),
            pltpu.VMEM((2, 2 * length, tile_width), F32),
            pltpu.VMEM((2 * EDGE, tile_width), F32),
            pltpu.VMEM((3, length + EDGE, tile_width), F32),
        ],
        4 * 6 * 2 * length * length * width,
    )

    kept = list(kept)
    for level in range(len(bits) + 1):
        arrived = swap(kept[level], 1 << level)
        for later in range(level + 1, len(kept)):
            first = (1 << (later - level - 1)) % arrived.shape[0]
            kept[later] = kept[later] + arrived[first :: 1 << (later - level)]
    grad_filter = kept[-1][0]
    step = 1
    while step < chans:
        grad_filter = grad_filter + lax.ppermute(
            grad_filter, "chan", [(i, i ^ step) for i in range(chans)]
        )
        step *= 2
    return (*results, grad_filter)


def solution(mesh):
    in_specs = (
        P("seq", "chan"),
        P("seq", "chan"),
        P("seq", "chan"),
        P(None, None, "chan"),
        P("seq", None),
        P("seq", "chan"),
    )
    out_specs = (
        P("seq", "chan"),
        P("seq", "chan"),
        P("seq", "chan"),
        P("seq", "chan"),
        P("seq", None),
    )
    return jax.shard_map(
        per_device, mesh=mesh, in_specs=in_specs, out_specs=out_specs, check_vma=False
    )
```

```python
import functools

import jax
import jax.numpy as jnp
import ml_dtypes
import numpy as np
from jax import lax
from jax.experimental import pallas as pl
from jax.experimental.pallas import tpu as pltpu
from jax.sharding import PartitionSpec as P

F32 = jnp.float32
BF16 = jnp.bfloat16
EDGE = 8
HEAD = 16
VMEM = pl.BlockSpec(memory_space=pltpu.VMEM)
HBM = pl.BlockSpec(memory_space=pltpu.HBM)


def split_table(table):
    high = table.astype(ml_dtypes.bfloat16)
    low = (table - high.astype(np.float64)).astype(ml_dtypes.bfloat16)
    return high, low


def dft_tables(length, width):
    frequency = np.pi * (2 * np.arange(length) + 1) / (2 * length)
    into = frequency[:, None] * np.arange(length)[None, :]
    back = np.arange(length + EDGE)[:, None] * frequency[None, :]
    parts = [
        *split_table(np.concatenate([np.cos(into), -np.sin(into)], axis=0)),
        *split_table(np.concatenate([np.cos(back), -np.sin(back)], axis=1) / length),
    ]
    placed = np.zeros(table_shape(length, width), ml_dtypes.bfloat16)
    for part, (row, lane) in zip(parts, table_places(length, width)):
        placed[row : row + part.shape[0], lane : lane + part.shape[1]] = part
    return jnp.asarray(placed)


def table_places(length, width):
    if width >= 6 * length:
        return (0, 0), (0, length), (0, 2 * length), (0, 4 * length)
    return (0, 0), (0, length), (2 * length, 0), (4 * length, 0)


def table_shape(length, width):
    return (2 * length if width >= 6 * length else 6 * length, width)


def tables_in(rows_ref):
    width = rows_ref.shape[1]
    length = rows_ref.shape[0] // (6 if width // (rows_ref.shape[0] // 6) >= 6 else 10)
    parts = []
    shapes = [(2 * length, length)] * 2 + [(length + EDGE, 2 * length)] * 2
    for (row, lane), (count, lanes) in zip(table_places(length, width), shapes):
        row += 4 * length
        parts.append(rows_ref[row : row + count, lane : lane + lanes])
    return (
        jnp.concatenate([parts[0], parts[0], parts[1]], axis=1),
        jnp.concatenate([parts[2], parts[2], parts[3]], axis=1),
    )


def halves(values):
    high = values.astype(BF16)
    return high, (values - high.astype(F32)).astype(BF16)


def table_dot(table, values):
    high, low = halves(values)
    return jnp.dot(
        table, jnp.concatenate([high, low, high], axis=0), preferred_element_type=F32
    )


def tap_sum(rows_ref, first, count, weights):
    total = weights[0:1] * rows_ref[first : first + count]
    for shift in range(1, weights.shape[0]):
        total = total + weights[shift : shift + 1] * rows_ref[first - shift : first - shift + count]
    return total


def put_filter(unit, first, filter_high, filter_low):
    length, groups = filter_high.shape
    width = unit.shape[1]
    rows = length * groups // width
    for tile in range(width // groups):
        lanes = slice(tile * groups, (tile + 1) * groups)
        part = slice(tile * rows, (tile + 1) * rows)
        unit[first : first + rows, lanes] = filter_high[part]
        unit[first + rows : first + 2 * rows, lanes] = filter_low[part]


def get_filter(unit, first, length, groups):
    width = unit.shape[1]
    rows = length * groups // width
    pieces = []
    for tile in range(width // groups):
        lanes = slice(tile * groups, (tile + 1) * groups)
        pieces.append(
            unit[first : first + rows, lanes].astype(F32)
            + unit[first + rows : first + 2 * rows, lanes].astype(F32)
        )
    return jnp.concatenate(pieces, axis=0)


def cross_add(cross, distance, early, late, groups):
    length = early.shape[0] // 2
    e_re, e_im = early[0:length], early[length:]
    l_re, l_im = late[0:length], late[length:]
    re = e_re * l_re + e_im * l_im
    im = e_re * l_im - e_im * l_re
    parts = range(early.shape[1] // groups)
    cross[distance, 0:length] += sum(re[:, p * groups : (p + 1) * groups] for p in parts)
    cross[distance, length:] += sum(im[:, p * groups : (p + 1) * groups] for p in parts)


def signs(length, groups):
    row = lax.broadcasted_iota(jnp.int32, (length, groups), 0)
    return jnp.where(row % 2 == 0, 1.0, -1.0)


def body_kernel(
    bits, tile_width, rows_ref, taps_ref, pair_ref, conv_ref, tails_ref, top_ref, *refs
):
    unit_refs, rows_scratch = refs[:-1], refs[-1]
    length, width = rows_scratch.shape[1], rows_ref.shape[1]
    half, body = width // 2, length - HEAD
    me = lax.axis_index("seq")
    margin = taps_ref.shape[1] - 1
    tails_ref[...] = jnp.zeros(tails_ref.shape, F32)
    for tile in range(width // tile_width):
        lanes = slice(tile * tile_width, (tile + 1) * tile_width)
        convs = []
        for p in range(3):
            rows_scratch[p] = rows_ref[p * length : (p + 1) * length, lanes].astype(F32)
            top_ref[p, :, lanes] = rows_scratch[p, 0:HEAD]
            tails_ref[p * margin : (p + 1) * margin, lanes] = rows_scratch[p, length - margin :]
            conv = tap_sum(rows_scratch.at[p], HEAD, body, taps_ref[p, :, lanes])
            conv_ref[p, :, lanes] = conv
            convs.append(conv)
        incoming = rows_ref[3 * length : 4 * length, lanes].astype(F32)
        top_ref[3, :, lanes] = incoming[0:HEAD]
        parts = [*halves(convs[1] * convs[2]), *halves(incoming[HEAD:] * convs[0])]
        for index, part in enumerate(parts):
            pair_ref[index * body : (index + 1) * body, lanes] = part
        in_half = tile * tile_width // half
        lanes_half = slice(tile * tile_width % half, tile * tile_width % half + tile_width)
        for index, bit in enumerate(bits):
            low_side = (me // bit) % 2 == 0
            first, later = unit_refs[2 * index : 2 * index + 2]
            target_low, target_high = (first, later) if in_half == 0 else (later, first)

            @pl.when(low_side)
            def _():
                target_low[0:body, lanes_half] = parts[0]
                target_low[body:, lanes_half] = parts[1]

            @pl.when(jnp.logical_not(low_side))
            def _():
                target_high[0:body, lanes_half] = parts[2]
                target_high[body:, lanes_half] = parts[3]


def head_kernel(
    bits, tails_ref, top_ref, taps_ref, filter_ref, conv_ref, pair_ref, *refs
):
    unit_refs, window, edge = refs[: len(bits)], refs[-2], refs[-1]
    me = lax.axis_index("seq")
    margin = taps_ref.shape[1] - 1
    filter_high, filter_low = halves(filter_ref[...])
    convs = []
    for p in range(3):
        window[EDGE - margin : EDGE] = tails_ref[p * margin : (p + 1) * margin]
        window[EDGE:] = top_ref[p]
        conv = tap_sum(window, EDGE, HEAD, taps_ref[p])
        conv_ref[p] = conv
        convs.append(conv)
    incoming = top_ref[3]
    edge[...] = jnp.zeros(edge.shape, F32)
    for p, rows in enumerate((convs[1], convs[2], incoming)):
        edge[p * margin : (p + 1) * margin] = rows[0:margin]
    parts = [*halves(convs[1] * convs[2]), *halves(incoming * convs[0])]
    high = edge[...].astype(BF16).astype(F32)
    edges = jnp.concatenate([high, edge[...] - high], axis=0).astype(BF16)
    for index, part in enumerate(parts):
        pair_ref[index * HEAD : (index + 1) * HEAD] = part
    pair_ref[4 * HEAD : 5 * HEAD] = edges
    put_filter(pair_ref, 5 * HEAD, filter_high, filter_low)
    for unit, bit in zip(unit_refs, bits):
        low_side = (me // bit) % 2 == 0
        for index in range(2):

            @pl.when(low_side)
            def _():
                unit[index * HEAD : (index + 1) * HEAD] = parts[index]

            @pl.when(jnp.logical_not(low_side))
            def _():
                unit[index * HEAD : (index + 1) * HEAD] = parts[2 + index]

        unit[2 * HEAD : 3 * HEAD] = edges
        put_filter(unit, 3 * HEAD, filter_high, filter_low)


def spectrum(forward, head_ref, head_first, head_lanes, body_ref, body_first, body_lanes):
    body = forward.shape[0] // 2 - HEAD
    high, low = [
        jnp.concatenate(
            [
                head_ref[head_first + part * HEAD : head_first + (part + 1) * HEAD, head_lanes],
                body_ref[body_first + part * body : body_first + (part + 1) * body, body_lanes],
            ],
            axis=0,
        )
        for part in range(2)
    ]
    return jnp.dot(
        forward, jnp.concatenate([high, low, high], axis=0), preferred_element_type=F32
    )


def chip_kernel(
    tile_width,
    groups,
    own_body,
    own_head,
    other_body,
    other_head,
    rows_ref,
    spec_ref,
    cross_ref,
):
    forward, _ = tables_in(rows_ref)
    length = forward.shape[0] // 2
    width = own_body.shape[1]
    core = lax.axis_index("seq") % 2
    cross_ref[...] = jnp.zeros(cross_ref.shape, F32)

    def one_tile(step, carry):
        lanes = pl.ds(pl.multiple_of(step * tile_width, tile_width), tile_width)
        for head, body, slot in ((own_head, own_body, core), (other_head, other_body, 1 - core)):
            for kind in range(2):
                spec_ref[2 * kind + slot, :, lanes] = spectrum(
                    forward,
                    head,
                    2 * kind * HEAD,
                    lanes,
                    body,
                    2 * kind * (length - HEAD),
                    lanes,
                )
        cross_add(cross_ref, 0, spec_ref[core, :, lanes], spec_ref[2 + core, :, lanes], groups)

        @pl.when(2 * step * tile_width // width == core)
        def _():
            cross_add(cross_ref, 1, spec_ref[0, :, lanes], spec_ref[3, :, lanes], groups)

        return carry

    lax.fori_loop(0, width // tile_width, one_tile, 0)


def filter_grad_kernel(blocks, tile_width, spec_ref, near_ref, rows_ref, *refs):
    others = blocks // 2 - 1
    units = list(zip(refs[:others], refs[others : 2 * others]))
    gf_refs, cross = refs[2 * others : -1], refs[-1]
    forward, inverse = tables_in(rows_ref)
    length = forward.shape[0] // 2
    groups = near_ref.shape[2]
    half = spec_ref.shape[2] // 2
    me = lax.axis_index("seq")
    core, chip = me % 2, me // 2
    cross[0:2] = near_ref[...]
    cross[2:] = jnp.zeros((blocks - 1, 2 * length, groups), F32)
    for index, (head, body) in enumerate(units):
        other = chip ^ (index + 1)
        first = jnp.where(other < chip, 0, half)

        def one_tile(step, carry):
            start = pl.multiple_of(step * tile_width, tile_width)
            lanes = pl.ds(start, tile_width)
            wide_lanes = pl.ds(pl.multiple_of(first + start, tile_width), tile_width)
            spec = spectrum(forward, head, 0, wide_lanes, body, 0, lanes)

            @pl.when(other < chip)
            def _():
                for slot in range(2):
                    distance = 2 * chip + slot - (2 * other + core)
                    cross_add(cross, distance, spec, spec_ref[2 + slot, :, wide_lanes], groups)

            @pl.when(other > chip)
            def _():
                for slot in range(2):
                    distance = 2 * other + core - (2 * chip + slot)
                    cross_add(cross, distance, spec_ref[slot, :, wide_lanes], spec, groups)

            return carry

        lax.fori_loop(0, half // tile_width, one_tile, 0)

    inverse = inverse[0:length]
    sign = signs(length, groups)
    for level, ref in enumerate(gf_refs):
        for place, index in enumerate(range(1 << level, blocks, 2 << level) or (0,)):
            block = me ^ index
            re = cross[block, 0:length] + sign * cross[block + 1, length:]
            im = cross[block, length:] - sign * cross[block + 1, 0:length]
            ref[place] = table_dot(inverse, jnp.concatenate([re, im], axis=0))


def filter_windows(blocks, filter_ref, other_head, heads, forward, spectra, filter_rows):
    length, groups = filter_ref.shape
    me = lax.axis_index("seq")
    sign = signs(length, groups)
    for edge in (0, 1, blocks + 2):
        filter_rows[edge] = jnp.zeros((length, groups), F32)
    filter_rows[me + 2] = filter_ref[...]
    filter_rows[(me ^ 1) + 2] = get_filter(other_head, 5 * HEAD, length, groups)
    for index, (own, forwarded) in enumerate(heads):
        block = me ^ (2 * (index + 1))
        filter_rows[block + 2] = get_filter(own, 3 * HEAD, length, groups)
        filter_rows[(block ^ 1) + 2] = get_filter(forwarded, 3 * HEAD, length, groups)
    previous = None
    for distance in range(blocks):
        own = table_dot(forward, filter_rows[distance + 2])
        if previous is None:
            spectra[distance] = own
        else:
            spectra[distance, 0:length] = own[0:length] - sign * previous[length:]
            spectra[distance, length:] = own[length:] + sign * previous[0:length]
        previous = own


def result_kernel(blocks, tile_width, stage, *refs):
    others = blocks // 2 - 1
    (
        rows_ref,
        taps_ref,
        filter_ref,
        conv_head,
        conv_body,
        own_head,
        other_head,
        spec_ref,
    ) = refs[:8]
    refs = refs[8:]
    heads = [refs[2 * index : 2 * index + 2] for index in range(others)]
    refs = refs[2 * others :]
    single = others == 1
    bodies = []
    for index in range(others):
        if single:
            bodies.append([(refs[0], refs[0]), (refs[1], refs[1])])
            refs = refs[2:]
        else:
            first, first_forwarded, later, later_forwarded = refs[:4]
            bodies.append(
                [
                    (first, later) if stage == 0 else (later, first),
                    (first_forwarded, later_forwarded)
                    if stage == 0
                    else (later_forwarded, first_forwarded),
                ]
            )
            refs = refs[4:]
    if stage == 0:
        outs, (spectra, filter_rows) = refs[:4], refs[4:6]
        refs = refs[6:]
    else:
        spectra, filter_rows = refs[:2]
        outs = refs[6:10]
        refs = refs[10:]
    after, acc, fix, grads, rows_out, sems = refs
    length, groups = filter_ref.shape
    width = rows_ref.shape[1]
    half, body = width // 2, length - HEAD
    margin = taps_ref.shape[1] - 1
    me = lax.axis_index("seq")
    core, chip = me % 2, me // 2
    forward, inverse = tables_in(rows_ref)
    if stage == 0:
        filter_windows(blocks, filter_ref, other_head, heads, forward, spectra, filter_rows)
    base = stage * half
    if single:
        base = jnp.where((chip == 1) == (stage == 0), 0, half)

    def wide(values):
        return jnp.concatenate([values] * (tile_width // groups), axis=1)

    def filter_row(block, row):
        return wide(filter_rows[block + 2, pl.ds(row, 1)])

    def first_rows(ref, first, lanes):
        return ref[first : first + HEAD, lanes].astype(F32) + ref[
            first + HEAD : first + 2 * HEAD, lanes
        ].astype(F32)

    def add_lower(distance, signal, spec, fresh=False):
        re, im = spec[0:length], spec[length:]
        h_re, h_im = wide(spectra[distance, 0:length]), wide(spectra[distance, length:])
        new_re = h_re * re - h_im * im
        new_im = h_re * im + h_im * re
        acc[0, 0:length] = new_re if fresh else acc[0, 0:length] + new_re
        acc[0, length:] = new_im if fresh else acc[0, length:] + new_im
        near = filter_row(distance + 1, 0) + filter_row(distance - 1, 0)
        far = filter_row(distance + 1, 1) + filter_row(distance - 1, 1)
        fix[0:1] += signal[0:1] * near
        fix[1:2] += signal[0:1] * far + signal[1:2] * near

    def add_upper(distance, signal, spec, fresh=False):
        re, im = spec[0:length], spec[length:]
        h_re, h_im = wide(spectra[distance, 0:length]), wide(spectra[distance, length:])
        new_re = h_re * re + h_im * im
        new_im = h_re * im - h_im * re
        acc[1, 0:length] = new_re if fresh else acc[1, 0:length] + new_re
        acc[1, length:] = new_im if fresh else acc[1, length:] + new_im
        fix[EDGE + 1 : EDGE + 2] += signal[0:1] * (
            filter_row(distance - 2, length - 1) + filter_row(distance, length - 1)
        )

    copies = []
    for tile in range(half // tile_width):
        lanes = pl.ds(pl.multiple_of(base + tile * tile_width, tile_width), tile_width)
        lanes_half = slice(tile * tile_width, (tile + 1) * tile_width)
        weights = [taps_ref[p, :, lanes] for p in range(3)]
        fix[...] = jnp.zeros(fix.shape, F32)
        after[...] = jnp.zeros(after.shape, F32)

        add_lower(0, first_rows(own_head, 0, lanes), spec_ref[core, :, lanes], True)
        add_upper(0, first_rows(own_head, 2 * HEAD, lanes), spec_ref[2 + core, :, lanes], True)

        def edge_rows(ref, first):
            rows = ref[first : first + HEAD, lanes].astype(F32)
            after[...] = rows[0:EDGE] + rows[EDGE:]

        @pl.when(core == 1)
        def _():
            add_lower(1, first_rows(other_head, 0, lanes), spec_ref[0, :, lanes])

        @pl.when(core == 0)
        def _():
            add_upper(1, first_rows(other_head, 2 * HEAD, lanes), spec_ref[3, :, lanes])
            edge_rows(other_head, 4 * HEAD)

        for index in range(others):
            other = chip ^ (index + 1)
            for side in range(2):
                head_ref = heads[index][side]
                body_low, body_high = bodies[index][side]
                block = 2 * other + (core if side == 0 else 1 - core)

                @pl.when(other < chip)
                def _():
                    spec = spectrum(forward, head_ref, 0, lanes, body_low, 0, lanes_half)
                    add_lower(me - block, first_rows(head_ref, 0, lanes), spec)

                @pl.when(other > chip)
                def _():
                    spec = spectrum(forward, head_ref, 0, lanes, body_high, 0, lanes_half)
                    add_upper(block - me, first_rows(head_ref, 0, lanes), spec)

                if side == 1:

                    @pl.when(block == me + 1)
                    def _():
                        edge_rows(head_ref, 2 * HEAD)

        after_key, after_value, after_incoming = [
            after[p * margin : (p + 1) * margin] for p in range(3)
        ]
        gated = after_key * after_value
        zero_lag, one_lag = filter_row(0, 0), filter_row(0, 1)
        fix[0:1] += gated[0:1] * zero_lag
        fix[1:2] += gated[1:2] * zero_lag + gated[0:1] * one_lag

        long_conv = table_dot(inverse, acc[0])
        gated_grad = table_dot(inverse, acc[1])
        query_conv, key_conv, value_conv = [
            jnp.concatenate([conv_head[p, :, lanes], conv_body[p, :, lanes]], axis=0)
            for p in range(3)
        ]
        incoming = rows_ref[3 * length : 4 * length, lanes].astype(F32)
        beyond = slice(length, length + margin)
        grad_edge = gated_grad[beyond] + fix[EDGE : EDGE + margin]
        grads[0, 0:length] = incoming * long_conv[0:length]
        grads[0, beyond] = after_incoming * (long_conv[beyond] + fix[0:margin])
        grads[1, 0:length] = gated_grad[0:length] * value_conv
        grads[1, beyond] = grad_edge * after_value
        grads[2, 0:length] = gated_grad[0:length] * key_conv
        grads[2, beyond] = grad_edge * after_key
        rows_out[0, :, lanes_half] = (query_conv * long_conv[0:length]).astype(BF16)
        for p in range(3):
            total = weights[p][0:1] * grads[p, 0:length]
            for shift in range(1, margin + 1):
                total = total + weights[p][shift : shift + 1] * grads[p, shift : shift + length]
            rows_out[1 + p, :, lanes_half] = total.astype(BF16)
        for p, out in enumerate(outs):
            copy = pltpu.make_async_copy(
                rows_out.at[p, :, lanes_half], out.at[:, lanes], sems.at[4 * tile + p]
            )
            copy.start()
            copies.append(copy)
    for copy in copies:
        copy.wait()


def per_device(query_rows, key_rows, value_rows, short_taps, long_filter, cotangent):
    length, width = query_rows.shape
    groups = long_filter.shape[1]
    blocks = lax.axis_size("seq")
    chans = lax.axis_size("chan")
    chips, half, body = blocks // 2, width // 2, length - HEAD
    tile_width = min(half, 256)
    tiles = half // tile_width
    bits = []
    while 2 << len(bits) < blocks:
        bits.append(2 << len(bits))
    bits.reverse()
    shape = jax.ShapeDtypeStruct
    room = 40 * 1024 * 1024

    def swap(block, bit):
        return lax.ppermute(block, "seq", [(i, i ^ bit) for i in range(blocks)])

    def call(kernel, outs, args, scratch, flops, space_in=VMEM, out_specs=None, aliases={}, limit=room):
        return list(
            pl.pallas_call(
                kernel,
                out_shape=outs,
                in_specs=[space_in] * len(args) if space_in in (VMEM, HBM) else space_in,
                out_specs=out_specs or [VMEM] * len(outs),
                scratch_shapes=scratch,
                input_output_aliases=aliases,
                compiler_params=pltpu.CompilerParams(vmem_limit_bytes=limit),
                cost_estimate=pl.CostEstimate(
                    flops=flops, bytes_accessed=4 * length * width, transcendentals=0
                ),
            )(*args)
        )

    def after(value, *others):
        return lax.optimization_barrier((value, *others))[0]

    unit = shape((2 * body, half), BF16)
    rows = jnp.concatenate(
        [query_rows, key_rows, value_rows, cotangent, dft_tables(length, width)], axis=0
    )
    pair_body, conv_body, tails, top, *own_units = call(
        functools.partial(body_kernel, bits, tile_width),
        [
            shape((4 * body, width), BF16),
            shape((3, body, width), F32),
            shape((EDGE, width), F32),
            shape((4, HEAD, width), F32),
        ]
        + [unit, unit] * len(bits),
        [rows, short_taps],
        [pltpu.VMEM((3, length, tile_width), F32)],
        length * width * 64,
    )
    own_firsts, own_laters = own_units[0::2], own_units[1::2]

    def gather(own):
        units = {}
        for bit, block in zip(bits, own):
            arrived = {bit // 2: swap(block, bit)}
            for index, unit in units.items():
                arrived[index ^ bit // 2] = swap(unit, bit)
            units.update(arrived)
        return [units[index] for index in range(1, chips)]

    firsts = gather(own_firsts)
    tails = lax.ppermute(tails, "seq", [(i, i + 1) for i in range(blocks - 1)])
    other_body = swap(pair_body, 1)
    filter_rows = length * groups // width
    conv_head, pair_head, *own_heads = call(
        functools.partial(head_kernel, bits),
        [
            shape((3, HEAD, width), F32),
            shape((5 * HEAD + 2 * filter_rows, width), BF16),
        ]
        + [shape((3 * HEAD + 2 * filter_rows, width), BF16)] * len(bits),
        [tails, top, short_taps, long_filter],
        [pltpu.VMEM((EDGE + HEAD, width), F32), pltpu.VMEM((EDGE, width), F32)],
        length * width,
    )
    other_head = swap(pair_head, 1)
    heads = gather(own_heads)
    spec, near = call(
        functools.partial(chip_kernel, tile_width, groups),
        [shape((4, 2 * length, width), F32), shape((2, 2 * length, groups), F32)],
        [pair_body, pair_head, other_body, other_head, rows],
        [],
        4 * 6 * 2 * length * length * width,
    )
    kept = call(
        functools.partial(filter_grad_kernel, blocks, tile_width),
        [
            shape((max(1, blocks >> (level + 1)), length, groups), F32)
            for level in range(len(bits) + 2)
        ],
        [spec, near, rows, *heads, *firsts],
        [pltpu.VMEM((blocks + 1, 2 * length, groups), F32)],
        6 * 2 * length * length * width,
    )

    for level in range(len(bits) + 1):
        arrived = swap(kept[level], 1 << level)
        for later in range(level + 1, len(kept)):
            first = (1 << (later - level - 1)) % arrived.shape[0]
            kept[later] = kept[later] + arrived[first :: 1 << (later - level)]
    grad_filter = kept[-1][0]

    own_laters = [after(unit, grad_filter) for unit in own_laters]
    laters = gather(own_laters)
    heads_forwarded = [swap(after(unit, kept[0]), 1) for unit in heads]
    firsts_forwarded = [swap(after(unit, kept[0]), 1) for unit in firsts]
    laters_forwarded = [swap(unit, 1) for unit in laters]
    rows_out = shape((length, width), BF16)
    windows = [
        shape((blocks, 2 * length, groups), F32),
        shape((blocks + 3, length, groups), F32),
    ]

    def results(stage, extra, outs, out_specs, extra_specs, aliased):
        args = [
            rows,
            short_taps,
            long_filter,
            conv_head,
            conv_body,
            pair_head,
            other_head,
            spec,
        ]
        for pair in zip(heads, heads_forwarded):
            args += pair
        for bodies in zip(firsts, firsts_forwarded, laters, laters_forwarded):
            if chips == 2:
                bodies = bodies[2 * stage : 2 * stage + 2]
            args += bodies
        count = len(args)
        return call(
            functools.partial(result_kernel, blocks, tile_width, stage),
            outs,
            args + extra,
            [
                pltpu.VMEM((EDGE, tile_width), F32),
                pltpu.VMEM((2, 2 * length, tile_width), F32),
                pltpu.VMEM((2 * EDGE, tile_width), F32),
                pltpu.VMEM((3, length + EDGE, tile_width), F32),
                pltpu.VMEM((4, length, half), BF16),
                pltpu.SemaphoreType.DMA((4 * tiles,)),
            ],
            2 * 6 * 2 * length * length * width,
            [VMEM] * count + extra_specs,
            out_specs,
            {count + 2 + index: index for index in range(4)} if aliased else {},
        )

    *partial, spectra, filter_windows_rows = results(
        0, [], [rows_out] * 4 + windows, [HBM] * 4 + [VMEM] * 2, [], False
    )
    final = results(
        1, [spectra, filter_windows_rows, *partial], [rows_out] * 4, [HBM] * 4, [VMEM] * 2 + [HBM] * 4, True
    )

    step = 1
    while step < chans:
        if step == 2:
            grad_filter = after(grad_filter, spectra)
        grad_filter = grad_filter + lax.ppermute(
            grad_filter, "chan", [(i, i ^ step) for i in range(chans)]
        )
        step *= 2
    return (*final, grad_filter)


def solution(mesh):
    in_specs = (
        P("seq", "chan"),
        P("seq", "chan"),
        P("seq", "chan"),
        P(None, None, "chan"),
        P("seq", None),
        P("seq", "chan"),
    )
    out_specs = (
        P("seq", "chan"),
        P("seq", "chan"),
        P("seq", "chan"),
        P("seq", "chan"),
        P("seq", None),
    )
    return jax.shard_map(
        per_device, mesh=mesh, in_specs=in_specs, out_specs=out_specs, check_vma=False
    )
```

```python
import functools

import jax
import jax.numpy as jnp
import ml_dtypes
import numpy as np
from jax import lax
from jax.experimental import pallas as pl
from jax.experimental.pallas import tpu as pltpu
from jax.sharding import PartitionSpec as P

F32 = jnp.float32
BF16 = jnp.bfloat16
EDGE = 8
HEAD = 16
VMEM = pl.BlockSpec(memory_space=pltpu.VMEM)
HBM = pl.BlockSpec(memory_space=pltpu.HBM)


def split_table(table):
    high = table.astype(ml_dtypes.bfloat16)
    low = (table - high.astype(np.float64)).astype(ml_dtypes.bfloat16)
    return high, low


def dft_tables(length):
    frequency = np.pi * (2 * np.arange(length) + 1) / (2 * length)
    into = frequency[:, None] * np.arange(length)[None, :]
    high, low = split_table(np.concatenate([np.cos(into), -np.sin(into)], axis=0))
    forward = np.concatenate([high, high, low], axis=1)
    forward = np.pad(forward, ((0, EDGE), (0, 0)))
    back = np.arange(length + EDGE)[:, None] * frequency[None, :]
    high, low = split_table(np.concatenate([np.cos(back), -np.sin(back)], axis=1) / length)
    inverse = np.concatenate([high, high, low], axis=1)
    return jnp.asarray(forward), jnp.asarray(inverse)


def halves(values):
    high = values.astype(BF16)
    return high, (values - high.astype(F32)).astype(BF16)


def table_dot(table, values):
    high, low = halves(values)
    return jnp.dot(
        table, jnp.concatenate([high, low, high], axis=0), preferred_element_type=F32
    )


def tap_sum(rows_ref, first, count, weights):
    total = weights[0:1] * rows_ref[first : first + count]
    for shift in range(1, weights.shape[0]):
        total = total + weights[shift : shift + 1] * rows_ref[first - shift : first - shift + count]
    return total


def put_filter(unit, first, filter_high, filter_low):
    length, groups = filter_high.shape
    width = unit.shape[1]
    rows = length * groups // width
    for tile in range(width // groups):
        lanes = slice(tile * groups, (tile + 1) * groups)
        part = slice(tile * rows, (tile + 1) * rows)
        unit[first : first + rows, lanes] = filter_high[part]
        unit[first + rows : first + 2 * rows, lanes] = filter_low[part]


def get_filter(unit, first, length, groups):
    width = unit.shape[1]
    rows = length * groups // width
    pieces = []
    for tile in range(width // groups):
        lanes = slice(tile * groups, (tile + 1) * groups)
        pieces.append(
            unit[first : first + rows, lanes].astype(F32)
            + unit[first + rows : first + 2 * rows, lanes].astype(F32)
        )
    return jnp.concatenate(pieces, axis=0)


def fetch_kernel(
    q_hbm, k_hbm, v_hbm, c_hbm, *refs
):
    others = refs[:4]
    rows_ref, tails_ref, *other_refs = refs[4:10]
    sems = refs[10]
    length = q_hbm.shape[0]
    sources = (q_hbm, k_hbm, v_hbm, c_hbm)
    copies = [
        pltpu.make_async_copy(source, rows_ref.at[index], sems.at[index])
        for index, source in enumerate(sources)
    ]
    copies += [
        pltpu.make_async_copy(source, target, sems.at[4 + index])
        for index, (source, target) in enumerate(zip(others, other_refs))
    ]
    for copy in copies:
        copy.start()
    for copy in copies[:3]:
        copy.wait()
    for p in range(3):
        last = rows_ref[p, length - HEAD : length].astype(F32)
        tails_ref[p * EDGE : (p + 1) * EDGE] = last[HEAD - EDGE :]
    for copy in copies[3:]:
        copy.wait()


def own_kernel(
    bits,
    tile_width,
    rows_ref,
    taps_ref,
    filter_ref,
    tails_ref,
    pair_ref,
    conv_ref,
    *refs,
):
    unit_refs, (window, edge) = refs[:-2], refs[-2:]
    length, width = rows_ref.shape[1:]
    half = width // 2
    me = lax.axis_index("seq")
    margin = taps_ref.shape[1] - 1
    filter_high, filter_low = halves(filter_ref[...])
    put_filter(pair_ref, 4 * length + HEAD, filter_high, filter_low)
    for later in unit_refs[1::2]:
        put_filter(later, 2 * length + 2 * HEAD, filter_high, filter_low)
    edge[...] = jnp.zeros(edge.shape, F32)
    for tile in range(width // tile_width):
        lanes = slice(tile * tile_width, (tile + 1) * tile_width)
        convs = []
        for p in range(3):
            window[p, 0:EDGE] = tails_ref[p * EDGE : (p + 1) * EDGE, lanes]
            window[p, EDGE:] = rows_ref[p, :, lanes].astype(F32)
            conv = tap_sum(window.at[p], EDGE, length, taps_ref[p, :, lanes])
            conv_ref[p, :, lanes] = conv
            convs.append(conv)
        incoming = rows_ref[3, :, lanes].astype(F32)
        parts = [*halves(convs[1] * convs[2]), *halves(incoming * convs[0])]
        for index, part in enumerate(parts):
            pair_ref[index * length : (index + 1) * length, lanes] = part
        for p, values in enumerate((convs[1], convs[2], incoming)):
            edge[p * margin : (p + 1) * margin] = values[0:margin]
        high = edge[...].astype(BF16).astype(F32)
        edges = jnp.concatenate([high, edge[...] - high], axis=0).astype(BF16)
        pair_ref[4 * length : 4 * length + HEAD, lanes] = edges
        in_half = tile * tile_width // half
        lanes_half = slice(tile * tile_width % half, tile * tile_width % half + tile_width)
        for index, bit in enumerate(bits):
            low_side = (me // bit) % 2 == 0
            first, later = unit_refs[2 * index : 2 * index + 2]
            place = 2 * length + in_half * HEAD
            later[place : place + HEAD, lanes_half] = edges
            target_low, target_high = (first, later) if in_half == 0 else (later, first)

            @pl.when(low_side)
            def _():
                target_low[0:length, lanes_half] = parts[0]
                target_low[length : 2 * length, lanes_half] = parts[1]

            @pl.when(jnp.logical_not(low_side))
            def _():
                target_high[0:length, lanes_half] = parts[2]
                target_high[length : 2 * length, lanes_half] = parts[3]


def spectrum(forward, high, low):
    return jnp.dot(
        forward, jnp.concatenate([high, low, high], axis=0), preferred_element_type=F32
    )


def cross_add(cross, distance, early, late, groups):
    length = early.shape[0] // 2
    e_re, e_im = early[0:length], early[length:]
    l_re, l_im = late[0:length], late[length:]
    re = e_re * l_re + e_im * l_im
    im = e_re * l_im - e_im * l_re
    parts = range(early.shape[1] // groups)
    cross[distance, 0:length] += sum(re[:, p * groups : (p + 1) * groups] for p in parts)
    cross[distance, length:] += sum(im[:, p * groups : (p + 1) * groups] for p in parts)


def chip_kernel(tile_width, groups, own_ref, other_ref, forward_ref, spec_ref, cross_ref):
    length = forward_ref.shape[1] // 3
    width = own_ref.shape[1]
    core = lax.axis_index("seq") % 2
    forward = forward_ref[0 : 2 * length]
    cross_ref[...] = jnp.zeros(cross_ref.shape, F32)

    def one_tile(step, carry):
        lanes = pl.ds(pl.multiple_of(step * tile_width, tile_width), tile_width)
        for ref, slot in ((own_ref, core), (other_ref, 1 - core)):
            for kind in range(2):
                first = 2 * kind * length
                spec_ref[2 * kind + slot, :, lanes] = spectrum(
                    forward,
                    ref[first : first + length, lanes],
                    ref[first + length : first + 2 * length, lanes],
                )
        cross_add(cross_ref, 0, spec_ref[core, :, lanes], spec_ref[2 + core, :, lanes], groups)

        @pl.when(2 * step * tile_width // width == core)
        def _():
            cross_add(cross_ref, 1, spec_ref[0, :, lanes], spec_ref[3, :, lanes], groups)

        return carry

    lax.fori_loop(0, width // tile_width, one_tile, 0)


def filter_grad_kernel(blocks, tile_width, spec_ref, near_ref, forward_ref, inverse_ref, *refs):
    chips = blocks // 2
    units = refs[: chips - 1]
    gf_refs, cross = refs[chips - 1 : -1], refs[-1]
    length = forward_ref.shape[1] // 3
    groups = near_ref.shape[2]
    half = spec_ref.shape[2] // 2
    me = lax.axis_index("seq")
    core, chip = me % 2, me // 2
    forward = forward_ref[0 : 2 * length]
    cross[0:2] = near_ref[...]
    cross[2:] = jnp.zeros((blocks - 1, 2 * length, groups), F32)
    for index, unit in enumerate(units):
        other = chip ^ (index + 1)

        def one_tile(step, carry):
            start = pl.multiple_of(step * tile_width, tile_width)
            lanes = pl.ds(start, tile_width)
            spec = spectrum(forward, unit[0:length, lanes], unit[length : 2 * length, lanes])

            @pl.when(other < chip)
            def _():
                for slot in range(2):
                    distance = 2 * chip + slot - (2 * other + core)
                    cross_add(cross, distance, spec, spec_ref[2 + slot, :, lanes], groups)

            @pl.when(other > chip)
            def _():
                upper = pl.ds(pl.multiple_of(half + start, tile_width), tile_width)
                for slot in range(2):
                    distance = 2 * other + core - (2 * chip + slot)
                    cross_add(cross, distance, spec_ref[slot, :, upper], spec, groups)

            return carry

        lax.fori_loop(0, half // tile_width, one_tile, 0)

    inverse = inverse_ref[0:length]
    sign = signs(length, groups)
    for parity, ref in zip((1, 0), gf_refs):
        for place in range(blocks // 2):
            block = me ^ (2 * place + parity)
            re = cross[block, 0:length] + sign * cross[block + 1, length:]
            im = cross[block, length:] - sign * cross[block + 1, 0:length]
            ref[place] = table_dot(inverse, jnp.concatenate([re, im], axis=0))


def signs(length, groups):
    row = lax.broadcasted_iota(jnp.int32, (length, groups), 0)
    return jnp.where(row % 2 == 0, 1.0, -1.0)


def result_kernel(blocks, tile_width, stage, *refs):
    others = blocks // 2 - 1
    (
        rows_ref,
        taps_ref,
        filter_ref,
        conv_ref,
        own_ref,
        other_ref,
        spec_ref,
        forward_ref,
        inverse_ref,
    ) = refs[:9]
    refs = refs[9:]
    units = [refs[4 * index : 4 * index + 4] for index in range(others)]
    refs = refs[4 * others :]
    if stage == 0:
        outs, (spectra, filter_rows) = refs[:4], refs[4:6]
        refs = refs[6:]
    else:
        spectra, filter_rows = refs[:2]
        outs = refs[6:10]
        refs = refs[10:]
    after, acc, fix, grads, rows_out, sems = refs
    length, width = rows_ref.shape[1:]
    groups = filter_ref.shape[1]
    half = width // 2
    margin = taps_ref.shape[1] - 1
    me = lax.axis_index("seq")
    core, chip = me % 2, me // 2
    forward, inverse = forward_ref[0 : 2 * length], inverse_ref[...]

    if stage == 0:
        sign = signs(length, groups)
        for edge in (0, 1, blocks + 2):
            filter_rows[edge] = jnp.zeros((length, groups), F32)
        filter_rows[me + 2] = filter_ref[...]
        filter_rows[(me ^ 1) + 2] = get_filter(other_ref, 4 * length + HEAD, length, groups)
        for index, unit in enumerate(units):
            block = me ^ (2 * (index + 1))
            first = 2 * length + 2 * HEAD
            filter_rows[block + 2] = get_filter(unit[1], first, length, groups)
            filter_rows[(block ^ 1) + 2] = get_filter(unit[3], first, length, groups)
        previous = None
        for distance in range(blocks):
            own = table_dot(forward, filter_rows[distance + 2])
            if previous is None:
                spectra[distance] = own
            else:
                spectra[distance, 0:length] = own[0:length] - sign * previous[length:]
                spectra[distance, length:] = own[length:] + sign * previous[0:length]
            previous = own

    def wide(values):
        return jnp.concatenate([values] * (tile_width // groups), axis=1)

    def filter_row(block, row):
        return wide(filter_rows[block + 2, pl.ds(row, 1)])

    def first_rows(ref, first, lanes):
        return (
            ref[first : first + HEAD, lanes].astype(F32)
            + ref[first + length : first + length + HEAD, lanes].astype(F32)
        )

    def add_lower(distance, signal, spec, fresh=False):
        re, im = spec[0:length], spec[length:]
        h_re, h_im = wide(spectra[distance, 0:length]), wide(spectra[distance, length:])
        new_re = h_re * re - h_im * im
        new_im = h_re * im + h_im * re
        acc[0, 0:length] = new_re if fresh else acc[0, 0:length] + new_re
        acc[0, length:] = new_im if fresh else acc[0, length:] + new_im
        near = filter_row(distance + 1, 0) + filter_row(distance - 1, 0)
        far = filter_row(distance + 1, 1) + filter_row(distance - 1, 1)
        fix[0:1] += signal[0:1] * near
        fix[1:2] += signal[0:1] * far + signal[1:2] * near

    def add_upper(distance, signal, spec, fresh=False):
        re, im = spec[0:length], spec[length:]
        h_re, h_im = wide(spectra[distance, 0:length]), wide(spectra[distance, length:])
        new_re = h_re * re + h_im * im
        new_im = h_re * im - h_im * re
        acc[1, 0:length] = new_re if fresh else acc[1, 0:length] + new_re
        acc[1, length:] = new_im if fresh else acc[1, length:] + new_im
        fix[EDGE + 1 : EDGE + 2] += signal[0:1] * (
            filter_row(distance - 2, length - 1) + filter_row(distance, length - 1)
        )

    copies = []
    for tile in range(half // tile_width):
        start = stage * half + tile * tile_width
        lanes = slice(start, start + tile_width)
        lanes_half = slice(tile * tile_width, (tile + 1) * tile_width)
        weights = [taps_ref[p, :, lanes] for p in range(3)]
        fix[...] = jnp.zeros(fix.shape, F32)
        after[...] = jnp.zeros(after.shape, F32)

        add_lower(0, first_rows(own_ref, 0, lanes), spec_ref[core, :, lanes], True)
        add_upper(0, first_rows(own_ref, 2 * length, lanes), spec_ref[2 + core, :, lanes], True)

        def edge_rows(rows):
            rows = rows.astype(F32)
            after[...] = rows[0:EDGE] + rows[EDGE:]

        @pl.when(core == 1)
        def _():
            add_lower(1, first_rows(other_ref, 0, lanes), spec_ref[0, :, lanes])

        @pl.when(core == 0)
        def _():
            add_upper(1, first_rows(other_ref, 2 * length, lanes), spec_ref[3, :, lanes])
            edge_rows(other_ref[4 * length : 4 * length + HEAD, lanes])

        for index, unit in enumerate(units):
            other = chip ^ (index + 1)
            for side in range(2):
                first, later = unit[2 * side : 2 * side + 2]
                body_low, body_high = (first, later) if stage == 0 else (later, first)
                block = 2 * other + (core if side == 0 else 1 - core)

                def spec_of(ref):
                    return spectrum(
                        forward, ref[0:length, lanes_half], ref[length : 2 * length, lanes_half]
                    )

                @pl.when(other < chip)
                def _():
                    signal = first_rows(body_low, 0, lanes_half)
                    add_lower(me - block, signal, spec_of(body_low))

                @pl.when(other > chip)
                def _():
                    signal = first_rows(body_high, 0, lanes_half)
                    add_upper(block - me, signal, spec_of(body_high))

            @pl.when((other == chip + 1) & (core == 1))
            def _():
                place = 2 * length + stage * HEAD
                edge_rows(unit[3][place : place + HEAD, lanes_half])

        after_key, after_value, after_incoming = [
            after[p * margin : (p + 1) * margin] for p in range(3)
        ]
        gated = after_key * after_value
        zero_lag, one_lag = filter_row(0, 0), filter_row(0, 1)
        fix[0:1] += gated[0:1] * zero_lag
        fix[1:2] += gated[1:2] * zero_lag + gated[0:1] * one_lag

        long_conv = table_dot(inverse, acc[0])
        gated_grad = table_dot(inverse, acc[1])
        query_conv, key_conv, value_conv = [conv_ref[p, :, lanes] for p in range(3)]
        incoming = rows_ref[3, :, lanes].astype(F32)
        beyond = slice(length, length + margin)
        grad_edge = gated_grad[beyond] + fix[EDGE : EDGE + margin]
        grads[0, 0:length] = incoming * long_conv[0:length]
        grads[0, beyond] = after_incoming * (long_conv[beyond] + fix[0:margin])
        grads[1, 0:length] = gated_grad[0:length] * value_conv
        grads[1, beyond] = grad_edge * after_value
        grads[2, 0:length] = gated_grad[0:length] * key_conv
        grads[2, beyond] = grad_edge * after_key
        rows_out[0, :, lanes_half] = (query_conv * long_conv[0:length]).astype(BF16)
        for p in range(3):
            total = weights[p][0:1] * grads[p, 0:length]
            for shift in range(1, margin + 1):
                total = total + weights[p][shift : shift + 1] * grads[p, shift : shift + length]
            rows_out[1 + p, :, lanes_half] = total.astype(BF16)
        for p, out in enumerate(outs):
            copy = pltpu.make_async_copy(
                rows_out.at[p, :, lanes_half], out.at[:, lanes], sems.at[4 * tile + p]
            )
            copy.start()
            copies.append(copy)
    for copy in copies:
        copy.wait()


def per_device(query_rows, key_rows, value_rows, short_taps, long_filter, cotangent):
    length, width = query_rows.shape
    groups = long_filter.shape[1]
    blocks = lax.axis_size("seq")
    chans = lax.axis_size("chan")
    chips, half = blocks // 2, width // 2
    tile_width = min(half, 256)
    tiles = half // tile_width
    bits = []
    while 2 << len(bits) < blocks:
        bits.append(2 << len(bits))
    bits.reverse()
    forward, inverse = dft_tables(length)
    shape = jax.ShapeDtypeStruct

    def swap(block, bit):
        return lax.ppermute(block, "seq", [(i, i ^ bit) for i in range(blocks)])

    def call(kernel, outs, args, scratch, in_specs=None, out_specs=None, aliases={}, cost=1):
        return list(
            pl.pallas_call(
                kernel,
                out_shape=outs,
                in_specs=in_specs or [VMEM] * len(args),
                out_specs=out_specs or [VMEM] * len(outs),
                scratch_shapes=scratch,
                input_output_aliases=aliases,
                compiler_params=pltpu.CompilerParams(vmem_limit_bytes=40 * 1024 * 1024),
                cost_estimate=pl.CostEstimate(flops=1, bytes_accessed=cost, transcendentals=0),
            )(*args)
        )

    def after(value, *others):
        return lax.optimization_barrier((value, *others))[0]

    rows, tails, short_taps, long_filter, forward, inverse = call(
        fetch_kernel,
        [
            shape((4, length, width), BF16),
            shape((3 * EDGE, width), F32),
            shape(short_taps.shape, F32),
            shape(long_filter.shape, F32),
            shape(forward.shape, BF16),
            shape(inverse.shape, BF16),
        ],
        [
            pltpu.with_memory_space_constraint(array, pltpu.HBM)
            for array in (
                query_rows,
                key_rows,
                value_rows,
                cotangent,
                short_taps,
                long_filter,
                forward,
                inverse,
            )
        ],
        [pltpu.SemaphoreType.DMA((8,))],
        [HBM] * 8,
    )
    tails = lax.ppermute(tails, "seq", [(i, i + 1) for i in range(blocks - 1)])
    filter_rows = length * groups // width
    pair_shape = shape((4 * length + HEAD + 2 * filter_rows, width), BF16)
    first_shape = shape((2 * length, half), BF16)
    later_shape = shape((2 * length + 2 * HEAD + 4 * filter_rows, half), BF16)
    pair, conv, *own_units = call(
        functools.partial(own_kernel, bits, tile_width),
        [pair_shape, shape((3, length, width), F32)] + [first_shape, later_shape] * len(bits),
        [rows, short_taps, long_filter, tails],
        [pltpu.VMEM((3, EDGE + length, tile_width), F32), pltpu.VMEM((EDGE, tile_width), F32)],
    )

    def gather(own):
        units = {}
        for bit, block in zip(bits, own):
            arrived = {bit // 2: swap(block, bit)}
            for index, unit in units.items():
                arrived[index ^ bit // 2] = swap(unit, bit)
            units.update(arrived)
        return [units[index] for index in range(1, chips)]

    firsts = gather(own_units[0::2])
    sibling = swap(pair, 1)
    laters = gather(own_units[1::2])
    spec, near = call(
        functools.partial(chip_kernel, tile_width, groups),
        [shape((4, 2 * length, width), F32), shape((2, 2 * length, groups), F32)],
        [pair, sibling, forward],
        [],
    )
    odd, even = call(
        functools.partial(filter_grad_kernel, blocks, tile_width),
        [shape((blocks // 2, length, groups), F32)] * 2,
        [spec, near, forward, inverse, *firsts],
        [pltpu.VMEM((blocks + 1, 2 * length, groups), F32)],
    )
    even = even + swap(odd, 1)
    step = 1
    if chans > 1:
        even = even + lax.ppermute(even, "chan", [(i, i ^ 1) for i in range(chans)])
        step = 2
    even = after(even, *laters)
    units = []
    for first, later in zip(firsts, laters):
        units += [first, later, swap(after(first, even), 1), swap(after(later, even), 1)]
    for bit in reversed(bits):
        arrived = swap(even[1::2], bit)
        even = even[0::2] + arrived
    grad_filter = even[0]

    rows_out = shape((length, width), BF16)
    windows = [
        shape((blocks, 2 * length, groups), F32),
        shape((blocks + 3, length, groups), F32),
    ]

    def results(stage, extra, outs, out_specs):
        args = [rows, short_taps, long_filter, conv, pair, sibling, spec, forward, inverse, *units]
        count = len(args)
        return call(
            functools.partial(result_kernel, blocks, tile_width, stage),
            outs,
            args + extra,
            [
                pltpu.VMEM((EDGE, tile_width), F32),
                pltpu.VMEM((2, 2 * length, tile_width), F32),
                pltpu.VMEM((2 * EDGE, tile_width), F32),
                pltpu.VMEM((3, length + EDGE, tile_width), F32),
                pltpu.VMEM((4, length, half), BF16),
                pltpu.SemaphoreType.DMA((4 * tiles,)),
            ],
            [VMEM] * count + ([VMEM] * 2 + [HBM] * 4 if extra else []),
            out_specs,
            {count + 2 + index: index for index in range(4)} if extra else {},
            80 * length * width,
        )

    *partial, spectra, filter_blocks = results(
        0, [], [rows_out] * 4 + windows, [HBM] * 4 + [VMEM] * 2
    )
    final = results(1, [spectra, filter_blocks, *partial], [rows_out] * 4, [HBM] * 4)

    while step < chans:
        arrived = lax.ppermute(grad_filter, "chan", [(i, i ^ step) for i in range(chans)])
        if 2 * step < chans <= 4 * step:
            grad_filter = after(grad_filter, spectra)
        grad_filter = grad_filter + arrived
        step *= 2
    return (*final, grad_filter)


def solution(mesh):
    in_specs = (
        P("seq", "chan"),
        P("seq", "chan"),
        P("seq", "chan"),
        P(None, None, "chan"),
        P("seq", None),
        P("seq", "chan"),
    )
    out_specs = (
        P("seq", "chan"),
        P("seq", "chan"),
        P("seq", "chan"),
        P("seq", "chan"),
        P("seq", None),
    )
    return jax.shard_map(
        per_device, mesh=mesh, in_specs=in_specs, out_specs=out_specs, check_vma=False
    )
```

```python
import functools

import jax
import jax.numpy as jnp
import ml_dtypes
import numpy as np
from jax import lax
from jax.experimental import pallas as pl
from jax.experimental.pallas import tpu as pltpu
from jax.sharding import PartitionSpec as P

F32 = jnp.float32
BF16 = jnp.bfloat16
EDGE = 8
HEAD = 16
VMEM = pl.BlockSpec(memory_space=pltpu.VMEM)
HBM = pl.BlockSpec(memory_space=pltpu.HBM)


def split_table(table):
    high = table.astype(ml_dtypes.bfloat16)
    low = (table - high.astype(np.float64)).astype(ml_dtypes.bfloat16)
    return high, low


def dft_tables(length):
    frequency = np.pi * (2 * np.arange(length) + 1) / (2 * length)
    into = frequency[:, None] * np.arange(length)[None, :]
    high, low = split_table(np.concatenate([np.cos(into), -np.sin(into)], axis=0))
    forward = np.concatenate([high, high, low], axis=1)
    forward = np.pad(forward, ((0, EDGE), (0, 0)))
    back = np.arange(length + EDGE)[:, None] * frequency[None, :]
    high, low = split_table(np.concatenate([np.cos(back), -np.sin(back)], axis=1) / length)
    inverse = np.concatenate([high, high, low], axis=1)
    return jnp.asarray(forward), jnp.asarray(inverse)


def halves(values):
    high = values.astype(BF16)
    return high, (values - high.astype(F32)).astype(BF16)


def table_dot(table, values):
    high, low = halves(values)
    return jnp.dot(
        table, jnp.concatenate([high, low, high], axis=0), preferred_element_type=F32
    )


def tap_sum(rows_ref, first, count, weights):
    total = weights[0:1] * rows_ref[first : first + count]
    for shift in range(1, weights.shape[0]):
        total = total + weights[shift : shift + 1] * rows_ref[first - shift : first - shift + count]
    return total


def put_filter(unit, first, filter_high, filter_low):
    length, groups = filter_high.shape
    width = unit.shape[1]
    rows = length * groups // width
    for tile in range(width // groups):
        lanes = slice(tile * groups, (tile + 1) * groups)
        part = slice(tile * rows, (tile + 1) * rows)
        unit[first : first + rows, lanes] = filter_high[part]
        unit[first + rows : first + 2 * rows, lanes] = filter_low[part]


def get_filter(unit, first, length, groups):
    width = unit.shape[1]
    rows = length * groups // width
    pieces = []
    for tile in range(width // groups):
        lanes = slice(tile * groups, (tile + 1) * groups)
        pieces.append(
            unit[first : first + rows, lanes].astype(F32)
            + unit[first + rows : first + 2 * rows, lanes].astype(F32)
        )
    return jnp.concatenate(pieces, axis=0)


def fetch_kernel(q_hbm, k_hbm, v_hbm, c_hbm, *refs):
    others = refs[:4]
    rows_ref, marks_ref, *other_refs = refs[4:10]
    edge, sems = refs[10:]
    length = q_hbm.shape[0]
    copies = [
        pltpu.make_async_copy(source, rows_ref.at[index], sems.at[index])
        for index, source in enumerate((q_hbm, k_hbm, v_hbm, c_hbm))
    ]
    copies += [
        pltpu.make_async_copy(source, target, sems.at[4 + index])
        for index, (source, target) in enumerate(zip(others, other_refs))
    ]
    for copy in copies:
        copy.start()
    for copy in copies[:4]:
        copy.wait()
    margin = others[0].shape[1] - 1
    edge[...] = jnp.zeros(edge.shape, F32)
    for p in range(4):
        first = rows_ref[p, 0:HEAD].astype(F32)
        edge[(3 + p) * margin : (4 + p) * margin] = first[0:margin]
        if p < 3:
            last = rows_ref[p, length - HEAD :].astype(F32)
            edge[p * margin : (p + 1) * margin] = last[HEAD - margin :]
    marks_ref[...] = edge[...].astype(BF16)
    for copy in copies[4:]:
        copy.wait()


def own_kernel(bits, tile_width, rows_ref, taps_ref, filter_ref, pair_ref, conv_ref, *refs):
    unit_refs, window = refs[:-1], refs[-1]
    length, width = rows_ref.shape[1:]
    half = width // 2
    me = lax.axis_index("seq")
    filter_high, filter_low = halves(filter_ref[...])
    put_filter(pair_ref, 4 * length, filter_high, filter_low)
    for later in unit_refs[1::2]:
        put_filter(later, 2 * length, filter_high, filter_low)
    window[:, 0:EDGE] = jnp.zeros((3, EDGE, tile_width), F32)
    for tile in range(width // tile_width):
        lanes = slice(tile * tile_width, (tile + 1) * tile_width)
        convs = []
        for p in range(3):
            window[p, EDGE:] = rows_ref[p, :, lanes].astype(F32)
            conv = tap_sum(window.at[p], EDGE, length, taps_ref[p, :, lanes])
            conv_ref[p, :, lanes] = conv
            convs.append(conv)
        incoming = rows_ref[3, :, lanes].astype(F32)
        parts = [*halves(convs[1] * convs[2]), *halves(incoming * convs[0])]
        for index, part in enumerate(parts):
            pair_ref[index * length : (index + 1) * length, lanes] = part
        in_half = tile * tile_width // half
        lanes_half = slice(tile * tile_width % half, tile * tile_width % half + tile_width)
        for index, bit in enumerate(bits):
            low_side = (me // bit) % 2 == 0
            first, later = unit_refs[2 * index : 2 * index + 2]
            target_low, target_high = (first, later) if in_half == 0 else (later, first)

            @pl.when(low_side)
            def _():
                target_low[0:length, lanes_half] = parts[0]
                target_low[length : 2 * length, lanes_half] = parts[1]

            @pl.when(jnp.logical_not(low_side))
            def _():
                target_high[0:length, lanes_half] = parts[2]
                target_high[length : 2 * length, lanes_half] = parts[3]


def first_kernel(marks_refs, taps_ref, own_marks, *refs):
    arrived = refs[:marks_refs]
    firsts_ref, conv_ref, after_ref, marks, convs, window = refs[marks_refs:]
    blocks = firsts_ref.shape[0]
    me = lax.axis_index("seq")
    margin = taps_ref.shape[1] - 1
    nothing = jnp.zeros(marks.shape[1:], F32)
    marks[0] = nothing
    marks[blocks + 1] = nothing
    marks[me + 1] = own_marks[...].astype(F32)
    index = 1
    for ref in arrived:
        for place in range(ref.shape[0] // HEAD):
            marks[(me ^ index_of(index, blocks)) + 1] = ref[
                place * HEAD : (place + 1) * HEAD
            ].astype(F32)
            index += 1
    window[...] = jnp.zeros(window.shape, F32)
    convs[blocks] = jnp.zeros(convs.shape[1:], F32)
    for block in range(blocks):
        for p in range(3):
            window[EDGE - margin : EDGE] = marks[block, p * margin : (p + 1) * margin]
            window[EDGE : EDGE + margin] = marks[block + 1, (3 + p) * margin : (4 + p) * margin]
            convs[block, p] = tap_sum(window, EDGE, EDGE, taps_ref[p])
        window[EDGE : EDGE + margin] = marks[block + 1, 6 * margin : 7 * margin]
        firsts_ref[block, 0] = convs[block, 1] * convs[block, 2]
        firsts_ref[block, 1] = window[EDGE:] * convs[block, 0]
    conv_ref[...] = convs[me]
    after_ref[0:2] = convs[me + 1, 1:3]
    window[EDGE : EDGE + margin] = marks[me + 2, 6 * margin : 7 * margin]
    after_ref[2] = window[EDGE:]


def index_of(count, blocks):
    order, bit = [0], blocks // 2
    while bit:
        order += [index ^ bit for index in order]
        bit //= 2
    return order[count]


def with_first(margin, first, rows):
    true = jnp.concatenate([first, jnp.zeros((HEAD - EDGE, first.shape[1]), F32)], axis=0)
    row = lax.broadcasted_iota(jnp.int32, true.shape, 0)
    return jnp.where(row < margin, true, rows)


def spectrum(forward, margin, first, ref, place, lanes):
    length = forward.shape[1] // 3
    parts = []
    for index, part in enumerate(halves(first)):
        begin = place + index * length
        head = with_first(margin, part.astype(F32), ref[begin : begin + HEAD, lanes].astype(F32))
        parts += [head.astype(BF16), ref[begin + HEAD : begin + length, lanes]]
    return jnp.dot(
        forward, jnp.concatenate([*parts, *parts[0:2]], axis=0), preferred_element_type=F32
    )


def cross_add(cross, distance, early, late, groups):
    length = early.shape[0] // 2
    e_re, e_im = early[0:length], early[length:]
    l_re, l_im = late[0:length], late[length:]
    re = e_re * l_re + e_im * l_im
    im = e_re * l_im - e_im * l_re
    parts = range(early.shape[1] // groups)
    cross[distance, 0:length] += sum(re[:, p * groups : (p + 1) * groups] for p in parts)
    cross[distance, length:] += sum(im[:, p * groups : (p + 1) * groups] for p in parts)


def chip_kernel(
    tile_width,
    groups,
    margin,
    own_ref,
    other_ref,
    firsts_ref,
    forward_ref,
    spec_ref,
    cross_ref,
):
    length = forward_ref.shape[1] // 3
    width = own_ref.shape[1]
    me = lax.axis_index("seq")
    core = me % 2
    forward = forward_ref[0 : 2 * length]
    cross_ref[...] = jnp.zeros(cross_ref.shape, F32)

    def one_tile(step, carry):
        lanes = pl.ds(pl.multiple_of(step * tile_width, tile_width), tile_width)
        for ref, slot, block in ((own_ref, core, me), (other_ref, 1 - core, me ^ 1)):
            for kind in range(2):
                first = firsts_ref[block, kind, :, lanes]
                spec_ref[2 * kind + slot, :, lanes] = spectrum(
                    forward, margin, first, ref, 2 * kind * length, lanes
                )
        cross_add(cross_ref, 0, spec_ref[core, :, lanes], spec_ref[2 + core, :, lanes], groups)

        @pl.when(2 * step * tile_width // width == core)
        def _():
            cross_add(cross_ref, 1, spec_ref[0, :, lanes], spec_ref[3, :, lanes], groups)

        return carry

    lax.fori_loop(0, width // tile_width, one_tile, 0)


def filter_grad_kernel(
    blocks,
    tile_width,
    margin,
    spec_ref,
    near_ref,
    firsts_ref,
    forward_ref,
    inverse_ref,
    *refs,
):
    chips = blocks // 2
    units = refs[: chips - 1]
    gf_refs, cross = refs[chips - 1 : -1], refs[-1]
    length = forward_ref.shape[1] // 3
    groups = near_ref.shape[2]
    half = spec_ref.shape[2] // 2
    me = lax.axis_index("seq")
    core, chip = me % 2, me // 2
    forward = forward_ref[0 : 2 * length]
    cross[0:2] = near_ref[...]
    cross[2:] = jnp.zeros((blocks - 1, 2 * length, groups), F32)
    for index, unit in enumerate(units):
        other = chip ^ (index + 1)

        def one_tile(step, carry):
            start = pl.multiple_of(step * tile_width, tile_width)
            lanes = pl.ds(start, tile_width)
            kind = jnp.where(other < chip, 0, 1)
            wide_lanes = pl.ds(pl.multiple_of(kind * half + start, tile_width), tile_width)
            first = firsts_ref[2 * other + core, kind, :, wide_lanes]
            spec = spectrum(forward, margin, first, unit, 0, lanes)

            @pl.when(other < chip)
            def _():
                for slot in range(2):
                    distance = 2 * chip + slot - (2 * other + core)
                    cross_add(cross, distance, spec, spec_ref[2 + slot, :, wide_lanes], groups)

            @pl.when(other > chip)
            def _():
                for slot in range(2):
                    distance = 2 * other + core - (2 * chip + slot)
                    cross_add(cross, distance, spec_ref[slot, :, wide_lanes], spec, groups)

            return carry

        lax.fori_loop(0, half // tile_width, one_tile, 0)

    inverse = inverse_ref[0:length]
    sign = signs(length, groups)
    for parity, ref in zip((1, 0), gf_refs):
        for place in range(blocks // 2):
            block = me ^ (2 * place + parity)
            re = cross[block, 0:length] + sign * cross[block + 1, length:]
            im = cross[block, length:] - sign * cross[block + 1, 0:length]
            ref[place] = table_dot(inverse, jnp.concatenate([re, im], axis=0))


def signs(length, groups):
    row = lax.broadcasted_iota(jnp.int32, (length, groups), 0)
    return jnp.where(row % 2 == 0, 1.0, -1.0)


def result_kernel(blocks, tile_width, stage, *refs):
    others = blocks // 2 - 1
    (
        rows_ref,
        taps_ref,
        filter_ref,
        conv_ref,
        conv_first,
        firsts_ref,
        after_ref,
        other_ref,
        spec_ref,
        forward_ref,
        inverse_ref,
    ) = refs[:11]
    refs = refs[11:]
    units = [refs[4 * index : 4 * index + 4] for index in range(others)]
    refs = refs[4 * others :]
    if stage == 0:
        outs, (spectra, filter_rows) = refs[:4], refs[4:6]
        refs = refs[6:]
    else:
        spectra, filter_rows = refs[:2]
        outs = refs[6:10]
        refs = refs[10:]
    acc, fix, grads, rows_out, sems = refs
    length, width = rows_ref.shape[1:]
    groups = filter_ref.shape[1]
    half = width // 2
    margin = taps_ref.shape[1] - 1
    me = lax.axis_index("seq")
    core, chip = me % 2, me // 2
    forward, inverse = forward_ref[0 : 2 * length], inverse_ref[...]

    if stage == 0:
        sign = signs(length, groups)
        for edge in (0, 1, blocks + 2):
            filter_rows[edge] = jnp.zeros((length, groups), F32)
        filter_rows[me + 2] = filter_ref[...]
        filter_rows[(me ^ 1) + 2] = get_filter(other_ref, 4 * length, length, groups)
        for index, unit in enumerate(units):
            block = me ^ (2 * (index + 1))
            filter_rows[block + 2] = get_filter(unit[1], 2 * length, length, groups)
            filter_rows[(block ^ 1) + 2] = get_filter(unit[3], 2 * length, length, groups)
        previous = None
        for distance in range(blocks):
            own = table_dot(forward, filter_rows[distance + 2])
            if previous is None:
                spectra[distance] = own
            else:
                spectra[distance, 0:length] = own[0:length] - sign * previous[length:]
                spectra[distance, length:] = own[length:] + sign * previous[0:length]
            previous = own

    def wide(values):
        return jnp.concatenate([values] * (tile_width // groups), axis=1)

    def filter_row(block, row):
        return wide(filter_rows[block + 2, pl.ds(row, 1)])

    def add_lower(distance, signal, spec, fresh=False):
        re, im = spec[0:length], spec[length:]
        h_re, h_im = wide(spectra[distance, 0:length]), wide(spectra[distance, length:])
        new_re = h_re * re - h_im * im
        new_im = h_re * im + h_im * re
        acc[0, 0:length] = new_re if fresh else acc[0, 0:length] + new_re
        acc[0, length:] = new_im if fresh else acc[0, length:] + new_im
        near = filter_row(distance + 1, 0) + filter_row(distance - 1, 0)
        far = filter_row(distance + 1, 1) + filter_row(distance - 1, 1)
        fix[0:1] += signal[0:1] * near
        fix[1:2] += signal[0:1] * far + signal[1:2] * near

    def add_upper(distance, signal, spec, fresh=False):
        re, im = spec[0:length], spec[length:]
        h_re, h_im = wide(spectra[distance, 0:length]), wide(spectra[distance, length:])
        new_re = h_re * re + h_im * im
        new_im = h_re * im - h_im * re
        acc[1, 0:length] = new_re if fresh else acc[1, 0:length] + new_re
        acc[1, length:] = new_im if fresh else acc[1, length:] + new_im
        fix[EDGE + 1 : EDGE + 2] += signal[0:1] * (
            filter_row(distance - 2, length - 1) + filter_row(distance, length - 1)
        )

    copies = []
    for tile in range(half // tile_width):
        start = stage * half + tile * tile_width
        lanes = slice(start, start + tile_width)
        lanes_half = slice(tile * tile_width, (tile + 1) * tile_width)
        weights = [taps_ref[p, :, lanes] for p in range(3)]
        fix[...] = jnp.zeros(fix.shape, F32)

        add_lower(0, firsts_ref[me, 0, :, lanes], spec_ref[core, :, lanes], True)
        add_upper(0, firsts_ref[me, 1, :, lanes], spec_ref[2 + core, :, lanes], True)

        @pl.when(core == 1)
        def _():
            add_lower(1, firsts_ref[me - 1, 0, :, lanes], spec_ref[0, :, lanes])

        @pl.when(core == 0)
        def _():
            add_upper(1, firsts_ref[me + 1, 1, :, lanes], spec_ref[3, :, lanes])

        for index, unit in enumerate(units):
            other = chip ^ (index + 1)
            for side in range(2):
                first, later = unit[2 * side : 2 * side + 2]
                body_low, body_high = (first, later) if stage == 0 else (later, first)
                block = 2 * other + (core if side == 0 else 1 - core)

                @pl.when(other < chip)
                def _():
                    signal = firsts_ref[block, 0, :, lanes]
                    spec = spectrum(forward, margin, signal, body_low, 0, lanes_half)
                    add_lower(me - block, signal, spec)

                @pl.when(other > chip)
                def _():
                    signal = firsts_ref[block, 1, :, lanes]
                    spec = spectrum(forward, margin, signal, body_high, 0, lanes_half)
                    add_upper(block - me, signal, spec)

        after_key, after_value, after_incoming = [
            after_ref[p, :, lanes][0:margin] for p in range(3)
        ]
        gated = after_key * after_value
        zero_lag, one_lag = filter_row(0, 0), filter_row(0, 1)
        fix[0:1] += gated[0:1] * zero_lag
        fix[1:2] += gated[1:2] * zero_lag + gated[0:1] * one_lag

        long_conv = table_dot(inverse, acc[0])
        gated_grad = table_dot(inverse, acc[1])
        query_conv, key_conv, value_conv = [
            jnp.concatenate(
                [
                    with_first(margin, conv_first[p, :, lanes], conv_ref[p, 0:HEAD, lanes]),
                    conv_ref[p, HEAD:, lanes],
                ],
                axis=0,
            )
            for p in range(3)
        ]
        incoming = rows_ref[3, :, lanes].astype(F32)
        beyond = slice(length, length + margin)
        grad_edge = gated_grad[beyond] + fix[EDGE : EDGE + margin]
        grads[0, 0:length] = incoming * long_conv[0:length]
        grads[0, beyond] = after_incoming * (long_conv[beyond] + fix[0:margin])
        grads[1, 0:length] = gated_grad[0:length] * value_conv
        grads[1, beyond] = grad_edge * after_value
        grads[2, 0:length] = gated_grad[0:length] * key_conv
        grads[2, beyond] = grad_edge * after_key
        rows_out[0, :, lanes_half] = (query_conv * long_conv[0:length]).astype(BF16)
        for p in range(3):
            total = weights[p][0:1] * grads[p, 0:length]
            for shift in range(1, margin + 1):
                total = total + weights[p][shift : shift + 1] * grads[p, shift : shift + length]
            rows_out[1 + p, :, lanes_half] = total.astype(BF16)
        for p, out in enumerate(outs):
            copy = pltpu.make_async_copy(
                rows_out.at[p, :, lanes_half], out.at[:, lanes], sems.at[4 * tile + p]
            )
            copy.start()
            copies.append(copy)
    for copy in copies:
        copy.wait()


def per_device(query_rows, key_rows, value_rows, short_taps, long_filter, cotangent):
    length, width = query_rows.shape
    groups = long_filter.shape[1]
    blocks = lax.axis_size("seq")
    chans = lax.axis_size("chan")
    chips, half = blocks // 2, width // 2
    margin = short_taps.shape[1] - 1
    tile_width = min(half, 256)
    tiles = half // tile_width
    bits = []
    while 2 << len(bits) < blocks:
        bits.append(2 << len(bits))
    bits.reverse()
    forward, inverse = dft_tables(length)
    shape = jax.ShapeDtypeStruct

    def swap(block, bit):
        return lax.ppermute(block, "seq", [(i, i ^ bit) for i in range(blocks)])

    def call(kernel, outs, args, scratch, in_specs=None, out_specs=None, aliases={}, cost=1):
        return list(
            pl.pallas_call(
                kernel,
                out_shape=outs,
                in_specs=in_specs or [VMEM] * len(args),
                out_specs=out_specs or [VMEM] * len(outs),
                scratch_shapes=scratch,
                input_output_aliases=aliases,
                compiler_params=pltpu.CompilerParams(vmem_limit_bytes=40 * 1024 * 1024),
                cost_estimate=pl.CostEstimate(flops=1, bytes_accessed=cost, transcendentals=0),
            )(*args)
        )

    def after(value, *others):
        return lax.optimization_barrier((value, *others))[0]

    rows, marks, short_taps, long_filter, forward, inverse = call(
        fetch_kernel,
        [
            shape((4, length, width), BF16),
            shape((HEAD, width), BF16),
            shape(short_taps.shape, F32),
            shape(long_filter.shape, F32),
            shape(forward.shape, BF16),
            shape(inverse.shape, BF16),
        ],
        [
            pltpu.with_memory_space_constraint(array, pltpu.HBM)
            for array in (
                query_rows,
                key_rows,
                value_rows,
                cotangent,
                short_taps,
                long_filter,
                forward,
                inverse,
            )
        ],
        [pltpu.VMEM((HEAD, width), F32), pltpu.SemaphoreType.DMA((8,))],
        [HBM] * 8,
    )
    all_marks = []
    for bit in bits + [1]:
        all_marks.append(swap(jnp.concatenate([marks] + all_marks, axis=0), bit))
    firsts_true, conv_first, after_rows = call(
        functools.partial(first_kernel, len(all_marks)),
        [
            shape((blocks, 2, EDGE, width), F32),
            shape((3, EDGE, width), F32),
            shape((3, EDGE, width), F32),
        ],
        [short_taps, marks, *all_marks],
        [
            pltpu.VMEM((blocks + 2, HEAD, width), F32),
            pltpu.VMEM((blocks + 1, 3, EDGE, width), F32),
            pltpu.VMEM((2 * EDGE, width), F32),
        ],
    )
    filter_rows = length * groups // width
    pair_shape = shape((4 * length + 2 * filter_rows, width), BF16)
    first_shape = shape((2 * length, half), BF16)
    later_shape = shape((2 * length + 4 * filter_rows, half), BF16)
    pair, conv, *own_units = call(
        functools.partial(own_kernel, bits, tile_width),
        [pair_shape, shape((3, length, width), F32)] + [first_shape, later_shape] * len(bits),
        [rows, short_taps, long_filter],
        [pltpu.VMEM((3, EDGE + length, tile_width), F32)],
    )

    def gather(own):
        units = {}
        for bit, block in zip(bits, own):
            arrived = {bit // 2: swap(block, bit)}
            for index, unit in units.items():
                arrived[index ^ bit // 2] = swap(unit, bit)
            units.update(arrived)
        return [units[index] for index in range(1, chips)]

    firsts = gather([after(unit, all_marks[0]) for unit in own_units[0::2]])
    sibling = swap(pair, 1)
    laters = gather(own_units[1::2])
    spec, near = call(
        functools.partial(chip_kernel, tile_width, groups, margin),
        [shape((4, 2 * length, width), F32), shape((2, 2 * length, groups), F32)],
        [pair, sibling, firsts_true, forward],
        [],
    )
    odd, even = call(
        functools.partial(filter_grad_kernel, blocks, tile_width, margin),
        [shape((blocks // 2, length, groups), F32)] * 2,
        [spec, near, firsts_true, forward, inverse, *firsts],
        [pltpu.VMEM((blocks + 1, 2 * length, groups), F32)],
    )
    even = even + swap(odd, 1)
    step = 1
    if chans > 1:
        even = even + lax.ppermute(even, "chan", [(i, i ^ 1) for i in range(chans)])
        step = 2
    even = after(even, *laters)
    units = []
    for first, later in zip(firsts, laters):
        units += [first, later, swap(after(first, even), 1), swap(after(later, even), 1)]
    for bit in reversed(bits):
        arrived = swap(even[1::2], bit)
        even = even[0::2] + arrived
    grad_filter = even[0]

    rows_out = shape((length, width), BF16)
    windows = [
        shape((blocks, 2 * length, groups), F32),
        shape((blocks + 3, length, groups), F32),
    ]

    def results(stage, extra, outs, out_specs):
        args = [rows, short_taps, long_filter, conv, conv_first, firsts_true, after_rows]
        args += [sibling, spec, forward, inverse, *units]
        count = len(args)
        return call(
            functools.partial(result_kernel, blocks, tile_width, stage),
            outs,
            args + extra,
            [
                pltpu.VMEM((2, 2 * length, tile_width), F32),
                pltpu.VMEM((2 * EDGE, tile_width), F32),
                pltpu.VMEM((3, length + EDGE, tile_width), F32),
                pltpu.VMEM((4, length, half), BF16),
                pltpu.SemaphoreType.DMA((4 * tiles,)),
            ],
            [VMEM] * count + ([VMEM] * 2 + [HBM] * 4 if extra else []),
            out_specs,
            {count + 2 + index: index for index in range(4)} if extra else {},
            80 * length * width,
        )

    *partial, spectra, filter_blocks = results(
        0, [], [rows_out] * 4 + windows, [HBM] * 4 + [VMEM] * 2
    )
    final = results(1, [spectra, filter_blocks, *partial], [rows_out] * 4, [HBM] * 4)

    while step < chans:
        arrived = lax.ppermute(grad_filter, "chan", [(i, i ^ step) for i in range(chans)])
        if 2 * step < chans <= 4 * step:
            grad_filter = after(grad_filter, spectra)
        grad_filter = grad_filter + arrived
        step *= 2
    return (*final, grad_filter)


def solution(mesh):
    in_specs = (
        P("seq", "chan"),
        P("seq", "chan"),
        P("seq", "chan"),
        P(None, None, "chan"),
        P("seq", None),
        P("seq", "chan"),
    )
    out_specs = (
        P("seq", "chan"),
        P("seq", "chan"),
        P("seq", "chan"),
        P("seq", "chan"),
        P("seq", None),
    )
    return jax.shard_map(
        per_device, mesh=mesh, in_specs=in_specs, out_specs=out_specs, check_vma=False
    )
```

```python
import functools

import jax
import jax.numpy as jnp
import ml_dtypes
import numpy as np
from jax import lax
from jax.experimental import pallas as pl
from jax.experimental.pallas import tpu as pltpu
from jax.sharding import PartitionSpec as P

F32 = jnp.float32
BF16 = jnp.bfloat16
EDGE = 8
HEAD = 16
VMEM = pl.BlockSpec(memory_space=pltpu.VMEM)
HBM = pl.BlockSpec(memory_space=pltpu.HBM)


def split_table(table):
    high = table.astype(ml_dtypes.bfloat16)
    low = (table - high.astype(np.float64)).astype(ml_dtypes.bfloat16)
    return high, low


def dft_tables(length):
    frequency = np.pi * (2 * np.arange(length) + 1) / (2 * length)
    into = frequency[:, None] * np.arange(length)[None, :]
    high, low = split_table(np.concatenate([np.cos(into), -np.sin(into)], axis=0))
    forward = np.concatenate([high, high, low], axis=1)
    forward = np.pad(forward, ((0, EDGE), (0, 0)))
    back = np.arange(length + EDGE)[:, None] * frequency[None, :]
    high, low = split_table(np.concatenate([np.cos(back), -np.sin(back)], axis=1) / length)
    inverse = np.concatenate([high, high, low], axis=1)
    return jnp.asarray(forward), jnp.asarray(inverse)


def halves(values):
    high = values.astype(BF16)
    return high, (values - high.astype(F32)).astype(BF16)


def table_dot(table, values):
    high, low = halves(values)
    return jnp.dot(
        table, jnp.concatenate([high, low, high], axis=0), preferred_element_type=F32
    )


def tap_sum(rows_ref, first, count, weights):
    total = weights[0:1] * rows_ref[first : first + count]
    for shift in range(1, weights.shape[0]):
        total = total + weights[shift : shift + 1] * rows_ref[first - shift : first - shift + count]
    return total


def put_filter(unit, first, filter_high, filter_low):
    length, groups = filter_high.shape
    width = unit.shape[1]
    rows = length * groups // width
    for tile in range(width // groups):
        lanes = slice(tile * groups, (tile + 1) * groups)
        part = slice(tile * rows, (tile + 1) * rows)
        unit[first : first + rows, lanes] = filter_high[part]
        unit[first + rows : first + 2 * rows, lanes] = filter_low[part]


def get_filter(unit, first, length, groups):
    width = unit.shape[1]
    rows = length * groups // width
    pieces = []
    for tile in range(width // groups):
        lanes = slice(tile * groups, (tile + 1) * groups)
        pieces.append(
            unit[first : first + rows, lanes].astype(F32)
            + unit[first + rows : first + 2 * rows, lanes].astype(F32)
        )
    return jnp.concatenate(pieces, axis=0)


def fetch_kernel(q_hbm, k_hbm, v_hbm, c_hbm, *refs):
    others = refs[:4]
    rows_ref, marks_ref, *other_refs = refs[4:10]
    edge, sems = refs[10:]
    length = q_hbm.shape[0]
    copies = [
        pltpu.make_async_copy(source, rows_ref.at[index], sems.at[index])
        for index, source in enumerate((q_hbm, k_hbm, v_hbm, c_hbm))
    ]
    copies += [
        pltpu.make_async_copy(source, target, sems.at[4 + index])
        for index, (source, target) in enumerate(zip(others, other_refs))
    ]
    for copy in copies:
        copy.start()
    for copy in copies[:4]:
        copy.wait()
    margin = others[0].shape[1] - 1
    edge[...] = jnp.zeros(edge.shape, F32)
    for p in range(4):
        first = rows_ref[p, 0:HEAD].astype(F32)
        edge[(3 + p) * margin : (4 + p) * margin] = first[0:margin]
        if p < 3:
            last = rows_ref[p, length - HEAD :].astype(F32)
            edge[p * margin : (p + 1) * margin] = last[HEAD - margin :]
    marks_ref[...] = edge[...].astype(BF16)
    for copy in copies[4:]:
        copy.wait()


def own_kernel(bits, tile_width, rows_ref, taps_ref, filter_ref, pair_ref, conv_ref, *refs):
    unit_refs, window = refs[:-1], refs[-1]
    length, width = rows_ref.shape[1:]
    half = width // 2
    me = lax.axis_index("seq")
    filter_high, filter_low = halves(filter_ref[...])
    put_filter(pair_ref, 4 * length, filter_high, filter_low)
    for later in unit_refs[1::2]:
        put_filter(later, 2 * length, filter_high, filter_low)
    window[:, 0:EDGE] = jnp.zeros((3, EDGE, tile_width), F32)
    for tile in range(width // tile_width):
        lanes = slice(tile * tile_width, (tile + 1) * tile_width)
        convs = []
        for p in range(3):
            window[p, EDGE:] = rows_ref[p, :, lanes].astype(F32)
            conv = tap_sum(window.at[p], EDGE, length, taps_ref[p, :, lanes])
            conv_ref[p, :, lanes] = conv
            convs.append(conv)
        incoming = rows_ref[3, :, lanes].astype(F32)
        parts = [*halves(convs[1] * convs[2]), *halves(incoming * convs[0])]
        for index, part in enumerate(parts):
            pair_ref[index * length : (index + 1) * length, lanes] = part
        in_half = tile * tile_width // half
        lanes_half = slice(tile * tile_width % half, tile * tile_width % half + tile_width)
        for index, bit in enumerate(bits):
            low_side = (me // bit) % 2 == 0
            first, later = unit_refs[2 * index : 2 * index + 2]
            target_low, target_high = (first, later) if in_half == 0 else (later, first)

            @pl.when(low_side)
            def _():
                target_low[0:length, lanes_half] = parts[0]
                target_low[length : 2 * length, lanes_half] = parts[1]

            @pl.when(jnp.logical_not(low_side))
            def _():
                target_high[0:length, lanes_half] = parts[2]
                target_high[length : 2 * length, lanes_half] = parts[3]


def first_kernel(marks_refs, taps_ref, own_marks, *refs):
    arrived = refs[:marks_refs]
    firsts_ref, conv_ref, after_ref, marks, convs, window = refs[marks_refs:]
    blocks = firsts_ref.shape[0]
    me = lax.axis_index("seq")
    margin = taps_ref.shape[1] - 1
    nothing = jnp.zeros(marks.shape[1:], F32)
    marks[0] = nothing
    marks[blocks + 1] = nothing
    marks[me + 1] = own_marks[...].astype(F32)
    index = 1
    for ref in arrived:
        for place in range(ref.shape[0] // HEAD):
            marks[(me ^ index_of(index, blocks)) + 1] = ref[
                place * HEAD : (place + 1) * HEAD
            ].astype(F32)
            index += 1
    window[...] = jnp.zeros(window.shape, F32)
    convs[blocks] = jnp.zeros(convs.shape[1:], F32)
    for block in range(blocks):
        for p in range(3):
            window[EDGE - margin : EDGE] = marks[block, p * margin : (p + 1) * margin]
            window[EDGE : EDGE + margin] = marks[block + 1, (3 + p) * margin : (4 + p) * margin]
            convs[block, p] = tap_sum(window, EDGE, EDGE, taps_ref[p])
        window[EDGE : EDGE + margin] = marks[block + 1, 6 * margin : 7 * margin]
        firsts_ref[block, 0] = convs[block, 1] * convs[block, 2]
        firsts_ref[block, 1] = window[EDGE:] * convs[block, 0]
    conv_ref[...] = convs[me]
    after_ref[0:2] = convs[me + 1, 1:3]
    window[EDGE : EDGE + margin] = marks[me + 2, 6 * margin : 7 * margin]
    after_ref[2] = window[EDGE:]


def index_of(count, blocks):
    order, bit = [0], blocks // 2
    while bit:
        order += [index ^ bit for index in order]
        bit //= 2
    return order[count]


def with_first(margin, first, rows):
    true = jnp.concatenate([first, jnp.zeros((HEAD - EDGE, first.shape[1]), F32)], axis=0)
    row = lax.broadcasted_iota(jnp.int32, true.shape, 0)
    return jnp.where(row < margin, true, rows)


def spectrum(forward, margin, first, ref, place, lanes):
    length = forward.shape[1] // 3
    parts = []
    for index, part in enumerate(halves(first)):
        begin = place + index * length
        head = with_first(margin, part.astype(F32), ref[begin : begin + HEAD, lanes].astype(F32))
        parts += [head.astype(BF16), ref[begin + HEAD : begin + length, lanes]]
    return jnp.dot(
        forward, jnp.concatenate([*parts, *parts[0:2]], axis=0), preferred_element_type=F32
    )


def cross_add(cross, distance, early, late, groups):
    length = early.shape[0] // 2
    e_re, e_im = early[0:length], early[length:]
    l_re, l_im = late[0:length], late[length:]
    re = e_re * l_re + e_im * l_im
    im = e_re * l_im - e_im * l_re
    parts = range(early.shape[1] // groups)
    cross[distance, 0:length] += sum(re[:, p * groups : (p + 1) * groups] for p in parts)
    cross[distance, length:] += sum(im[:, p * groups : (p + 1) * groups] for p in parts)


def chip_kernel(
    tile_width,
    groups,
    margin,
    own_ref,
    other_ref,
    firsts_ref,
    forward_ref,
    spec_ref,
    cross_ref,
):
    length = forward_ref.shape[1] // 3
    width = own_ref.shape[1]
    me = lax.axis_index("seq")
    core = me % 2
    forward = forward_ref[0 : 2 * length]
    cross_ref[...] = jnp.zeros(cross_ref.shape, F32)

    def one_tile(step, carry):
        lanes = pl.ds(pl.multiple_of(step * tile_width, tile_width), tile_width)
        for ref, slot, block in ((own_ref, core, me), (other_ref, 1 - core, me ^ 1)):
            for kind in range(2):
                first = firsts_ref[block, kind, :, lanes]
                spec_ref[2 * kind + slot, :, lanes] = spectrum(
                    forward, margin, first, ref, 2 * kind * length, lanes
                )
        cross_add(cross_ref, 0, spec_ref[core, :, lanes], spec_ref[2 + core, :, lanes], groups)

        @pl.when(2 * step * tile_width // width == core)
        def _():
            cross_add(cross_ref, 1, spec_ref[0, :, lanes], spec_ref[3, :, lanes], groups)

        return carry

    lax.fori_loop(0, width // tile_width, one_tile, 0)


def filter_grad_kernel(
    blocks,
    tile_width,
    margin,
    spec_ref,
    near_ref,
    firsts_ref,
    forward_ref,
    inverse_ref,
    *refs,
):
    chips = blocks // 2
    units = refs[: chips - 1]
    gf_refs, cross = refs[chips - 1 : -1], refs[-1]
    length = forward_ref.shape[1] // 3
    groups = near_ref.shape[2]
    half = spec_ref.shape[2] // 2
    me = lax.axis_index("seq")
    core, chip = me % 2, me // 2
    forward = forward_ref[0 : 2 * length]
    cross[0:2] = near_ref[...]
    cross[2:] = jnp.zeros((blocks - 1, 2 * length, groups), F32)
    for index, unit in enumerate(units):
        other = chip ^ (index + 1)

        def one_tile(step, carry):
            start = pl.multiple_of(step * tile_width, tile_width)
            lanes = pl.ds(start, tile_width)
            kind = jnp.where(other < chip, 0, 1)
            wide_lanes = pl.ds(pl.multiple_of(kind * half + start, tile_width), tile_width)
            first = firsts_ref[2 * other + core, kind, :, wide_lanes]
            spec = spectrum(forward, margin, first, unit, 0, lanes)

            @pl.when(other < chip)
            def _():
                for slot in range(2):
                    distance = 2 * chip + slot - (2 * other + core)
                    cross_add(cross, distance, spec, spec_ref[2 + slot, :, wide_lanes], groups)

            @pl.when(other > chip)
            def _():
                for slot in range(2):
                    distance = 2 * other + core - (2 * chip + slot)
                    cross_add(cross, distance, spec_ref[slot, :, wide_lanes], spec, groups)

            return carry

        lax.fori_loop(0, half // tile_width, one_tile, 0)

    inverse = inverse_ref[0:length]
    sign = signs(length, groups)
    for parity, ref in zip((1, 0), gf_refs):
        for place in range(blocks // 2):
            block = me ^ (2 * place + parity)
            re = cross[block, 0:length] + sign * cross[block + 1, length:]
            im = cross[block, length:] - sign * cross[block + 1, 0:length]
            ref[place] = table_dot(inverse, jnp.concatenate([re, im], axis=0))


def signs(length, groups):
    row = lax.broadcasted_iota(jnp.int32, (length, groups), 0)
    return jnp.where(row % 2 == 0, 1.0, -1.0)


def result_kernel(blocks, tile_width, stage, *refs):
    others = blocks // 2 - 1
    (
        rows_ref,
        taps_ref,
        filter_ref,
        conv_ref,
        conv_first,
        firsts_ref,
        after_ref,
        other_ref,
        spec_ref,
        forward_ref,
        inverse_ref,
    ) = refs[:11]
    refs = refs[11:]
    units = [refs[4 * index : 4 * index + 4] for index in range(others)]
    refs = refs[4 * others :]
    if stage == 0:
        outs, (spectra, filter_rows) = refs[:4], refs[4:6]
        refs = refs[6:]
    else:
        spectra, filter_rows = refs[:2]
        outs = refs[6:10]
        refs = refs[10:]
    acc, fix, grads, rows_out, sems = refs
    length, width = rows_ref.shape[1:]
    groups = filter_ref.shape[1]
    half = width // 2
    margin = taps_ref.shape[1] - 1
    me = lax.axis_index("seq")
    core, chip = me % 2, me // 2
    forward, inverse = forward_ref[0 : 2 * length], inverse_ref[...]

    if stage == 0:
        sign = signs(length, groups)
        for edge in (0, 1, blocks + 2):
            filter_rows[edge] = jnp.zeros((length, groups), F32)
        filter_rows[me + 2] = filter_ref[...]
        filter_rows[(me ^ 1) + 2] = get_filter(other_ref, 4 * length, length, groups)
        for index, unit in enumerate(units):
            block = me ^ (2 * (index + 1))
            filter_rows[block + 2] = get_filter(unit[1], 2 * length, length, groups)
            filter_rows[(block ^ 1) + 2] = get_filter(unit[3], 2 * length, length, groups)
        previous = None
        for distance in range(blocks):
            own = table_dot(forward, filter_rows[distance + 2])
            if previous is None:
                spectra[distance] = own
            else:
                spectra[distance, 0:length] = own[0:length] - sign * previous[length:]
                spectra[distance, length:] = own[length:] + sign * previous[0:length]
            previous = own

    def wide(values):
        return jnp.concatenate([values] * (tile_width // groups), axis=1)

    def filter_row(block, row):
        return wide(filter_rows[block + 2, pl.ds(row, 1)])

    def add_lower(distance, signal, spec, fresh=False):
        re, im = spec[0:length], spec[length:]
        h_re, h_im = wide(spectra[distance, 0:length]), wide(spectra[distance, length:])
        new_re = h_re * re - h_im * im
        new_im = h_re * im + h_im * re
        acc[0, 0:length] = new_re if fresh else acc[0, 0:length] + new_re
        acc[0, length:] = new_im if fresh else acc[0, length:] + new_im
        near = filter_row(distance + 1, 0) + filter_row(distance - 1, 0)
        far = filter_row(distance + 1, 1) + filter_row(distance - 1, 1)
        fix[0:1] += signal[0:1] * near
        fix[1:2] += signal[0:1] * far + signal[1:2] * near

    def add_upper(distance, signal, spec, fresh=False):
        re, im = spec[0:length], spec[length:]
        h_re, h_im = wide(spectra[distance, 0:length]), wide(spectra[distance, length:])
        new_re = h_re * re + h_im * im
        new_im = h_re * im - h_im * re
        acc[1, 0:length] = new_re if fresh else acc[1, 0:length] + new_re
        acc[1, length:] = new_im if fresh else acc[1, length:] + new_im
        fix[EDGE + 1 : EDGE + 2] += signal[0:1] * (
            filter_row(distance - 2, length - 1) + filter_row(distance, length - 1)
        )

    copies = []
    for tile in range(half // tile_width):
        start = stage * half + tile * tile_width
        lanes = slice(start, start + tile_width)
        lanes_half = slice(tile * tile_width, (tile + 1) * tile_width)
        weights = [taps_ref[p, :, lanes] for p in range(3)]
        fix[...] = jnp.zeros(fix.shape, F32)

        add_lower(0, firsts_ref[me, 0, :, lanes], spec_ref[core, :, lanes], True)
        add_upper(0, firsts_ref[me, 1, :, lanes], spec_ref[2 + core, :, lanes], True)

        @pl.when(core == 1)
        def _():
            add_lower(1, firsts_ref[me - 1, 0, :, lanes], spec_ref[0, :, lanes])

        @pl.when(core == 0)
        def _():
            add_upper(1, firsts_ref[me + 1, 1, :, lanes], spec_ref[3, :, lanes])

        for index, unit in enumerate(units):
            other = chip ^ (index + 1)
            for side in range(2):
                first, later = unit[2 * side : 2 * side + 2]
                body_low, body_high = (first, later) if stage == 0 else (later, first)
                block = 2 * other + (core if side == 0 else 1 - core)

                @pl.when(other < chip)
                def _():
                    signal = firsts_ref[block, 0, :, lanes]
                    spec = spectrum(forward, margin, signal, body_low, 0, lanes_half)
                    add_lower(me - block, signal, spec)

                @pl.when(other > chip)
                def _():
                    signal = firsts_ref[block, 1, :, lanes]
                    spec = spectrum(forward, margin, signal, body_high, 0, lanes_half)
                    add_upper(block - me, signal, spec)

        after_key, after_value, after_incoming = [
            after_ref[p, :, lanes][0:margin] for p in range(3)
        ]
        gated = after_key * after_value
        zero_lag, one_lag = filter_row(0, 0), filter_row(0, 1)
        fix[0:1] += gated[0:1] * zero_lag
        fix[1:2] += gated[1:2] * zero_lag + gated[0:1] * one_lag

        long_conv = table_dot(inverse, acc[0])
        gated_grad = table_dot(inverse, acc[1])
        query_conv, key_conv, value_conv = [
            jnp.concatenate(
                [
                    with_first(margin, conv_first[p, :, lanes], conv_ref[p, 0:HEAD, lanes]),
                    conv_ref[p, HEAD:, lanes],
                ],
                axis=0,
            )
            for p in range(3)
        ]
        incoming = rows_ref[3, :, lanes].astype(F32)
        beyond = slice(length, length + margin)
        grad_edge = gated_grad[beyond] + fix[EDGE : EDGE + margin]
        grads[0, 0:length] = incoming * long_conv[0:length]
        grads[0, beyond] = after_incoming * (long_conv[beyond] + fix[0:margin])
        grads[1, 0:length] = gated_grad[0:length] * value_conv
        grads[1, beyond] = grad_edge * after_value
        grads[2, 0:length] = gated_grad[0:length] * key_conv
        grads[2, beyond] = grad_edge * after_key
        rows_out[0, :, lanes_half] = (query_conv * long_conv[0:length]).astype(BF16)
        for p in range(3):
            total = weights[p][0:1] * grads[p, 0:length]
            for shift in range(1, margin + 1):
                total = total + weights[p][shift : shift + 1] * grads[p, shift : shift + length]
            rows_out[1 + p, :, lanes_half] = total.astype(BF16)
        for p, out in enumerate(outs):
            copy = pltpu.make_async_copy(
                rows_out.at[p, :, lanes_half], out.at[:, lanes], sems.at[4 * tile + p]
            )
            copy.start()
            copies.append(copy)
    for copy in copies:
        copy.wait()


def per_device(query_rows, key_rows, value_rows, short_taps, long_filter, cotangent):
    length, width = query_rows.shape
    groups = long_filter.shape[1]
    blocks = lax.axis_size("seq")
    chans = lax.axis_size("chan")
    chips, half = blocks // 2, width // 2
    margin = short_taps.shape[1] - 1
    tile_width = min(half, 256)
    tiles = half // tile_width
    bits = []
    while 2 << len(bits) < blocks:
        bits.append(2 << len(bits))
    bits.reverse()
    forward, inverse = dft_tables(length)
    shape = jax.ShapeDtypeStruct

    def swap(block, bit):
        return lax.ppermute(block, "seq", [(i, i ^ bit) for i in range(blocks)])

    def call(kernel, outs, args, scratch, in_specs=None, out_specs=None, aliases={}, cost=1):
        return list(
            pl.pallas_call(
                kernel,
                out_shape=outs,
                in_specs=in_specs or [VMEM] * len(args),
                out_specs=out_specs or [VMEM] * len(outs),
                scratch_shapes=scratch,
                input_output_aliases=aliases,
                compiler_params=pltpu.CompilerParams(vmem_limit_bytes=40 * 1024 * 1024),
                cost_estimate=pl.CostEstimate(flops=1, bytes_accessed=cost, transcendentals=0),
            )(*args)
        )

    def after(value, *others):
        return lax.optimization_barrier((value, *others))[0]

    rows, marks, short_taps, long_filter, forward, inverse = call(
        fetch_kernel,
        [
            shape((4, length, width), BF16),
            shape((HEAD, width), BF16),
            shape(short_taps.shape, F32),
            shape(long_filter.shape, F32),
            shape(forward.shape, BF16),
            shape(inverse.shape, BF16),
        ],
        [
            pltpu.with_memory_space_constraint(array, pltpu.HBM)
            for array in (
                query_rows,
                key_rows,
                value_rows,
                cotangent,
                short_taps,
                long_filter,
                forward,
                inverse,
            )
        ],
        [pltpu.VMEM((HEAD, width), F32), pltpu.SemaphoreType.DMA((8,))],
        [HBM] * 8,
    )
    all_marks = []
    for bit in bits + [1]:
        all_marks.append(swap(jnp.concatenate([marks] + all_marks, axis=0), bit))
    firsts_true, conv_first, after_rows = call(
        functools.partial(first_kernel, len(all_marks)),
        [
            shape((blocks, 2, EDGE, width), F32),
            shape((3, EDGE, width), F32),
            shape((3, EDGE, width), F32),
        ],
        [short_taps, marks, *all_marks],
        [
            pltpu.VMEM((blocks + 2, HEAD, width), F32),
            pltpu.VMEM((blocks + 1, 3, EDGE, width), F32),
            pltpu.VMEM((2 * EDGE, width), F32),
        ],
    )
    filter_rows = length * groups // width
    pair_shape = shape((4 * length + 2 * filter_rows, width), BF16)
    first_shape = shape((2 * length, half), BF16)
    later_shape = shape((2 * length + 4 * filter_rows, half), BF16)
    pair, conv, *own_units = call(
        functools.partial(own_kernel, bits, tile_width),
        [pair_shape, shape((3, length, width), F32)] + [first_shape, later_shape] * len(bits),
        [rows, short_taps, long_filter],
        [pltpu.VMEM((3, EDGE + length, tile_width), F32)],
        cost=40 * length * width,
    )

    def gather(own):
        units = {}
        for bit, block in zip(bits, own):
            arrived = {bit // 2: swap(block, bit)}
            for index, unit in units.items():
                arrived[index ^ bit // 2] = swap(unit, bit)
            units.update(arrived)
        return [units[index] for index in range(1, chips)]

    firsts = gather([after(unit, all_marks[0]) for unit in own_units[0::2]])
    sibling = swap(pair, 1)
    spec, near = call(
        functools.partial(chip_kernel, tile_width, groups, margin),
        [shape((4, 2 * length, width), F32), shape((2, 2 * length, groups), F32)],
        [pair, sibling, firsts_true, forward],
        [],
    )
    odd, even = call(
        functools.partial(filter_grad_kernel, blocks, tile_width, margin),
        [shape((blocks // 2, length, groups), F32)] * 2,
        [spec, near, firsts_true, forward, inverse, *firsts],
        [pltpu.VMEM((blocks + 1, 2 * length, groups), F32)],
    )
    laters = gather([after(unit, near) for unit in own_units[1::2]])
    even = even + swap(odd, 1)
    step = 1
    if chans > 1:
        even = even + lax.ppermute(even, "chan", [(i, i ^ 1) for i in range(chans)])
        step = 2
    even = after(even, *laters)
    units = []
    for first, later in zip(firsts, laters):
        units += [first, later, swap(after(first, even), 1), swap(after(later, even), 1)]
    for bit in reversed(bits):
        arrived = swap(even[1::2], bit)
        even = even[0::2] + arrived
    grad_filter = even[0]

    rows_out = shape((length, width), BF16)
    windows = [
        shape((blocks, 2 * length, groups), F32),
        shape((blocks + 3, length, groups), F32),
    ]

    def results(stage, extra, outs, out_specs):
        args = [rows, short_taps, long_filter, conv, conv_first, firsts_true, after_rows]
        args += [sibling, spec, forward, inverse, *units]
        count = len(args)
        return call(
            functools.partial(result_kernel, blocks, tile_width, stage),
            outs,
            args + extra,
            [
                pltpu.VMEM((2, 2 * length, tile_width), F32),
                pltpu.VMEM((2 * EDGE, tile_width), F32),
                pltpu.VMEM((3, length + EDGE, tile_width), F32),
                pltpu.VMEM((4, length, half), BF16),
                pltpu.SemaphoreType.DMA((4 * tiles,)),
            ],
            [VMEM] * count + ([VMEM] * 2 + [HBM] * 4 if extra else []),
            out_specs,
            {count + 2 + index: index for index in range(4)} if extra else {},
            80 * length * width,
        )

    *partial, spectra, filter_blocks = results(
        0, [], [rows_out] * 4 + windows, [HBM] * 4 + [VMEM] * 2
    )
    final = results(1, [spectra, filter_blocks, *partial], [rows_out] * 4, [HBM] * 4)

    while step < chans:
        arrived = lax.ppermute(grad_filter, "chan", [(i, i ^ step) for i in range(chans)])
        if 2 * step < chans <= 4 * step:
            grad_filter = after(grad_filter, spectra)
        grad_filter = grad_filter + arrived
        step *= 2
    return (*final, grad_filter)


def solution(mesh):
    in_specs = (
        P("seq", "chan"),
        P("seq", "chan"),
        P("seq", "chan"),
        P(None, None, "chan"),
        P("seq", None),
        P("seq", "chan"),
    )
    out_specs = (
        P("seq", "chan"),
        P("seq", "chan"),
        P("seq", "chan"),
        P("seq", "chan"),
        P("seq", None),
    )
    return jax.shard_map(
        per_device, mesh=mesh, in_specs=in_specs, out_specs=out_specs, check_vma=False
    )
```

```python
import functools

import jax
import jax.numpy as jnp
import ml_dtypes
import numpy as np
from jax import lax
from jax.experimental import pallas as pl
from jax.experimental.pallas import tpu as pltpu
from jax.sharding import PartitionSpec as P

F32 = jnp.float32
BF16 = jnp.bfloat16
EDGE = 8
HEAD = 16
VMEM = pl.BlockSpec(memory_space=pltpu.VMEM)
HBM = pl.BlockSpec(memory_space=pltpu.HBM)


def split_table(table):
    high = table.astype(ml_dtypes.bfloat16)
    low = (table - high.astype(np.float64)).astype(ml_dtypes.bfloat16)
    return high, low


def dft_tables(length):
    frequency = np.pi * (2 * np.arange(length) + 1) / (2 * length)
    into = frequency[:, None] * np.arange(length)[None, :]
    high, low = split_table(np.concatenate([np.cos(into), -np.sin(into)], axis=0))
    forward = np.concatenate([high, high, low], axis=1)
    forward = np.pad(forward, ((0, EDGE), (0, 0)))
    back = np.arange(length + EDGE)[:, None] * frequency[None, :]
    high, low = split_table(np.concatenate([np.cos(back), -np.sin(back)], axis=1) / length)
    inverse = np.concatenate([high, high, low], axis=1)
    return jnp.asarray(forward), jnp.asarray(inverse)


def halves(values):
    high = values.astype(BF16)
    return high, (values - high.astype(F32)).astype(BF16)


def table_dot(table, values):
    high, low = halves(values)
    return jnp.dot(
        table, jnp.concatenate([high, low, high], axis=0), preferred_element_type=F32
    )


def tap_sum(rows_ref, first, count, weights):
    total = weights[0:1] * rows_ref[first : first + count]
    for shift in range(1, weights.shape[0]):
        total = total + weights[shift : shift + 1] * rows_ref[first - shift : first - shift + count]
    return total


def put_filter(unit, first, filter_high, filter_low):
    length, groups = filter_high.shape
    width = unit.shape[1]
    rows = length * groups // width
    for tile in range(width // groups):
        lanes = slice(tile * groups, (tile + 1) * groups)
        part = slice(tile * rows, (tile + 1) * rows)
        unit[first : first + rows, lanes] = filter_high[part]
        unit[first + rows : first + 2 * rows, lanes] = filter_low[part]


def get_filter(unit, first, length, groups):
    width = unit.shape[1]
    rows = length * groups // width
    pieces = []
    for tile in range(width // groups):
        lanes = slice(tile * groups, (tile + 1) * groups)
        pieces.append(
            unit[first : first + rows, lanes].astype(F32)
            + unit[first + rows : first + 2 * rows, lanes].astype(F32)
        )
    return jnp.concatenate(pieces, axis=0)


def fetch_kernel(q_hbm, k_hbm, v_hbm, c_hbm, *refs):
    others = refs[:4]
    rows_ref, marks_ref, *other_refs = refs[4:10]
    edge, sems = refs[10:]
    length = q_hbm.shape[0]
    copies = [
        pltpu.make_async_copy(source, rows_ref.at[index], sems.at[index])
        for index, source in enumerate((q_hbm, k_hbm, v_hbm, c_hbm))
    ]
    copies += [
        pltpu.make_async_copy(source, target, sems.at[4 + index])
        for index, (source, target) in enumerate(zip(others, other_refs))
    ]
    for copy in copies:
        copy.start()
    for copy in copies[:4]:
        copy.wait()
    margin = others[0].shape[1] - 1
    edge[...] = jnp.zeros(edge.shape, F32)
    for p in range(4):
        first = rows_ref[p, 0:HEAD].astype(F32)
        edge[(3 + p) * margin : (4 + p) * margin] = first[0:margin]
        if p < 3:
            last = rows_ref[p, length - HEAD :].astype(F32)
            edge[p * margin : (p + 1) * margin] = last[HEAD - margin :]
    marks_ref[...] = edge[...].astype(BF16)
    for copy in copies[4:]:
        copy.wait()


def own_kernel(bits, tile_width, rows_ref, taps_ref, filter_ref, pair_ref, conv_ref, *refs):
    unit_refs, window = refs[:-1], refs[-1]
    length, width = rows_ref.shape[1:]
    half = width // 2
    me = lax.axis_index("seq")
    filter_high, filter_low = halves(filter_ref[...])
    put_filter(pair_ref, 4 * length, filter_high, filter_low)
    for later in unit_refs[1::2]:
        put_filter(later, 2 * length, filter_high, filter_low)
    window[:, 0:EDGE] = jnp.zeros((3, EDGE, tile_width), F32)
    for tile in range(width // tile_width):
        lanes = slice(tile * tile_width, (tile + 1) * tile_width)
        convs = []
        for p in range(3):
            window[p, EDGE:] = rows_ref[p, :, lanes].astype(F32)
            conv = tap_sum(window.at[p], EDGE, length, taps_ref[p, :, lanes])
            conv_ref[p, :, lanes] = conv
            convs.append(conv)
        incoming = rows_ref[3, :, lanes].astype(F32)
        parts = [*halves(convs[1] * convs[2]), *halves(incoming * convs[0])]
        for index, part in enumerate(parts):
            pair_ref[index * length : (index + 1) * length, lanes] = part
        in_half = tile * tile_width // half
        lanes_half = slice(tile * tile_width % half, tile * tile_width % half + tile_width)
        for index, bit in enumerate(bits):
            low_side = (me // bit) % 2 == 0
            first, later = unit_refs[2 * index : 2 * index + 2]
            target_low, target_high = (first, later) if in_half == 0 else (later, first)

            @pl.when(low_side)
            def _():
                target_low[0:length, lanes_half] = parts[0]
                target_low[length : 2 * length, lanes_half] = parts[1]

            @pl.when(jnp.logical_not(low_side))
            def _():
                target_high[0:length, lanes_half] = parts[2]
                target_high[length : 2 * length, lanes_half] = parts[3]


def first_kernel(marks_refs, taps_ref, own_marks, *refs):
    arrived = refs[:marks_refs]
    firsts_ref, conv_ref, after_ref, marks, convs, window = refs[marks_refs:]
    blocks = firsts_ref.shape[0]
    me = lax.axis_index("seq")
    margin = taps_ref.shape[1] - 1
    nothing = jnp.zeros(marks.shape[1:], F32)
    marks[0] = nothing
    marks[blocks + 1] = nothing
    marks[me + 1] = own_marks[...].astype(F32)
    index = 1
    for ref in arrived:
        for place in range(ref.shape[0] // HEAD):
            marks[(me ^ index_of(index, blocks)) + 1] = ref[
                place * HEAD : (place + 1) * HEAD
            ].astype(F32)
            index += 1
    window[...] = jnp.zeros(window.shape, F32)
    convs[blocks] = jnp.zeros(convs.shape[1:], F32)
    for block in range(blocks):
        for p in range(3):
            window[EDGE - margin : EDGE] = marks[block, p * margin : (p + 1) * margin]
            window[EDGE : EDGE + margin] = marks[block + 1, (3 + p) * margin : (4 + p) * margin]
            convs[block, p] = tap_sum(window, EDGE, EDGE, taps_ref[p])
        window[EDGE : EDGE + margin] = marks[block + 1, 6 * margin : 7 * margin]
        firsts_ref[block, 0] = convs[block, 1] * convs[block, 2]
        firsts_ref[block, 1] = window[EDGE:] * convs[block, 0]
    conv_ref[...] = convs[me]
    after_ref[0:2] = convs[me + 1, 1:3]
    window[EDGE : EDGE + margin] = marks[me + 2, 6 * margin : 7 * margin]
    after_ref[2] = window[EDGE:]


def index_of(count, blocks):
    order, bit = [0], blocks // 2
    while bit:
        order += [index ^ bit for index in order]
        bit //= 2
    return order[count]


def with_first(margin, first, rows):
    true = jnp.concatenate([first, jnp.zeros((HEAD - EDGE, first.shape[1]), F32)], axis=0)
    row = lax.broadcasted_iota(jnp.int32, true.shape, 0)
    return jnp.where(row < margin, true, rows)


def spectrum(forward, margin, first, ref, place, lanes):
    length = forward.shape[1] // 3
    parts = []
    for index, part in enumerate(halves(first)):
        begin = place + index * length
        head = with_first(margin, part.astype(F32), ref[begin : begin + HEAD, lanes].astype(F32))
        parts += [head.astype(BF16), ref[begin + HEAD : begin + length, lanes]]
    return jnp.dot(
        forward, jnp.concatenate([*parts, *parts[0:2]], axis=0), preferred_element_type=F32
    )


def cross_add(cross, distance, early, late, groups):
    length = early.shape[0] // 2
    e_re, e_im = early[0:length], early[length:]
    l_re, l_im = late[0:length], late[length:]
    re = e_re * l_re + e_im * l_im
    im = e_re * l_im - e_im * l_re
    parts = range(early.shape[1] // groups)
    cross[distance, 0:length] += sum(re[:, p * groups : (p + 1) * groups] for p in parts)
    cross[distance, length:] += sum(im[:, p * groups : (p + 1) * groups] for p in parts)


def chip_kernel(
    tile_width,
    groups,
    margin,
    own_ref,
    other_ref,
    firsts_ref,
    forward_ref,
    spec_ref,
    cross_ref,
):
    length = forward_ref.shape[1] // 3
    width = own_ref.shape[1]
    me = lax.axis_index("seq")
    core = me % 2
    forward = forward_ref[0 : 2 * length]
    cross_ref[...] = jnp.zeros(cross_ref.shape, F32)

    def one_tile(step, carry):
        lanes = pl.ds(pl.multiple_of(step * tile_width, tile_width), tile_width)
        for ref, slot, block in ((own_ref, core, me), (other_ref, 1 - core, me ^ 1)):
            for kind in range(2):
                first = firsts_ref[block, kind, :, lanes]
                spec_ref[2 * kind + slot, :, lanes] = spectrum(
                    forward, margin, first, ref, 2 * kind * length, lanes
                )
        cross_add(cross_ref, 0, spec_ref[core, :, lanes], spec_ref[2 + core, :, lanes], groups)

        @pl.when(2 * step * tile_width // width == core)
        def _():
            cross_add(cross_ref, 1, spec_ref[0, :, lanes], spec_ref[3, :, lanes], groups)

        return carry

    lax.fori_loop(0, width // tile_width, one_tile, 0)


def filter_grad_kernel(
    blocks,
    tile_width,
    margin,
    spec_ref,
    near_ref,
    firsts_ref,
    forward_ref,
    inverse_ref,
    *refs,
):
    chips = blocks // 2
    units = refs[: chips - 1]
    gf_refs, cross = refs[chips - 1 : -1], refs[-1]
    length = forward_ref.shape[1] // 3
    groups = near_ref.shape[2]
    half = spec_ref.shape[2] // 2
    me = lax.axis_index("seq")
    core, chip = me % 2, me // 2
    forward = forward_ref[0 : 2 * length]
    cross[0:2] = near_ref[...]
    cross[2:] = jnp.zeros((blocks - 1, 2 * length, groups), F32)
    for index, unit in enumerate(units):
        other = chip ^ (index + 1)

        def one_tile(step, carry):
            start = pl.multiple_of(step * tile_width, tile_width)
            lanes = pl.ds(start, tile_width)
            kind = jnp.where(other < chip, 0, 1)
            wide_lanes = pl.ds(pl.multiple_of(kind * half + start, tile_width), tile_width)
            first = firsts_ref[2 * other + core, kind, :, wide_lanes]
            spec = spectrum(forward, margin, first, unit, 0, lanes)

            @pl.when(other < chip)
            def _():
                for slot in range(2):
                    distance = 2 * chip + slot - (2 * other + core)
                    cross_add(cross, distance, spec, spec_ref[2 + slot, :, wide_lanes], groups)

            @pl.when(other > chip)
            def _():
                for slot in range(2):
                    distance = 2 * other + core - (2 * chip + slot)
                    cross_add(cross, distance, spec_ref[slot, :, wide_lanes], spec, groups)

            return carry

        lax.fori_loop(0, half // tile_width, one_tile, 0)

    inverse = inverse_ref[0:length]
    sign = signs(length, groups)
    for parity, ref in zip((1, 0), gf_refs):
        for place in range(blocks // 2):
            block = me ^ (2 * place + parity)
            re = cross[block, 0:length] + sign * cross[block + 1, length:]
            im = cross[block, length:] - sign * cross[block + 1, 0:length]
            ref[place] = table_dot(inverse, jnp.concatenate([re, im], axis=0))


def signs(length, groups):
    row = lax.broadcasted_iota(jnp.int32, (length, groups), 0)
    return jnp.where(row % 2 == 0, 1.0, -1.0)


def result_kernel(blocks, tile_width, tiles, *refs):
    others = blocks // 2 - 1
    (
        rows_ref,
        taps_ref,
        filter_ref,
        conv_ref,
        conv_first,
        firsts_ref,
        after_ref,
        other_ref,
        spec_ref,
        forward_ref,
        inverse_ref,
    ) = refs[:11]
    refs = refs[11:]
    units = [refs[4 * index : 4 * index + 4] for index in range(others)]
    refs = refs[4 * others :]
    if tiles[0] == 0:
        outs, (spectra, filter_rows) = refs[:4], refs[4:6]
        refs = refs[6:]
    else:
        spectra, filter_rows = refs[:2]
        outs = refs[6:10]
        refs = refs[10:]
    acc, fix, grads, rows_out, sems = refs
    length, width = rows_ref.shape[1:]
    groups = filter_ref.shape[1]
    half = width // 2
    margin = taps_ref.shape[1] - 1
    me = lax.axis_index("seq")
    core, chip = me % 2, me // 2
    forward, inverse = forward_ref[0 : 2 * length], inverse_ref[...]

    if tiles[0] == 0:
        sign = signs(length, groups)
        for edge in (0, 1, blocks + 2):
            filter_rows[edge] = jnp.zeros((length, groups), F32)
        filter_rows[me + 2] = filter_ref[...]
        filter_rows[(me ^ 1) + 2] = get_filter(other_ref, 4 * length, length, groups)
        for index, unit in enumerate(units):
            block = me ^ (2 * (index + 1))
            filter_rows[block + 2] = get_filter(unit[1], 2 * length, length, groups)
            filter_rows[(block ^ 1) + 2] = get_filter(unit[3], 2 * length, length, groups)
        previous = None
        for distance in range(blocks):
            own = table_dot(forward, filter_rows[distance + 2])
            if previous is None:
                spectra[distance] = own
            else:
                spectra[distance, 0:length] = own[0:length] - sign * previous[length:]
                spectra[distance, length:] = own[length:] + sign * previous[0:length]
            previous = own

    def wide(values):
        return jnp.concatenate([values] * (tile_width // groups), axis=1)

    def filter_row(block, row):
        return wide(filter_rows[block + 2, pl.ds(row, 1)])

    def add_lower(distance, signal, spec, fresh=False):
        re, im = spec[0:length], spec[length:]
        h_re, h_im = wide(spectra[distance, 0:length]), wide(spectra[distance, length:])
        new_re = h_re * re - h_im * im
        new_im = h_re * im + h_im * re
        acc[0, 0:length] = new_re if fresh else acc[0, 0:length] + new_re
        acc[0, length:] = new_im if fresh else acc[0, length:] + new_im
        near = filter_row(distance + 1, 0) + filter_row(distance - 1, 0)
        far = filter_row(distance + 1, 1) + filter_row(distance - 1, 1)
        fix[0:1] += signal[0:1] * near
        fix[1:2] += signal[0:1] * far + signal[1:2] * near

    def add_upper(distance, signal, spec, fresh=False):
        re, im = spec[0:length], spec[length:]
        h_re, h_im = wide(spectra[distance, 0:length]), wide(spectra[distance, length:])
        new_re = h_re * re + h_im * im
        new_im = h_re * im - h_im * re
        acc[1, 0:length] = new_re if fresh else acc[1, 0:length] + new_re
        acc[1, length:] = new_im if fresh else acc[1, length:] + new_im
        fix[EDGE + 1 : EDGE + 2] += signal[0:1] * (
            filter_row(distance - 2, length - 1) + filter_row(distance, length - 1)
        )

    copies = []
    for count, tile in enumerate(tiles):
        start = tile * tile_width
        in_half = start // half
        lanes = slice(start, start + tile_width)
        lanes_half = slice(start % half, start % half + tile_width)
        lanes_out = slice(count * tile_width, (count + 1) * tile_width)
        weights = [taps_ref[p, :, lanes] for p in range(3)]
        fix[...] = jnp.zeros(fix.shape, F32)

        add_lower(0, firsts_ref[me, 0, :, lanes], spec_ref[core, :, lanes], True)
        add_upper(0, firsts_ref[me, 1, :, lanes], spec_ref[2 + core, :, lanes], True)

        @pl.when(core == 1)
        def _():
            add_lower(1, firsts_ref[me - 1, 0, :, lanes], spec_ref[0, :, lanes])

        @pl.when(core == 0)
        def _():
            add_upper(1, firsts_ref[me + 1, 1, :, lanes], spec_ref[3, :, lanes])

        for index, unit in enumerate(units):
            other = chip ^ (index + 1)
            for side in range(2):
                first, later = unit[2 * side : 2 * side + 2]
                body_low, body_high = (first, later) if in_half == 0 else (later, first)
                block = 2 * other + (core if side == 0 else 1 - core)

                @pl.when(other < chip)
                def _():
                    signal = firsts_ref[block, 0, :, lanes]
                    spec = spectrum(forward, margin, signal, body_low, 0, lanes_half)
                    add_lower(me - block, signal, spec)

                @pl.when(other > chip)
                def _():
                    signal = firsts_ref[block, 1, :, lanes]
                    spec = spectrum(forward, margin, signal, body_high, 0, lanes_half)
                    add_upper(block - me, signal, spec)

        after_key, after_value, after_incoming = [
            after_ref[p, :, lanes][0:margin] for p in range(3)
        ]
        gated = after_key * after_value
        zero_lag, one_lag = filter_row(0, 0), filter_row(0, 1)
        fix[0:1] += gated[0:1] * zero_lag
        fix[1:2] += gated[1:2] * zero_lag + gated[0:1] * one_lag

        long_conv = table_dot(inverse, acc[0])
        gated_grad = table_dot(inverse, acc[1])
        query_conv, key_conv, value_conv = [
            jnp.concatenate(
                [
                    with_first(margin, conv_first[p, :, lanes], conv_ref[p, 0:HEAD, lanes]),
                    conv_ref[p, HEAD:, lanes],
                ],
                axis=0,
            )
            for p in range(3)
        ]
        incoming = rows_ref[3, :, lanes].astype(F32)
        beyond = slice(length, length + margin)
        grad_edge = gated_grad[beyond] + fix[EDGE : EDGE + margin]
        grads[0, 0:length] = incoming * long_conv[0:length]
        grads[0, beyond] = after_incoming * (long_conv[beyond] + fix[0:margin])
        grads[1, 0:length] = gated_grad[0:length] * value_conv
        grads[1, beyond] = grad_edge * after_value
        grads[2, 0:length] = gated_grad[0:length] * key_conv
        grads[2, beyond] = grad_edge * after_key
        rows_out[0, :, lanes_out] = (query_conv * long_conv[0:length]).astype(BF16)
        for p in range(3):
            total = weights[p][0:1] * grads[p, 0:length]
            for shift in range(1, margin + 1):
                total = total + weights[p][shift : shift + 1] * grads[p, shift : shift + length]
            rows_out[1 + p, :, lanes_out] = total.astype(BF16)
        for p, out in enumerate(outs):
            copy = pltpu.make_async_copy(
                rows_out.at[p, :, lanes_out], out.at[:, lanes], sems.at[4 * count + p]
            )
            copy.start()
            copies.append(copy)
    for copy in copies:
        copy.wait()


def per_device(query_rows, key_rows, value_rows, short_taps, long_filter, cotangent):
    length, width = query_rows.shape
    groups = long_filter.shape[1]
    blocks = lax.axis_size("seq")
    chans = lax.axis_size("chan")
    chips, half = blocks // 2, width // 2
    margin = short_taps.shape[1] - 1
    tile_width = min(half, 256)
    bits = []
    while 2 << len(bits) < blocks:
        bits.append(2 << len(bits))
    bits.reverse()
    forward, inverse = dft_tables(length)
    shape = jax.ShapeDtypeStruct

    def swap(block, bit):
        return lax.ppermute(block, "seq", [(i, i ^ bit) for i in range(blocks)])

    def call(kernel, outs, args, scratch, in_specs=None, out_specs=None, aliases={}, cost=1):
        return list(
            pl.pallas_call(
                kernel,
                out_shape=outs,
                in_specs=in_specs or [VMEM] * len(args),
                out_specs=out_specs or [VMEM] * len(outs),
                scratch_shapes=scratch,
                input_output_aliases=aliases,
                compiler_params=pltpu.CompilerParams(vmem_limit_bytes=40 * 1024 * 1024),
                cost_estimate=pl.CostEstimate(flops=1, bytes_accessed=cost, transcendentals=0),
            )(*args)
        )

    def after(value, *others):
        return lax.optimization_barrier((value, *others))[0]

    rows, marks, short_taps, long_filter, forward, inverse = call(
        fetch_kernel,
        [
            shape((4, length, width), BF16),
            shape((HEAD, width), BF16),
            shape(short_taps.shape, F32),
            shape(long_filter.shape, F32),
            shape(forward.shape, BF16),
            shape(inverse.shape, BF16),
        ],
        [
            pltpu.with_memory_space_constraint(array, pltpu.HBM)
            for array in (
                query_rows,
                key_rows,
                value_rows,
                cotangent,
                short_taps,
                long_filter,
                forward,
                inverse,
            )
        ],
        [pltpu.VMEM((HEAD, width), F32), pltpu.SemaphoreType.DMA((8,))],
        [HBM] * 8,
    )
    all_marks = []
    for bit in bits + [1]:
        all_marks.append(swap(jnp.concatenate([marks] + all_marks, axis=0), bit))
    firsts_true, conv_first, after_rows = call(
        functools.partial(first_kernel, len(all_marks)),
        [
            shape((blocks, 2, EDGE, width), F32),
            shape((3, EDGE, width), F32),
            shape((3, EDGE, width), F32),
        ],
        [short_taps, marks, *all_marks],
        [
            pltpu.VMEM((blocks + 2, HEAD, width), F32),
            pltpu.VMEM((blocks + 1, 3, EDGE, width), F32),
            pltpu.VMEM((2 * EDGE, width), F32),
        ],
    )
    filter_rows = length * groups // width
    pair_shape = shape((4 * length + 2 * filter_rows, width), BF16)
    first_shape = shape((2 * length, half), BF16)
    later_shape = shape((2 * length + 4 * filter_rows, half), BF16)
    pair, conv, *own_units = call(
        functools.partial(own_kernel, bits, tile_width),
        [pair_shape, shape((3, length, width), F32)] + [first_shape, later_shape] * len(bits),
        [rows, short_taps, long_filter],
        [pltpu.VMEM((3, EDGE + length, tile_width), F32)],
        cost=40 * length * width,
    )

    def gather(own):
        units = {}
        for bit, block in zip(bits, own):
            arrived = {bit // 2: swap(block, bit)}
            for index, unit in units.items():
                arrived[index ^ bit // 2] = swap(unit, bit)
            units.update(arrived)
        return [units[index] for index in range(1, chips)]

    firsts = gather([after(unit, all_marks[0]) for unit in own_units[0::2]])
    sibling = swap(after(pair, all_marks[0]), 1)
    spec, near = call(
        functools.partial(chip_kernel, tile_width, groups, margin),
        [shape((4, 2 * length, width), F32), shape((2, 2 * length, groups), F32)],
        [pair, sibling, firsts_true, forward],
        [],
    )
    odd, even = call(
        functools.partial(filter_grad_kernel, blocks, tile_width, margin),
        [shape((blocks // 2, length, groups), F32)] * 2,
        [spec, near, firsts_true, forward, inverse, *firsts],
        [pltpu.VMEM((blocks + 1, 2 * length, groups), F32)],
    )
    laters = gather([after(unit, near) for unit in own_units[1::2]])
    even = even + swap(odd, 1)
    step = 1
    if chans > 1:
        even = even + lax.ppermute(even, "chan", [(i, i ^ 1) for i in range(chans)])
        step = 2
    even = after(even, *laters)
    units = []
    for first, later in zip(firsts, laters):
        units += [first, later, swap(after(first, even), 1), swap(after(later, even), 1)]
    rows_out = shape((length, width), BF16)
    windows = [
        shape((blocks, 2 * length, groups), F32),
        shape((blocks + 3, length, groups), F32),
    ]

    def results(tiles, extra, outs, out_specs):
        args = [rows, short_taps, long_filter, conv, conv_first, firsts_true, after_rows]
        args += [sibling, spec, forward, inverse, *units]
        count = len(args)
        return call(
            functools.partial(result_kernel, blocks, tile_width, tiles),
            outs,
            args + extra,
            [
                pltpu.VMEM((2, 2 * length, tile_width), F32),
                pltpu.VMEM((2 * EDGE, tile_width), F32),
                pltpu.VMEM((3, length + EDGE, tile_width), F32),
                pltpu.VMEM((4, length, len(tiles) * tile_width), BF16),
                pltpu.SemaphoreType.DMA((4 * len(tiles),)),
            ],
            [VMEM] * count + ([VMEM] * 2 + [HBM] * 4 if extra else []),
            out_specs,
            {count + 2 + index: index for index in range(4)} if extra else {},
            80 * length * len(tiles) * tile_width,
        )

    tiles = width // tile_width
    cuts = [0, max(1, tiles // 4), tiles - tiles // 4, tiles]
    *final, spectra, filter_blocks = results(
        range(cuts[0], cuts[1]), [], [rows_out] * 4 + windows, [HBM] * 4 + [VMEM] * 2
    )
    ready = [final]
    for begin, end in zip(cuts[1:], cuts[2:]):
        if begin < end:
            final = results(
                range(begin, end), [spectra, filter_blocks, *final], [rows_out] * 4, [HBM] * 4
            )
        ready.append(final)

    for bit in reversed(bits):
        arrived = swap(even[1::2], bit)
        even = even[0::2]
        if bit == bits[0]:
            even = after(even, spectra)
        even = even + arrived
    grad_filter = even[0]
    while step < chans:
        arrived = lax.ppermute(grad_filter, "chan", [(i, i ^ step) for i in range(chans)])
        if 2 * step < chans <= 4 * step:
            grad_filter = after(grad_filter, ready[1][0])
        grad_filter = grad_filter + arrived
        step *= 2
    return (*final, grad_filter)


def solution(mesh):
    in_specs = (
        P("seq", "chan"),
        P("seq", "chan"),
        P("seq", "chan"),
        P(None, None, "chan"),
        P("seq", None),
        P("seq", "chan"),
    )
    out_specs = (
        P("seq", "chan"),
        P("seq", "chan"),
        P("seq", "chan"),
        P("seq", "chan"),
        P("seq", None),
    )
    return jax.shard_map(
        per_device, mesh=mesh, in_specs=in_specs, out_specs=out_specs, check_vma=False
    )
```

```python
import functools

import jax
import jax.numpy as jnp
import ml_dtypes
import numpy as np
from jax import lax
from jax.experimental import pallas as pl
from jax.experimental.pallas import tpu as pltpu
from jax.sharding import PartitionSpec as P

F32 = jnp.float32
BF16 = jnp.bfloat16
EDGE = 8
HEAD = 16
VMEM = pl.BlockSpec(memory_space=pltpu.VMEM)
HBM = pl.BlockSpec(memory_space=pltpu.HBM)


def split_table(table):
    high = table.astype(ml_dtypes.bfloat16)
    low = (table - high.astype(np.float64)).astype(ml_dtypes.bfloat16)
    return high, low


def dft_tables(length):
    frequency = np.pi * (2 * np.arange(length) + 1) / (2 * length)
    into = frequency[:, None] * np.arange(length)[None, :]
    high, low = split_table(np.concatenate([np.cos(into), -np.sin(into)], axis=0))
    forward = np.concatenate([high, high, low], axis=1)
    forward = np.pad(forward, ((0, EDGE), (0, 0)))
    back = np.arange(length + EDGE)[:, None] * frequency[None, :]
    high, low = split_table(np.concatenate([np.cos(back), -np.sin(back)], axis=1) / length)
    inverse = np.concatenate([high, high, low], axis=1)
    return jnp.asarray(forward), jnp.asarray(inverse)


def halves(values):
    high = values.astype(BF16)
    return high, (values - high.astype(F32)).astype(BF16)


def table_dot(table, values):
    high, low = halves(values)
    return jnp.dot(
        table, jnp.concatenate([high, low, high], axis=0), preferred_element_type=F32
    )


def tap_sum(rows_ref, first, count, weights):
    total = weights[0:1] * rows_ref[first : first + count]
    for shift in range(1, weights.shape[0]):
        total = total + weights[shift : shift + 1] * rows_ref[first - shift : first - shift + count]
    return total


def put_filter(unit, first, filter_high, filter_low):
    length, groups = filter_high.shape
    width = unit.shape[1]
    rows = length * groups // width
    for tile in range(width // groups):
        lanes = slice(tile * groups, (tile + 1) * groups)
        part = slice(tile * rows, (tile + 1) * rows)
        unit[first : first + rows, lanes] = filter_high[part]
        unit[first + rows : first + 2 * rows, lanes] = filter_low[part]


def get_filter(unit, first, length, groups):
    width = unit.shape[1]
    rows = length * groups // width
    pieces = []
    for tile in range(width // groups):
        lanes = slice(tile * groups, (tile + 1) * groups)
        pieces.append(
            unit[first : first + rows, lanes].astype(F32)
            + unit[first + rows : first + 2 * rows, lanes].astype(F32)
        )
    return jnp.concatenate(pieces, axis=0)


def fetch_kernel(q_hbm, k_hbm, v_hbm, c_hbm, *refs):
    others = refs[:4]
    rows_ref, marks_ref, *other_refs = refs[4:10]
    edge, sems = refs[10:]
    length = q_hbm.shape[0]
    copies = [
        pltpu.make_async_copy(source, rows_ref.at[index], sems.at[index])
        for index, source in enumerate((q_hbm, k_hbm, v_hbm, c_hbm))
    ]
    copies += [
        pltpu.make_async_copy(source, target, sems.at[4 + index])
        for index, (source, target) in enumerate(zip(others, other_refs))
    ]
    for copy in copies:
        copy.start()
    for copy in copies[:4]:
        copy.wait()
    margin = others[0].shape[1] - 1
    edge[...] = jnp.zeros(edge.shape, F32)
    for p in range(4):
        first = rows_ref[p, 0:HEAD].astype(F32)
        edge[(3 + p) * margin : (4 + p) * margin] = first[0:margin]
        if p < 3:
            last = rows_ref[p, length - HEAD :].astype(F32)
            edge[p * margin : (p + 1) * margin] = last[HEAD - margin :]
    marks_ref[...] = edge[...].astype(BF16)
    for copy in copies[4:]:
        copy.wait()


def own_kernel(bits, tile_width, rows_ref, taps_ref, filter_ref, pair_ref, conv_ref, *refs):
    unit_refs, window = refs[:-1], refs[-1]
    length, width = rows_ref.shape[1:]
    half = width // 2
    me = lax.axis_index("seq")
    filter_high, filter_low = halves(filter_ref[...])
    put_filter(pair_ref, 4 * length, filter_high, filter_low)
    for later in unit_refs[1::2]:
        put_filter(later, 2 * length, filter_high, filter_low)
    window[:, 0:EDGE] = jnp.zeros((3, EDGE, tile_width), F32)
    for tile in range(width // tile_width):
        lanes = slice(tile * tile_width, (tile + 1) * tile_width)
        convs = []
        for p in range(3):
            window[p, EDGE:] = rows_ref[p, :, lanes].astype(F32)
            conv = tap_sum(window.at[p], EDGE, length, taps_ref[p, :, lanes])
            conv_ref[p, :, lanes] = conv
            convs.append(conv)
        incoming = rows_ref[3, :, lanes].astype(F32)
        parts = [*halves(convs[1] * convs[2]), *halves(incoming * convs[0])]
        for index, part in enumerate(parts):
            pair_ref[index * length : (index + 1) * length, lanes] = part
        in_half = tile * tile_width // half
        lanes_half = slice(tile * tile_width % half, tile * tile_width % half + tile_width)
        for index, bit in enumerate(bits):
            low_side = (me // bit) % 2 == 0
            first, later = unit_refs[2 * index : 2 * index + 2]
            target_low, target_high = (first, later) if in_half == 0 else (later, first)

            @pl.when(low_side)
            def _():
                target_low[0:length, lanes_half] = parts[0]
                target_low[length : 2 * length, lanes_half] = parts[1]

            @pl.when(jnp.logical_not(low_side))
            def _():
                target_high[0:length, lanes_half] = parts[2]
                target_high[length : 2 * length, lanes_half] = parts[3]


def first_kernel(marks_refs, taps_ref, own_marks, *refs):
    arrived = refs[:marks_refs]
    firsts_ref, conv_ref, after_ref, marks, convs, window = refs[marks_refs:]
    blocks = firsts_ref.shape[0]
    me = lax.axis_index("seq")
    margin = taps_ref.shape[1] - 1
    nothing = jnp.zeros(marks.shape[1:], F32)
    marks[0] = nothing
    marks[blocks + 1] = nothing
    marks[me + 1] = own_marks[...].astype(F32)
    index = 1
    for ref in arrived:
        for place in range(ref.shape[0] // HEAD):
            marks[(me ^ index_of(index, blocks)) + 1] = ref[
                place * HEAD : (place + 1) * HEAD
            ].astype(F32)
            index += 1
    window[...] = jnp.zeros(window.shape, F32)
    convs[blocks] = jnp.zeros(convs.shape[1:], F32)
    for block in range(blocks):
        for p in range(3):
            window[EDGE - margin : EDGE] = marks[block, p * margin : (p + 1) * margin]
            window[EDGE : EDGE + margin] = marks[block + 1, (3 + p) * margin : (4 + p) * margin]
            convs[block, p] = tap_sum(window, EDGE, EDGE, taps_ref[p])
        window[EDGE : EDGE + margin] = marks[block + 1, 6 * margin : 7 * margin]
        firsts_ref[block, 0] = convs[block, 1] * convs[block, 2]
        firsts_ref[block, 1] = window[EDGE:] * convs[block, 0]
    conv_ref[...] = convs[me]
    after_ref[0:2] = convs[me + 1, 1:3]
    window[EDGE : EDGE + margin] = marks[me + 2, 6 * margin : 7 * margin]
    after_ref[2] = window[EDGE:]


def index_of(count, blocks):
    order, bit = [0], blocks // 2
    while bit:
        order += [index ^ bit for index in order]
        bit //= 2
    return order[count]


def with_first(margin, first, rows):
    true = jnp.concatenate([first, jnp.zeros((HEAD - EDGE, first.shape[1]), F32)], axis=0)
    row = lax.broadcasted_iota(jnp.int32, true.shape, 0)
    return jnp.where(row < margin, true, rows)


def spectrum(forward, margin, first, ref, place, lanes):
    length = forward.shape[1] // 3
    parts = []
    for index, part in enumerate(halves(first)):
        begin = place + index * length
        head = with_first(margin, part.astype(F32), ref[begin : begin + HEAD, lanes].astype(F32))
        parts += [head.astype(BF16), ref[begin + HEAD : begin + length, lanes]]
    return jnp.dot(
        forward, jnp.concatenate([*parts, *parts[0:2]], axis=0), preferred_element_type=F32
    )


def cross_add(cross, distance, early, late, groups):
    length = early.shape[0] // 2
    e_re, e_im = early[0:length], early[length:]
    l_re, l_im = late[0:length], late[length:]
    re = e_re * l_re + e_im * l_im
    im = e_re * l_im - e_im * l_re
    parts = range(early.shape[1] // groups)
    cross[distance, 0:length] += sum(re[:, p * groups : (p + 1) * groups] for p in parts)
    cross[distance, length:] += sum(im[:, p * groups : (p + 1) * groups] for p in parts)


def chip_kernel(
    tile_width,
    groups,
    margin,
    own_ref,
    other_ref,
    firsts_ref,
    forward_ref,
    spec_ref,
    cross_ref,
):
    length = forward_ref.shape[1] // 3
    width = own_ref.shape[1]
    me = lax.axis_index("seq")
    core = me % 2
    forward = forward_ref[0 : 2 * length]
    cross_ref[...] = jnp.zeros(cross_ref.shape, F32)

    def one_tile(step, carry):
        lanes = pl.ds(pl.multiple_of(step * tile_width, tile_width), tile_width)
        for ref, slot, block in ((own_ref, core, me), (other_ref, 1 - core, me ^ 1)):
            for kind in range(2):
                first = firsts_ref[block, kind, :, lanes]
                spec_ref[2 * kind + slot, :, lanes] = spectrum(
                    forward, margin, first, ref, 2 * kind * length, lanes
                )
        cross_add(cross_ref, 0, spec_ref[core, :, lanes], spec_ref[2 + core, :, lanes], groups)

        @pl.when(2 * step * tile_width // width == core)
        def _():
            cross_add(cross_ref, 1, spec_ref[0, :, lanes], spec_ref[3, :, lanes], groups)

        return carry

    lax.fori_loop(0, width // tile_width, one_tile, 0)


def filter_grad_kernel(
    blocks,
    tile_width,
    margin,
    spec_ref,
    near_ref,
    firsts_ref,
    forward_ref,
    inverse_ref,
    *refs,
):
    chips = blocks // 2
    units = refs[: chips - 1]
    gf_refs, cross = refs[chips - 1 : -1], refs[-1]
    length = forward_ref.shape[1] // 3
    groups = near_ref.shape[2]
    half = spec_ref.shape[2] // 2
    me = lax.axis_index("seq")
    core, chip = me % 2, me // 2
    forward = forward_ref[0 : 2 * length]
    cross[0:2] = near_ref[...]
    cross[2:] = jnp.zeros((blocks - 1, 2 * length, groups), F32)
    for index, unit in enumerate(units):
        other = chip ^ (index + 1)

        def one_tile(step, carry):
            start = pl.multiple_of(step * tile_width, tile_width)
            lanes = pl.ds(start, tile_width)
            kind = jnp.where(other < chip, 0, 1)
            wide_lanes = pl.ds(pl.multiple_of(kind * half + start, tile_width), tile_width)
            first = firsts_ref[2 * other + core, kind, :, wide_lanes]
            spec = spectrum(forward, margin, first, unit, 0, lanes)

            @pl.when(other < chip)
            def _():
                for slot in range(2):
                    distance = 2 * chip + slot - (2 * other + core)
                    cross_add(cross, distance, spec, spec_ref[2 + slot, :, wide_lanes], groups)

            @pl.when(other > chip)
            def _():
                for slot in range(2):
                    distance = 2 * other + core - (2 * chip + slot)
                    cross_add(cross, distance, spec_ref[slot, :, wide_lanes], spec, groups)

            return carry

        lax.fori_loop(0, half // tile_width, one_tile, 0)

    inverse = inverse_ref[0:length]
    sign = signs(length, groups)
    for place in range(blocks):
        block = (me | 1) ^ place
        re = cross[block, 0:length] + sign * cross[block + 1, length:]
        im = cross[block, length:] - sign * cross[block + 1, 0:length]
        gf_refs[place // chips][place % chips] = table_dot(inverse, jnp.concatenate([re, im], axis=0))


def signs(length, groups):
    row = lax.broadcasted_iota(jnp.int32, (length, groups), 0)
    return jnp.where(row % 2 == 0, 1.0, -1.0)


def result_kernel(blocks, tile_width, tiles, *refs):
    others = blocks // 2 - 1
    (
        rows_ref,
        taps_ref,
        filter_ref,
        conv_ref,
        conv_first,
        firsts_ref,
        after_ref,
        other_ref,
        spec_ref,
        forward_ref,
        inverse_ref,
    ) = refs[:11]
    refs = refs[11:]
    units = [refs[4 * index : 4 * index + 4] for index in range(others)]
    refs = refs[4 * others :]
    if tiles[0] == 0:
        outs, (spectra, filter_rows) = refs[:4], refs[4:6]
        refs = refs[6:]
    else:
        spectra, filter_rows = refs[:2]
        outs = refs[6:10]
        refs = refs[10:]
    acc, fix, grads, rows_out, sems = refs
    length, width = rows_ref.shape[1:]
    groups = filter_ref.shape[1]
    half = width // 2
    margin = taps_ref.shape[1] - 1
    me = lax.axis_index("seq")
    core, chip = me % 2, me // 2
    forward, inverse = forward_ref[0 : 2 * length], inverse_ref[...]

    if tiles[0] == 0:
        sign = signs(length, groups)
        for edge in (0, 1, blocks + 2):
            filter_rows[edge] = jnp.zeros((length, groups), F32)
        filter_rows[me + 2] = filter_ref[...]
        filter_rows[(me ^ 1) + 2] = get_filter(other_ref, 4 * length, length, groups)
        for index, unit in enumerate(units):
            block = me ^ (2 * (index + 1))
            filter_rows[block + 2] = get_filter(unit[1], 2 * length, length, groups)
            filter_rows[(block ^ 1) + 2] = get_filter(unit[3], 2 * length, length, groups)
        previous = None
        for distance in range(blocks):
            own = table_dot(forward, filter_rows[distance + 2])
            if previous is None:
                spectra[distance] = own
            else:
                spectra[distance, 0:length] = own[0:length] - sign * previous[length:]
                spectra[distance, length:] = own[length:] + sign * previous[0:length]
            previous = own

    def wide(values):
        return jnp.concatenate([values] * (tile_width // groups), axis=1)

    def filter_row(block, row):
        return wide(filter_rows[block + 2, pl.ds(row, 1)])

    def add_lower(distance, signal, spec, fresh=False):
        re, im = spec[0:length], spec[length:]
        h_re, h_im = wide(spectra[distance, 0:length]), wide(spectra[distance, length:])
        new_re = h_re * re - h_im * im
        new_im = h_re * im + h_im * re
        acc[0, 0:length] = new_re if fresh else acc[0, 0:length] + new_re
        acc[0, length:] = new_im if fresh else acc[0, length:] + new_im
        near = filter_row(distance + 1, 0) + filter_row(distance - 1, 0)
        far = filter_row(distance + 1, 1) + filter_row(distance - 1, 1)
        fix[0:1] += signal[0:1] * near
        fix[1:2] += signal[0:1] * far + signal[1:2] * near

    def add_upper(distance, signal, spec, fresh=False):
        re, im = spec[0:length], spec[length:]
        h_re, h_im = wide(spectra[distance, 0:length]), wide(spectra[distance, length:])
        new_re = h_re * re + h_im * im
        new_im = h_re * im - h_im * re
        acc[1, 0:length] = new_re if fresh else acc[1, 0:length] + new_re
        acc[1, length:] = new_im if fresh else acc[1, length:] + new_im
        fix[EDGE + 1 : EDGE + 2] += signal[0:1] * (
            filter_row(distance - 2, length - 1) + filter_row(distance, length - 1)
        )

    copies = []
    for count, tile in enumerate(tiles):
        start = tile * tile_width
        in_half = start // half
        lanes = slice(start, start + tile_width)
        lanes_half = slice(start % half, start % half + tile_width)
        lanes_out = slice(count * tile_width, (count + 1) * tile_width)
        weights = [taps_ref[p, :, lanes] for p in range(3)]
        fix[...] = jnp.zeros(fix.shape, F32)

        add_lower(0, firsts_ref[me, 0, :, lanes], spec_ref[core, :, lanes], True)
        add_upper(0, firsts_ref[me, 1, :, lanes], spec_ref[2 + core, :, lanes], True)

        @pl.when(core == 1)
        def _():
            add_lower(1, firsts_ref[me - 1, 0, :, lanes], spec_ref[0, :, lanes])

        @pl.when(core == 0)
        def _():
            add_upper(1, firsts_ref[me + 1, 1, :, lanes], spec_ref[3, :, lanes])

        for index, unit in enumerate(units):
            other = chip ^ (index + 1)
            for side in range(2):
                first, later = unit[2 * side : 2 * side + 2]
                body_low, body_high = (first, later) if in_half == 0 else (later, first)
                block = 2 * other + (core if side == 0 else 1 - core)

                @pl.when(other < chip)
                def _():
                    signal = firsts_ref[block, 0, :, lanes]
                    spec = spectrum(forward, margin, signal, body_low, 0, lanes_half)
                    add_lower(me - block, signal, spec)

                @pl.when(other > chip)
                def _():
                    signal = firsts_ref[block, 1, :, lanes]
                    spec = spectrum(forward, margin, signal, body_high, 0, lanes_half)
                    add_upper(block - me, signal, spec)

        after_key, after_value, after_incoming = [
            after_ref[p, :, lanes][0:margin] for p in range(3)
        ]
        gated = after_key * after_value
        zero_lag, one_lag = filter_row(0, 0), filter_row(0, 1)
        fix[0:1] += gated[0:1] * zero_lag
        fix[1:2] += gated[1:2] * zero_lag + gated[0:1] * one_lag

        long_conv = table_dot(inverse, acc[0])
        gated_grad = table_dot(inverse, acc[1])
        query_conv, key_conv, value_conv = [
            jnp.concatenate(
                [
                    with_first(margin, conv_first[p, :, lanes], conv_ref[p, 0:HEAD, lanes]),
                    conv_ref[p, HEAD:, lanes],
                ],
                axis=0,
            )
            for p in range(3)
        ]
        incoming = rows_ref[3, :, lanes].astype(F32)
        beyond = slice(length, length + margin)
        grad_edge = gated_grad[beyond] + fix[EDGE : EDGE + margin]
        grads[0, 0:length] = incoming * long_conv[0:length]
        grads[0, beyond] = after_incoming * (long_conv[beyond] + fix[0:margin])
        grads[1, 0:length] = gated_grad[0:length] * value_conv
        grads[1, beyond] = grad_edge * after_value
        grads[2, 0:length] = gated_grad[0:length] * key_conv
        grads[2, beyond] = grad_edge * after_key
        rows_out[0, :, lanes_out] = (query_conv * long_conv[0:length]).astype(BF16)
        for p in range(3):
            total = weights[p][0:1] * grads[p, 0:length]
            for shift in range(1, margin + 1):
                total = total + weights[p][shift : shift + 1] * grads[p, shift : shift + length]
            rows_out[1 + p, :, lanes_out] = total.astype(BF16)
        for p, out in enumerate(outs):
            copy = pltpu.make_async_copy(
                rows_out.at[p, :, lanes_out], out.at[:, lanes], sems.at[4 * count + p]
            )
            copy.start()
            copies.append(copy)
    for copy in copies:
        copy.wait()


def per_device(query_rows, key_rows, value_rows, short_taps, long_filter, cotangent):
    length, width = query_rows.shape
    groups = long_filter.shape[1]
    blocks = lax.axis_size("seq")
    chans = lax.axis_size("chan")
    chips, half = blocks // 2, width // 2
    margin = short_taps.shape[1] - 1
    tile_width = min(half, 256)
    bits = []
    while 2 << len(bits) < blocks:
        bits.append(2 << len(bits))
    bits.reverse()
    forward, inverse = dft_tables(length)
    shape = jax.ShapeDtypeStruct

    def swap(block, bit):
        return lax.ppermute(block, "seq", [(i, i ^ bit) for i in range(blocks)])

    def call(kernel, outs, args, scratch, in_specs=None, out_specs=None, aliases={}, cost=1):
        return list(
            pl.pallas_call(
                kernel,
                out_shape=outs,
                in_specs=in_specs or [VMEM] * len(args),
                out_specs=out_specs or [VMEM] * len(outs),
                scratch_shapes=scratch,
                input_output_aliases=aliases,
                compiler_params=pltpu.CompilerParams(vmem_limit_bytes=40 * 1024 * 1024),
                cost_estimate=pl.CostEstimate(flops=1, bytes_accessed=cost, transcendentals=0),
            )(*args)
        )

    def after(value, *others):
        return lax.optimization_barrier((value, *others))[0]

    rows, marks, short_taps, long_filter, forward, inverse = call(
        fetch_kernel,
        [
            shape((4, length, width), BF16),
            shape((HEAD, width), BF16),
            shape(short_taps.shape, F32),
            shape(long_filter.shape, F32),
            shape(forward.shape, BF16),
            shape(inverse.shape, BF16),
        ],
        [
            pltpu.with_memory_space_constraint(array, pltpu.HBM)
            for array in (
                query_rows,
                key_rows,
                value_rows,
                cotangent,
                short_taps,
                long_filter,
                forward,
                inverse,
            )
        ],
        [pltpu.VMEM((HEAD, width), F32), pltpu.SemaphoreType.DMA((8,))],
        [HBM] * 8,
    )
    all_marks = []
    for bit in bits + [1]:
        all_marks.append(swap(jnp.concatenate([marks] + all_marks, axis=0), bit))
    firsts_true, conv_first, after_rows = call(
        functools.partial(first_kernel, len(all_marks)),
        [
            shape((blocks, 2, EDGE, width), F32),
            shape((3, EDGE, width), F32),
            shape((3, EDGE, width), F32),
        ],
        [short_taps, marks, *all_marks],
        [
            pltpu.VMEM((blocks + 2, HEAD, width), F32),
            pltpu.VMEM((blocks + 1, 3, EDGE, width), F32),
            pltpu.VMEM((2 * EDGE, width), F32),
        ],
    )
    filter_rows = length * groups // width
    pair_shape = shape((4 * length + 2 * filter_rows, width), BF16)
    first_shape = shape((2 * length, half), BF16)
    later_shape = shape((2 * length + 4 * filter_rows, half), BF16)
    pair, conv, *own_units = call(
        functools.partial(own_kernel, bits, tile_width),
        [pair_shape, shape((3, length, width), F32)] + [first_shape, later_shape] * len(bits),
        [rows, short_taps, long_filter],
        [pltpu.VMEM((3, EDGE + length, tile_width), F32)],
        cost=40 * length * width,
    )

    def gather(own):
        units = {}
        for bit, block in zip(bits, own):
            arrived = {bit // 2: swap(block, bit)}
            for index, unit in units.items():
                arrived[index ^ bit // 2] = swap(unit, bit)
            units.update(arrived)
        return [units[index] for index in range(1, chips)]

    firsts = gather([after(unit, all_marks[0]) for unit in own_units[0::2]])
    sibling = swap(after(pair, all_marks[0]), 1)
    spec, near = call(
        functools.partial(chip_kernel, tile_width, groups, margin),
        [shape((4, 2 * length, width), F32), shape((2, 2 * length, groups), F32)],
        [pair, sibling, firsts_true, forward],
        [],
    )
    shares = call(
        functools.partial(filter_grad_kernel, blocks, tile_width, margin),
        [shape((chips, length, groups), F32)] * 2,
        [spec, near, firsts_true, forward, inverse, *firsts],
        [pltpu.VMEM((blocks + 1, 2 * length, groups), F32)],
    )
    laters = gather([after(unit, near) for unit in own_units[1::2]])
    def odd_swap(values, seq_bit, chan_bit):
        pairs = [
            (i * chans + j, (i ^ seq_bit) * chans + (j ^ chan_bit))
            for i in range(1, blocks, 2)
            for j in range(chans)
        ]
        return lax.ppermute(values, ("seq", "chan"), pairs)

    share, sent = [
        part + lax.ppermute(part, "seq", [(i, i + 1) for i in range(0, blocks, 2)])
        for part in shares
    ]
    for bit in bits:
        share = after(share, *laters) + odd_swap(sent, bit, 0)
        count = share.shape[0] // 2
        if bit > 2:
            share, sent = share[:count], share[count:]
    units = []
    for first, later in zip(firsts, laters):
        units += [first, later, swap(after(first, share), 1), swap(after(later, share), 1)]
    rows_out = shape((length, width), BF16)
    windows = [
        shape((blocks, 2 * length, groups), F32),
        shape((blocks + 3, length, groups), F32),
    ]

    def results(tiles, extra, outs, out_specs):
        args = [rows, short_taps, long_filter, conv, conv_first, firsts_true, after_rows]
        args += [sibling, spec, forward, inverse, *units]
        count = len(args)
        return call(
            functools.partial(result_kernel, blocks, tile_width, tiles),
            outs,
            args + extra,
            [
                pltpu.VMEM((2, 2 * length, tile_width), F32),
                pltpu.VMEM((2 * EDGE, tile_width), F32),
                pltpu.VMEM((3, length + EDGE, tile_width), F32),
                pltpu.VMEM((4, length, len(tiles) * tile_width), BF16),
                pltpu.SemaphoreType.DMA((4 * len(tiles),)),
            ],
            [VMEM] * count + ([VMEM] * 2 + [HBM] * 4 if extra else []),
            out_specs,
            {count + 2 + index: index for index in range(4)} if extra else {},
            80 * length * len(tiles) * tile_width,
        )

    tiles = width // tile_width
    cuts = [0, max(1, tiles // 4), tiles - tiles // 4, tiles]
    *final, spectra, filter_blocks = results(
        range(cuts[0], cuts[1]), [], [rows_out] * 4 + windows, [HBM] * 4 + [VMEM] * 2
    )
    ready = [final]
    for begin, end in zip(cuts[1:], cuts[2:]):
        if begin < end:
            final = results(
                range(begin, end), [spectra, filter_blocks, *final], [rows_out] * 4, [HBM] * 4
            )
        ready.append(final)

    steps = [1 << index for index in range(chans.bit_length() - 1)]
    for index, step in enumerate(steps):
        arrived = odd_swap(share, 0, step)
        beside = index + len(ready) - len(steps)
        if beside >= 0:
            share = after(share, ready[beside][0])
        share = share + arrived
    returned = lax.ppermute(share, "seq", [(i + 1, i) for i in range(0, blocks, 2)])
    grad_filter = jnp.where(lax.axis_index("seq") % 2 == 1, share[0], returned[1])
    return (*final, grad_filter)


def solution(mesh):
    in_specs = (
        P("seq", "chan"),
        P("seq", "chan"),
        P("seq", "chan"),
        P(None, None, "chan"),
        P("seq", None),
        P("seq", "chan"),
    )
    out_specs = (
        P("seq", "chan"),
        P("seq", "chan"),
        P("seq", "chan"),
        P("seq", "chan"),
        P("seq", None),
    )
    return jax.shard_map(
        per_device, mesh=mesh, in_specs=in_specs, out_specs=out_specs, check_vma=False
    )
```

```python
import functools

import jax
import jax.numpy as jnp
import ml_dtypes
import numpy as np
from jax import lax
from jax.experimental import pallas as pl
from jax.experimental.pallas import tpu as pltpu
from jax.sharding import PartitionSpec as P

F32 = jnp.float32
BF16 = jnp.bfloat16
EDGE = 8
HEAD = 16
VMEM = pl.BlockSpec(memory_space=pltpu.VMEM)
HBM = pl.BlockSpec(memory_space=pltpu.HBM)


def split_table(table):
    high = table.astype(ml_dtypes.bfloat16)
    low = (table - high.astype(np.float64)).astype(ml_dtypes.bfloat16)
    return high, low


def dft_tables(length):
    frequency = np.pi * (2 * np.arange(length) + 1) / (2 * length)
    into = frequency[:, None] * np.arange(length)[None, :]
    high, low = split_table(np.concatenate([np.cos(into), -np.sin(into)], axis=0))
    forward = np.concatenate([high, high, low], axis=1)
    forward = np.pad(forward, ((0, EDGE), (0, 0)))
    back = np.arange(length + EDGE)[:, None] * frequency[None, :]
    high, low = split_table(np.concatenate([np.cos(back), -np.sin(back)], axis=1) / length)
    inverse = np.concatenate([high, high, low], axis=1)
    return jnp.asarray(forward), jnp.asarray(inverse)


def halves(values):
    high = values.astype(BF16)
    return high, (values - high.astype(F32)).astype(BF16)


def table_dot(table, values):
    high, low = halves(values)
    return jnp.dot(
        table, jnp.concatenate([high, low, high], axis=0), preferred_element_type=F32
    )


def tap_sum(rows_ref, first, count, weights):
    total = weights[0:1] * rows_ref[first : first + count]
    for shift in range(1, weights.shape[0]):
        total = total + weights[shift : shift + 1] * rows_ref[first - shift : first - shift + count]
    return total


def put_filter(unit, first, filter_high, filter_low):
    length, groups = filter_high.shape
    width = unit.shape[1]
    rows = length * groups // width
    for tile in range(width // groups):
        lanes = slice(tile * groups, (tile + 1) * groups)
        part = slice(tile * rows, (tile + 1) * rows)
        unit[first : first + rows, lanes] = filter_high[part]
        unit[first + rows : first + 2 * rows, lanes] = filter_low[part]


def get_filter(unit, first, length, groups):
    width = unit.shape[1]
    rows = length * groups // width
    pieces = []
    for tile in range(width // groups):
        lanes = slice(tile * groups, (tile + 1) * groups)
        pieces.append(
            unit[first : first + rows, lanes].astype(F32)
            + unit[first + rows : first + 2 * rows, lanes].astype(F32)
        )
    return jnp.concatenate(pieces, axis=0)


def fetch_kernel(q_hbm, k_hbm, v_hbm, c_hbm, *refs):
    others = refs[:4]
    rows_ref, marks_ref, *other_refs = refs[4:10]
    edge, sems = refs[10:]
    length = q_hbm.shape[0]
    copies = [
        pltpu.make_async_copy(source, rows_ref.at[index], sems.at[index])
        for index, source in enumerate((q_hbm, k_hbm, v_hbm, c_hbm))
    ]
    copies += [
        pltpu.make_async_copy(source, target, sems.at[4 + index])
        for index, (source, target) in enumerate(zip(others, other_refs))
    ]
    for copy in copies:
        copy.start()
    for copy in copies[:4]:
        copy.wait()
    margin = others[0].shape[1] - 1
    edge[...] = jnp.zeros(edge.shape, F32)
    for p in range(4):
        first = rows_ref[p, 0:HEAD].astype(F32)
        edge[(3 + p) * margin : (4 + p) * margin] = first[0:margin]
        if p < 3:
            last = rows_ref[p, length - HEAD :].astype(F32)
            edge[p * margin : (p + 1) * margin] = last[HEAD - margin :]
    marks_ref[...] = edge[...].astype(BF16)
    for copy in copies[4:]:
        copy.wait()


def own_kernel(bits, tile_width, rows_ref, taps_ref, filter_ref, pair_ref, conv_ref, *refs):
    unit_refs, window = refs[:-1], refs[-1]
    length, width = rows_ref.shape[1:]
    half = width // 2
    me = lax.axis_index("seq")
    filter_high, filter_low = halves(filter_ref[...])
    put_filter(pair_ref, 4 * length, filter_high, filter_low)
    for later in unit_refs[1::2]:
        put_filter(later, 2 * length, filter_high, filter_low)
    window[:, 0:EDGE] = jnp.zeros((3, EDGE, tile_width), F32)
    for tile in range(width // tile_width):
        lanes = slice(tile * tile_width, (tile + 1) * tile_width)
        convs = []
        for p in range(3):
            window[p, EDGE:] = rows_ref[p, :, lanes].astype(F32)
            conv = tap_sum(window.at[p], EDGE, length, taps_ref[p, :, lanes])
            conv_ref[p, :, lanes] = conv
            convs.append(conv)
        incoming = rows_ref[3, :, lanes].astype(F32)
        parts = [*halves(convs[1] * convs[2]), *halves(incoming * convs[0])]
        for index, part in enumerate(parts):
            pair_ref[index * length : (index + 1) * length, lanes] = part
        in_half = tile * tile_width // half
        lanes_half = slice(tile * tile_width % half, tile * tile_width % half + tile_width)
        for index, bit in enumerate(bits):
            low_side = (me // bit) % 2 == 0
            first, later = unit_refs[2 * index : 2 * index + 2]
            target_low, target_high = (first, later) if in_half == 0 else (later, first)

            @pl.when(low_side)
            def _():
                target_low[0:length, lanes_half] = parts[0]
                target_low[length : 2 * length, lanes_half] = parts[1]

            @pl.when(jnp.logical_not(low_side))
            def _():
                target_high[0:length, lanes_half] = parts[2]
                target_high[length : 2 * length, lanes_half] = parts[3]


def first_kernel(marks_refs, taps_ref, own_marks, *refs):
    arrived = refs[:marks_refs]
    firsts_ref, conv_ref, after_ref, marks, convs, window = refs[marks_refs:]
    blocks = firsts_ref.shape[0]
    me = lax.axis_index("seq")
    margin = taps_ref.shape[1] - 1
    nothing = jnp.zeros(marks.shape[1:], F32)
    marks[0] = nothing
    marks[blocks + 1] = nothing
    marks[me + 1] = own_marks[...].astype(F32)
    index = 1
    for ref in arrived:
        for place in range(ref.shape[0] // HEAD):
            marks[(me ^ index_of(index, blocks)) + 1] = ref[
                place * HEAD : (place + 1) * HEAD
            ].astype(F32)
            index += 1
    window[...] = jnp.zeros(window.shape, F32)
    convs[blocks] = jnp.zeros(convs.shape[1:], F32)
    for block in range(blocks):
        for p in range(3):
            window[EDGE - margin : EDGE] = marks[block, p * margin : (p + 1) * margin]
            window[EDGE : EDGE + margin] = marks[block + 1, (3 + p) * margin : (4 + p) * margin]
            convs[block, p] = tap_sum(window, EDGE, EDGE, taps_ref[p])
        window[EDGE : EDGE + margin] = marks[block + 1, 6 * margin : 7 * margin]
        firsts_ref[block, 0] = convs[block, 1] * convs[block, 2]
        firsts_ref[block, 1] = window[EDGE:] * convs[block, 0]
    conv_ref[...] = convs[me]
    after_ref[0:2] = convs[me + 1, 1:3]
    window[EDGE : EDGE + margin] = marks[me + 2, 6 * margin : 7 * margin]
    after_ref[2] = window[EDGE:]


def index_of(count, blocks):
    order, bit = [0], blocks // 2
    while bit:
        order += [index ^ bit for index in order]
        bit //= 2
    return order[count]


def with_first(margin, first, rows):
    true = jnp.concatenate([first, jnp.zeros((HEAD - EDGE, first.shape[1]), F32)], axis=0)
    row = lax.broadcasted_iota(jnp.int32, true.shape, 0)
    return jnp.where(row < margin, true, rows)


def spectrum(forward, margin, first, ref, place, lanes):
    length = forward.shape[1] // 3
    parts = []
    for index, part in enumerate(halves(first)):
        begin = place + index * length
        head = with_first(margin, part.astype(F32), ref[begin : begin + HEAD, lanes].astype(F32))
        parts += [head.astype(BF16), ref[begin + HEAD : begin + length, lanes]]
    return jnp.dot(
        forward, jnp.concatenate([*parts, *parts[0:2]], axis=0), preferred_element_type=F32
    )


def cross_add(cross, distance, early, late, groups):
    length = early.shape[0] // 2
    e_re, e_im = early[0:length], early[length:]
    l_re, l_im = late[0:length], late[length:]
    re = e_re * l_re + e_im * l_im
    im = e_re * l_im - e_im * l_re
    parts = range(early.shape[1] // groups)
    cross[distance, 0:length] += sum(re[:, p * groups : (p + 1) * groups] for p in parts)
    cross[distance, length:] += sum(im[:, p * groups : (p + 1) * groups] for p in parts)


def chip_kernel(
    tile_width,
    groups,
    margin,
    own_ref,
    other_ref,
    firsts_ref,
    forward_ref,
    spec_ref,
    cross_ref,
):
    length = forward_ref.shape[1] // 3
    width = own_ref.shape[1]
    me = lax.axis_index("seq")
    core = me % 2
    forward = forward_ref[0 : 2 * length]
    cross_ref[...] = jnp.zeros(cross_ref.shape, F32)

    def one_tile(step, carry):
        lanes = pl.ds(pl.multiple_of(step * tile_width, tile_width), tile_width)
        for ref, slot, block in ((own_ref, core, me), (other_ref, 1 - core, me ^ 1)):
            for kind in range(2):
                first = firsts_ref[block, kind, :, lanes]
                spec_ref[2 * kind + slot, :, lanes] = spectrum(
                    forward, margin, first, ref, 2 * kind * length, lanes
                )
        cross_add(cross_ref, 0, spec_ref[core, :, lanes], spec_ref[2 + core, :, lanes], groups)

        @pl.when(2 * step * tile_width // width == core)
        def _():
            cross_add(cross_ref, 1, spec_ref[0, :, lanes], spec_ref[3, :, lanes], groups)

        return carry

    lax.fori_loop(0, width // tile_width, one_tile, 0)


def filter_grad_kernel(
    blocks,
    tile_width,
    margin,
    spec_ref,
    near_ref,
    firsts_ref,
    forward_ref,
    inverse_ref,
    *refs,
):
    chips = blocks // 2
    units = refs[: chips - 1]
    gf_refs, cross = refs[chips - 1 : -1], refs[-1]
    length = forward_ref.shape[1] // 3
    groups = near_ref.shape[2]
    half = spec_ref.shape[2] // 2
    me = lax.axis_index("seq")
    core, chip = me % 2, me // 2
    forward = forward_ref[0 : 2 * length]
    cross[0:2] = near_ref[...]
    cross[2:] = jnp.zeros((blocks - 1, 2 * length, groups), F32)
    for index, unit in enumerate(units):
        other = chip ^ (index + 1)

        def one_tile(step, carry):
            start = pl.multiple_of(step * tile_width, tile_width)
            lanes = pl.ds(start, tile_width)
            kind = jnp.where(other < chip, 0, 1)
            wide_lanes = pl.ds(pl.multiple_of(kind * half + start, tile_width), tile_width)
            first = firsts_ref[2 * other + core, kind, :, wide_lanes]
            spec = spectrum(forward, margin, first, unit, 0, lanes)

            @pl.when(other < chip)
            def _():
                for slot in range(2):
                    distance = 2 * chip + slot - (2 * other + core)
                    cross_add(cross, distance, spec, spec_ref[2 + slot, :, wide_lanes], groups)

            @pl.when(other > chip)
            def _():
                for slot in range(2):
                    distance = 2 * other + core - (2 * chip + slot)
                    cross_add(cross, distance, spec_ref[slot, :, wide_lanes], spec, groups)

            return carry

        lax.fori_loop(0, half // tile_width, one_tile, 0)

    inverse = inverse_ref[0:length]
    sign = signs(length, groups)
    for place in range(blocks):
        block = (me | 1) ^ place
        re = cross[block, 0:length] + sign * cross[block + 1, length:]
        im = cross[block, length:] - sign * cross[block + 1, 0:length]
        gf_refs[place // chips][place % chips] = table_dot(inverse, jnp.concatenate([re, im], axis=0))


def signs(length, groups):
    row = lax.broadcasted_iota(jnp.int32, (length, groups), 0)
    return jnp.where(row % 2 == 0, 1.0, -1.0)


def result_kernel(blocks, tile_width, tiles, *refs):
    others = blocks // 2 - 1
    (
        rows_ref,
        taps_ref,
        filter_ref,
        conv_ref,
        conv_first,
        firsts_ref,
        after_ref,
        other_ref,
        spec_ref,
        forward_ref,
        inverse_ref,
    ) = refs[:11]
    refs = refs[11:]
    units = [refs[4 * index : 4 * index + 4] for index in range(others)]
    refs = refs[4 * others :]
    if tiles[0] == 0:
        outs, (spectra, filter_rows) = refs[:4], refs[4:6]
        refs = refs[6:]
    else:
        spectra, filter_rows = refs[:2]
        outs = refs[6:10]
        refs = refs[10:]
    acc, fix, grads, rows_out, sems = refs
    length, width = rows_ref.shape[1:]
    groups = filter_ref.shape[1]
    half = width // 2
    margin = taps_ref.shape[1] - 1
    me = lax.axis_index("seq")
    core, chip = me % 2, me // 2
    forward, inverse = forward_ref[0 : 2 * length], inverse_ref[...]

    if tiles[0] == 0:
        sign = signs(length, groups)
        for edge in (0, 1, blocks + 2):
            filter_rows[edge] = jnp.zeros((length, groups), F32)
        filter_rows[me + 2] = filter_ref[...]
        filter_rows[(me ^ 1) + 2] = get_filter(other_ref, 4 * length, length, groups)
        for index, unit in enumerate(units):
            block = me ^ (2 * (index + 1))
            filter_rows[block + 2] = get_filter(unit[1], 2 * length, length, groups)
            filter_rows[(block ^ 1) + 2] = get_filter(unit[3], 2 * length, length, groups)
        previous = None
        for distance in range(blocks):
            own = table_dot(forward, filter_rows[distance + 2])
            if previous is None:
                spectra[distance] = own
            else:
                spectra[distance, 0:length] = own[0:length] - sign * previous[length:]
                spectra[distance, length:] = own[length:] + sign * previous[0:length]
            previous = own

    def wide(values):
        return jnp.concatenate([values] * (tile_width // groups), axis=1)

    def filter_row(block, row):
        return wide(filter_rows[block + 2, pl.ds(row, 1)])

    def add_lower(distance, signal, spec, fresh=False):
        re, im = spec[0:length], spec[length:]
        h_re, h_im = wide(spectra[distance, 0:length]), wide(spectra[distance, length:])
        new_re = h_re * re - h_im * im
        new_im = h_re * im + h_im * re
        acc[0, 0:length] = new_re if fresh else acc[0, 0:length] + new_re
        acc[0, length:] = new_im if fresh else acc[0, length:] + new_im
        near = filter_row(distance + 1, 0) + filter_row(distance - 1, 0)
        far = filter_row(distance + 1, 1) + filter_row(distance - 1, 1)
        fix[0:1] += signal[0:1] * near
        fix[1:2] += signal[0:1] * far + signal[1:2] * near

    def add_upper(distance, signal, spec, fresh=False):
        re, im = spec[0:length], spec[length:]
        h_re, h_im = wide(spectra[distance, 0:length]), wide(spectra[distance, length:])
        new_re = h_re * re + h_im * im
        new_im = h_re * im - h_im * re
        acc[1, 0:length] = new_re if fresh else acc[1, 0:length] + new_re
        acc[1, length:] = new_im if fresh else acc[1, length:] + new_im
        fix[EDGE + 1 : EDGE + 2] += signal[0:1] * (
            filter_row(distance - 2, length - 1) + filter_row(distance, length - 1)
        )

    copies = []
    for count, tile in enumerate(tiles):
        start = tile * tile_width
        in_half = start // half
        lanes = slice(start, start + tile_width)
        lanes_half = slice(start % half, start % half + tile_width)
        lanes_out = slice(count * tile_width, (count + 1) * tile_width)
        weights = [taps_ref[p, :, lanes] for p in range(3)]
        fix[...] = jnp.zeros(fix.shape, F32)

        add_lower(0, firsts_ref[me, 0, :, lanes], spec_ref[core, :, lanes], True)
        add_upper(0, firsts_ref[me, 1, :, lanes], spec_ref[2 + core, :, lanes], True)

        @pl.when(core == 1)
        def _():
            add_lower(1, firsts_ref[me - 1, 0, :, lanes], spec_ref[0, :, lanes])

        @pl.when(core == 0)
        def _():
            add_upper(1, firsts_ref[me + 1, 1, :, lanes], spec_ref[3, :, lanes])

        for index, unit in enumerate(units):
            other = chip ^ (index + 1)
            for side in range(2):
                first, later = unit[2 * side : 2 * side + 2]
                body_low, body_high = (first, later) if in_half == 0 else (later, first)
                block = 2 * other + (core if side == 0 else 1 - core)

                @pl.when(other < chip)
                def _():
                    signal = firsts_ref[block, 0, :, lanes]
                    spec = spectrum(forward, margin, signal, body_low, 0, lanes_half)
                    add_lower(me - block, signal, spec)

                @pl.when(other > chip)
                def _():
                    signal = firsts_ref[block, 1, :, lanes]
                    spec = spectrum(forward, margin, signal, body_high, 0, lanes_half)
                    add_upper(block - me, signal, spec)

        after_key, after_value, after_incoming = [
            after_ref[p, :, lanes][0:margin] for p in range(3)
        ]
        gated = after_key * after_value
        zero_lag, one_lag = filter_row(0, 0), filter_row(0, 1)
        fix[0:1] += gated[0:1] * zero_lag
        fix[1:2] += gated[1:2] * zero_lag + gated[0:1] * one_lag

        long_conv = table_dot(inverse, acc[0])
        gated_grad = table_dot(inverse, acc[1])
        query_conv, key_conv, value_conv = [
            jnp.concatenate(
                [
                    with_first(margin, conv_first[p, :, lanes], conv_ref[p, 0:HEAD, lanes]),
                    conv_ref[p, HEAD:, lanes],
                ],
                axis=0,
            )
            for p in range(3)
        ]
        incoming = rows_ref[3, :, lanes].astype(F32)
        beyond = slice(length, length + margin)
        grad_edge = gated_grad[beyond] + fix[EDGE : EDGE + margin]
        grads[0, 0:length] = incoming * long_conv[0:length]
        grads[0, beyond] = after_incoming * (long_conv[beyond] + fix[0:margin])
        grads[1, 0:length] = gated_grad[0:length] * value_conv
        grads[1, beyond] = grad_edge * after_value
        grads[2, 0:length] = gated_grad[0:length] * key_conv
        grads[2, beyond] = grad_edge * after_key
        rows_out[0, :, lanes_out] = (query_conv * long_conv[0:length]).astype(BF16)
        for p in range(3):
            total = weights[p][0:1] * grads[p, 0:length]
            for shift in range(1, margin + 1):
                total = total + weights[p][shift : shift + 1] * grads[p, shift : shift + length]
            rows_out[1 + p, :, lanes_out] = total.astype(BF16)
        for p, out in enumerate(outs):
            copy = pltpu.make_async_copy(
                rows_out.at[p, :, lanes_out], out.at[:, lanes], sems.at[4 * count + p]
            )
            copy.start()
            copies.append(copy)
    for copy in copies:
        copy.wait()


def per_device(query_rows, key_rows, value_rows, short_taps, long_filter, cotangent):
    length, width = query_rows.shape
    groups = long_filter.shape[1]
    blocks = lax.axis_size("seq")
    chans = lax.axis_size("chan")
    chips, half = blocks // 2, width // 2
    margin = short_taps.shape[1] - 1
    tile_width = min(half, 256)
    bits = []
    while 2 << len(bits) < blocks:
        bits.append(2 << len(bits))
    bits.reverse()
    forward, inverse = dft_tables(length)
    shape = jax.ShapeDtypeStruct

    def swap(block, bit):
        return lax.ppermute(block, "seq", [(i, i ^ bit) for i in range(blocks)])

    def call(kernel, outs, args, scratch, in_specs=None, out_specs=None, aliases={}, cost=1):
        return list(
            pl.pallas_call(
                kernel,
                out_shape=outs,
                in_specs=in_specs or [VMEM] * len(args),
                out_specs=out_specs or [VMEM] * len(outs),
                scratch_shapes=scratch,
                input_output_aliases=aliases,
                compiler_params=pltpu.CompilerParams(vmem_limit_bytes=40 * 1024 * 1024),
                cost_estimate=pl.CostEstimate(flops=1, bytes_accessed=cost, transcendentals=0),
            )(*args)
        )

    def after(value, *others):
        return lax.optimization_barrier((value, *others))[0]

    rows, marks, short_taps, long_filter, forward, inverse = call(
        fetch_kernel,
        [
            shape((4, length, width), BF16),
            shape((HEAD, width), BF16),
            shape(short_taps.shape, F32),
            shape(long_filter.shape, F32),
            shape(forward.shape, BF16),
            shape(inverse.shape, BF16),
        ],
        [
            pltpu.with_memory_space_constraint(array, pltpu.HBM)
            for array in (
                query_rows,
                key_rows,
                value_rows,
                cotangent,
                short_taps,
                long_filter,
                forward,
                inverse,
            )
        ],
        [pltpu.VMEM((HEAD, width), F32), pltpu.SemaphoreType.DMA((8,))],
        [HBM] * 8,
    )
    all_marks = []
    for bit in bits + [1]:
        all_marks.append(swap(jnp.concatenate([marks] + all_marks, axis=0), bit))
    firsts_true, conv_first, after_rows = call(
        functools.partial(first_kernel, len(all_marks)),
        [
            shape((blocks, 2, EDGE, width), F32),
            shape((3, EDGE, width), F32),
            shape((3, EDGE, width), F32),
        ],
        [short_taps, marks, *all_marks],
        [
            pltpu.VMEM((blocks + 2, HEAD, width), F32),
            pltpu.VMEM((blocks + 1, 3, EDGE, width), F32),
            pltpu.VMEM((2 * EDGE, width), F32),
        ],
    )
    filter_rows = length * groups // width
    pair_shape = shape((4 * length + 2 * filter_rows, width), BF16)
    first_shape = shape((2 * length, half), BF16)
    later_shape = shape((2 * length + 4 * filter_rows, half), BF16)
    pair, conv, *own_units = call(
        functools.partial(own_kernel, bits, tile_width),
        [pair_shape, shape((3, length, width), F32)] + [first_shape, later_shape] * len(bits),
        [rows, short_taps, long_filter],
        [pltpu.VMEM((3, EDGE + length, tile_width), F32)],
        cost=40 * length * width,
    )

    def gather(own):
        units = {}
        for bit, block in zip(bits, own):
            arrived = {bit // 2: swap(block, bit)}
            for index, unit in units.items():
                arrived[index ^ bit // 2] = swap(unit, bit)
            units.update(arrived)
        return [units[index] for index in range(1, chips)]

    firsts = gather([after(unit, all_marks[0]) for unit in own_units[0::2]])
    sibling = swap(after(pair, all_marks[0]), 1)
    spec, near = call(
        functools.partial(chip_kernel, tile_width, groups, margin),
        [shape((4, 2 * length, width), F32), shape((2, 2 * length, groups), F32)],
        [pair, sibling, firsts_true, forward],
        [],
    )
    shares = call(
        functools.partial(filter_grad_kernel, blocks, tile_width, margin),
        [shape((chips, length, groups), F32)] * 2,
        [spec, near, firsts_true, forward, inverse, *firsts],
        [pltpu.VMEM((blocks + 1, 2 * length, groups), F32)],
    )
    laters = gather([after(unit, near) for unit in own_units[1::2]])
    def odd_swap(values, seq_bit, chan_bit):
        pairs = [
            (i * chans + j, (i ^ seq_bit) * chans + (j ^ chan_bit) if i % 2 else i * chans + j)
            for i in range(blocks)
            for j in range(chans)
        ]
        return lax.ppermute(values, ("seq", "chan"), pairs)

    share, sent = [part + swap(part, 1) for part in shares]
    for bit in bits:
        share = after(share, *laters) + odd_swap(sent, bit, 0)
        count = share.shape[0] // 2
        if bit > 2:
            share, sent = share[:count], share[count:]
    units = []
    for first, later in zip(firsts, laters):
        units += [first, later, swap(after(first, share), 1), swap(after(later, share), 1)]
    rows_out = shape((length, width), BF16)
    windows = [
        shape((blocks, 2 * length, groups), F32),
        shape((blocks + 3, length, groups), F32),
    ]

    def results(tiles, extra, outs, out_specs):
        args = [rows, short_taps, long_filter, conv, conv_first, firsts_true, after_rows]
        args += [sibling, spec, forward, inverse, *units]
        count = len(args)
        return call(
            functools.partial(result_kernel, blocks, tile_width, tiles),
            outs,
            args + extra,
            [
                pltpu.VMEM((2, 2 * length, tile_width), F32),
                pltpu.VMEM((2 * EDGE, tile_width), F32),
                pltpu.VMEM((3, length + EDGE, tile_width), F32),
                pltpu.VMEM((4, length, len(tiles) * tile_width), BF16),
                pltpu.SemaphoreType.DMA((4 * len(tiles),)),
            ],
            [VMEM] * count + ([VMEM] * 2 + [HBM] * 4 if extra else []),
            out_specs,
            {count + 2 + index: index for index in range(4)} if extra else {},
            80 * length * len(tiles) * tile_width,
        )

    tiles = width // tile_width
    cuts = [0, max(1, tiles // 4), tiles - tiles // 4, tiles]
    *final, spectra, filter_blocks = results(
        range(cuts[0], cuts[1]), [], [rows_out] * 4 + windows, [HBM] * 4 + [VMEM] * 2
    )
    ready = [final]
    for begin, end in zip(cuts[1:], cuts[2:]):
        if begin < end:
            final = results(
                range(begin, end), [spectra, filter_blocks, *final], [rows_out] * 4, [HBM] * 4
            )
        ready.append(final)

    steps = [1 << index for index in range(chans.bit_length() - 1)]
    for index, step in enumerate(steps):
        arrived = odd_swap(share, 0, step)
        beside = index + len(ready) - len(steps)
        if beside >= 0:
            share = after(share, ready[beside][0])
        share = share + arrived
    returned = swap(share, 1)
    grad_filter = jnp.where(lax.axis_index("seq") % 2 == 1, share[0], returned[1])
    return (*final, grad_filter)


def solution(mesh):
    in_specs = (
        P("seq", "chan"),
        P("seq", "chan"),
        P("seq", "chan"),
        P(None, None, "chan"),
        P("seq", None),
        P("seq", "chan"),
    )
    out_specs = (
        P("seq", "chan"),
        P("seq", "chan"),
        P("seq", "chan"),
        P("seq", "chan"),
        P("seq", None),
    )
    return jax.shard_map(
        per_device, mesh=mesh, in_specs=in_specs, out_specs=out_specs, check_vma=False
    )
```

```python
import functools

import jax
import jax.numpy as jnp
import ml_dtypes
import numpy as np
from jax import lax
from jax.experimental import pallas as pl
from jax.experimental.pallas import tpu as pltpu
from jax.sharding import PartitionSpec as P

F32 = jnp.float32
BF16 = jnp.bfloat16
EDGE = 8
HEAD = 16
VMEM = pl.BlockSpec(memory_space=pltpu.VMEM)
HBM = pl.BlockSpec(memory_space=pltpu.HBM)


def split_table(table):
    high = table.astype(ml_dtypes.bfloat16)
    low = (table - high.astype(np.float64)).astype(ml_dtypes.bfloat16)
    return high, low


def dft_tables(length):
    frequency = np.pi * (2 * np.arange(length) + 1) / (2 * length)
    into = frequency[:, None] * np.arange(length)[None, :]
    high, low = split_table(np.concatenate([np.cos(into), -np.sin(into)], axis=0))
    forward = np.concatenate([high, high, low], axis=1)
    forward = np.pad(forward, ((0, EDGE), (0, 0)))
    back = np.arange(length + EDGE)[:, None] * frequency[None, :]
    high, low = split_table(np.concatenate([np.cos(back), -np.sin(back)], axis=1) / length)
    inverse = np.concatenate([high, high, low], axis=1)
    return jnp.asarray(forward), jnp.asarray(inverse)


def halves(values):
    high = values.astype(BF16)
    return high, (values - high.astype(F32)).astype(BF16)


def table_dot(table, values):
    high, low = halves(values)
    return jnp.dot(
        table, jnp.concatenate([high, low, high], axis=0), preferred_element_type=F32
    )


def tap_sum(rows_ref, first, count, weights):
    total = weights[0:1] * rows_ref[first : first + count]
    for shift in range(1, weights.shape[0]):
        total = total + weights[shift : shift + 1] * rows_ref[first - shift : first - shift + count]
    return total


def put_filter(unit, first, filter_high, filter_low):
    length, groups = filter_high.shape
    width = unit.shape[1]
    rows = length * groups // width
    for tile in range(width // groups):
        lanes = slice(tile * groups, (tile + 1) * groups)
        part = slice(tile * rows, (tile + 1) * rows)
        unit[first : first + rows, lanes] = filter_high[part]
        unit[first + rows : first + 2 * rows, lanes] = filter_low[part]


def get_filter(unit, first, length, groups):
    width = unit.shape[1]
    rows = length * groups // width
    pieces = []
    for tile in range(width // groups):
        lanes = slice(tile * groups, (tile + 1) * groups)
        pieces.append(
            unit[first : first + rows, lanes].astype(F32)
            + unit[first + rows : first + 2 * rows, lanes].astype(F32)
        )
    return jnp.concatenate(pieces, axis=0)


def fetch_kernel(q_hbm, k_hbm, v_hbm, c_hbm, *refs):
    others = refs[:4]
    rows_ref, marks_ref, *other_refs = refs[4:10]
    edge, sems = refs[10:]
    length = q_hbm.shape[0]
    copies = [
        pltpu.make_async_copy(source, rows_ref.at[index], sems.at[index])
        for index, source in enumerate((q_hbm, k_hbm, v_hbm, c_hbm))
    ]
    copies += [
        pltpu.make_async_copy(source, target, sems.at[4 + index])
        for index, (source, target) in enumerate(zip(others, other_refs))
    ]
    for copy in copies:
        copy.start()
    for copy in copies[:4]:
        copy.wait()
    margin = others[0].shape[1] - 1
    edge[...] = jnp.zeros(edge.shape, F32)
    for p in range(4):
        first = rows_ref[p, 0:HEAD].astype(F32)
        edge[(3 + p) * margin : (4 + p) * margin] = first[0:margin]
        if p < 3:
            last = rows_ref[p, length - HEAD :].astype(F32)
            edge[p * margin : (p + 1) * margin] = last[HEAD - margin :]
    marks_ref[...] = edge[...].astype(BF16)
    for copy in copies[4:]:
        copy.wait()


def own_kernel(bits, tile_width, rows_ref, taps_ref, filter_ref, pair_ref, conv_ref, *refs):
    unit_refs, window = refs[:-1], refs[-1]
    length, width = rows_ref.shape[1:]
    half = width // 2
    me = lax.axis_index("seq")
    filter_high, filter_low = halves(filter_ref[...])
    put_filter(pair_ref, 4 * length, filter_high, filter_low)
    for later in unit_refs[1::2]:
        put_filter(later, 2 * length, filter_high, filter_low)
    window[:, 0:EDGE] = jnp.zeros((3, EDGE, tile_width), F32)
    for tile in range(width // tile_width):
        lanes = slice(tile * tile_width, (tile + 1) * tile_width)
        convs = []
        for p in range(3):
            window[p, EDGE:] = rows_ref[p, :, lanes].astype(F32)
            conv = tap_sum(window.at[p], EDGE, length, taps_ref[p, :, lanes])
            conv_ref[p, :, lanes] = conv
            convs.append(conv)
        incoming = rows_ref[3, :, lanes].astype(F32)
        parts = [*halves(convs[1] * convs[2]), *halves(incoming * convs[0])]
        for index, part in enumerate(parts):
            pair_ref[index * length : (index + 1) * length, lanes] = part
        in_half = tile * tile_width // half
        lanes_half = slice(tile * tile_width % half, tile * tile_width % half + tile_width)
        for index, bit in enumerate(bits):
            low_side = (me // bit) % 2 == 0
            first, later = unit_refs[2 * index : 2 * index + 2]
            target_low, target_high = (first, later) if in_half == 0 else (later, first)

            @pl.when(low_side)
            def _():
                target_low[0:length, lanes_half] = parts[0]
                target_low[length : 2 * length, lanes_half] = parts[1]

            @pl.when(jnp.logical_not(low_side))
            def _():
                target_high[0:length, lanes_half] = parts[2]
                target_high[length : 2 * length, lanes_half] = parts[3]


def first_kernel(marks_refs, taps_ref, own_marks, *refs):
    arrived = refs[:marks_refs]
    firsts_ref, conv_ref, after_ref, marks, convs, window = refs[marks_refs:]
    blocks = firsts_ref.shape[0]
    me = lax.axis_index("seq")
    margin = taps_ref.shape[1] - 1
    nothing = jnp.zeros(marks.shape[1:], F32)
    marks[0] = nothing
    marks[blocks + 1] = nothing
    marks[me + 1] = own_marks[...].astype(F32)
    index = 1
    for ref in arrived:
        for place in range(ref.shape[0] // HEAD):
            marks[(me ^ index_of(index, blocks)) + 1] = ref[
                place * HEAD : (place + 1) * HEAD
            ].astype(F32)
            index += 1
    window[...] = jnp.zeros(window.shape, F32)
    convs[blocks] = jnp.zeros(convs.shape[1:], F32)
    for block in range(blocks):
        for p in range(3):
            window[EDGE - margin : EDGE] = marks[block, p * margin : (p + 1) * margin]
            window[EDGE : EDGE + margin] = marks[block + 1, (3 + p) * margin : (4 + p) * margin]
            convs[block, p] = tap_sum(window, EDGE, EDGE, taps_ref[p])
        window[EDGE : EDGE + margin] = marks[block + 1, 6 * margin : 7 * margin]
        firsts_ref[block, 0] = convs[block, 1] * convs[block, 2]
        firsts_ref[block, 1] = window[EDGE:] * convs[block, 0]
    conv_ref[...] = convs[me]
    after_ref[0:2] = convs[me + 1, 1:3]
    window[EDGE : EDGE + margin] = marks[me + 2, 6 * margin : 7 * margin]
    after_ref[2] = window[EDGE:]


def index_of(count, blocks):
    order, bit = [0], blocks // 2
    while bit:
        order += [index ^ bit for index in order]
        bit //= 2
    return order[count]


def with_first(margin, first, rows):
    true = jnp.concatenate([first, jnp.zeros((HEAD - EDGE, first.shape[1]), F32)], axis=0)
    row = lax.broadcasted_iota(jnp.int32, true.shape, 0)
    return jnp.where(row < margin, true, rows)


def spectrum(forward, margin, first, ref, place, lanes):
    length = forward.shape[1] // 3
    parts = []
    for index, part in enumerate(halves(first)):
        begin = place + index * length
        head = with_first(margin, part.astype(F32), ref[begin : begin + HEAD, lanes].astype(F32))
        parts += [head.astype(BF16), ref[begin + HEAD : begin + length, lanes]]
    return jnp.dot(
        forward, jnp.concatenate([*parts, *parts[0:2]], axis=0), preferred_element_type=F32
    )


def cross_add(cross, distance, early, late, groups):
    length = early.shape[0] // 2
    e_re, e_im = early[0:length], early[length:]
    l_re, l_im = late[0:length], late[length:]
    re = e_re * l_re + e_im * l_im
    im = e_re * l_im - e_im * l_re
    parts = range(early.shape[1] // groups)
    cross[distance, 0:length] += sum(re[:, p * groups : (p + 1) * groups] for p in parts)
    cross[distance, length:] += sum(im[:, p * groups : (p + 1) * groups] for p in parts)


def chip_kernel(
    tile_width,
    groups,
    margin,
    own_ref,
    other_ref,
    firsts_ref,
    forward_ref,
    spec_ref,
    cross_ref,
):
    length = forward_ref.shape[1] // 3
    width = own_ref.shape[1]
    me = lax.axis_index("seq")
    core = me % 2
    forward = forward_ref[0 : 2 * length]
    cross_ref[...] = jnp.zeros(cross_ref.shape, F32)

    def one_tile(step, carry):
        lanes = pl.ds(pl.multiple_of(step * tile_width, tile_width), tile_width)
        for ref, slot, block in ((own_ref, core, me), (other_ref, 1 - core, me ^ 1)):
            for kind in range(2):
                first = firsts_ref[block, kind, :, lanes]
                spec_ref[2 * kind + slot, :, lanes] = spectrum(
                    forward, margin, first, ref, 2 * kind * length, lanes
                )
        cross_add(cross_ref, 0, spec_ref[core, :, lanes], spec_ref[2 + core, :, lanes], groups)

        @pl.when(2 * step * tile_width // width == core)
        def _():
            cross_add(cross_ref, 1, spec_ref[0, :, lanes], spec_ref[3, :, lanes], groups)

        return carry

    lax.fori_loop(0, width // tile_width, one_tile, 0)


def filter_grad_kernel(
    blocks,
    tile_width,
    margin,
    spec_ref,
    near_ref,
    firsts_ref,
    forward_ref,
    inverse_ref,
    *refs,
):
    chips = blocks // 2
    units = refs[: chips - 1]
    gf_refs, cross = refs[chips - 1 : -1], refs[-1]
    length = forward_ref.shape[1] // 3
    groups = near_ref.shape[2]
    half = spec_ref.shape[2] // 2
    me = lax.axis_index("seq")
    core, chip = me % 2, me // 2
    forward = forward_ref[0 : 2 * length]
    cross[0:2] = near_ref[...]
    cross[2:] = jnp.zeros((blocks - 1, 2 * length, groups), F32)
    for index, unit in enumerate(units):
        other = chip ^ (index + 1)

        def one_tile(step, carry):
            start = pl.multiple_of(step * tile_width, tile_width)
            lanes = pl.ds(start, tile_width)
            kind = jnp.where(other < chip, 0, 1)
            wide_lanes = pl.ds(pl.multiple_of(kind * half + start, tile_width), tile_width)
            first = firsts_ref[2 * other + core, kind, :, wide_lanes]
            spec = spectrum(forward, margin, first, unit, 0, lanes)

            @pl.when(other < chip)
            def _():
                for slot in range(2):
                    distance = 2 * chip + slot - (2 * other + core)
                    cross_add(cross, distance, spec, spec_ref[2 + slot, :, wide_lanes], groups)

            @pl.when(other > chip)
            def _():
                for slot in range(2):
                    distance = 2 * other + core - (2 * chip + slot)
                    cross_add(cross, distance, spec_ref[slot, :, wide_lanes], spec, groups)

            return carry

        lax.fori_loop(0, half // tile_width, one_tile, 0)

    inverse = inverse_ref[0:length]
    sign = signs(length, groups)
    for place in range(blocks):
        block = me ^ place
        re = cross[block, 0:length] + sign * cross[block + 1, length:]
        im = cross[block, length:] - sign * cross[block + 1, 0:length]
        part = place // chips * 2 + place % 2
        gf_refs[part][place % chips // 2] = table_dot(inverse, jnp.concatenate([re, im], axis=0))


def signs(length, groups):
    row = lax.broadcasted_iota(jnp.int32, (length, groups), 0)
    return jnp.where(row % 2 == 0, 1.0, -1.0)


def result_kernel(blocks, tile_width, tiles, *refs):
    others = blocks // 2 - 1
    (
        rows_ref,
        taps_ref,
        filter_ref,
        conv_ref,
        conv_first,
        firsts_ref,
        after_ref,
        other_ref,
        spec_ref,
        forward_ref,
        inverse_ref,
    ) = refs[:11]
    refs = refs[11:]
    units = [refs[4 * index : 4 * index + 4] for index in range(others)]
    refs = refs[4 * others :]
    if tiles[0] == 0:
        outs, (spectra, filter_rows) = refs[:4], refs[4:6]
        refs = refs[6:]
    else:
        spectra, filter_rows = refs[:2]
        outs = refs[6:10]
        refs = refs[10:]
    acc, fix, grads, rows_out, sems = refs
    length, width = rows_ref.shape[1:]
    groups = filter_ref.shape[1]
    half = width // 2
    margin = taps_ref.shape[1] - 1
    me = lax.axis_index("seq")
    core, chip = me % 2, me // 2
    forward, inverse = forward_ref[0 : 2 * length], inverse_ref[...]

    if tiles[0] == 0:
        sign = signs(length, groups)
        for edge in (0, 1, blocks + 2):
            filter_rows[edge] = jnp.zeros((length, groups), F32)
        filter_rows[me + 2] = filter_ref[...]
        filter_rows[(me ^ 1) + 2] = get_filter(other_ref, 4 * length, length, groups)
        for index, unit in enumerate(units):
            block = me ^ (2 * (index + 1))
            filter_rows[block + 2] = get_filter(unit[1], 2 * length, length, groups)
            filter_rows[(block ^ 1) + 2] = get_filter(unit[3], 2 * length, length, groups)
        previous = None
        for distance in range(blocks):
            own = table_dot(forward, filter_rows[distance + 2])
            if previous is None:
                spectra[distance] = own
            else:
                spectra[distance, 0:length] = own[0:length] - sign * previous[length:]
                spectra[distance, length:] = own[length:] + sign * previous[0:length]
            previous = own

    def wide(values):
        return jnp.concatenate([values] * (tile_width // groups), axis=1)

    def filter_row(block, row):
        return wide(filter_rows[block + 2, pl.ds(row, 1)])

    def add_lower(distance, signal, spec, fresh=False):
        re, im = spec[0:length], spec[length:]
        h_re, h_im = wide(spectra[distance, 0:length]), wide(spectra[distance, length:])
        new_re = h_re * re - h_im * im
        new_im = h_re * im + h_im * re
        acc[0, 0:length] = new_re if fresh else acc[0, 0:length] + new_re
        acc[0, length:] = new_im if fresh else acc[0, length:] + new_im
        near = filter_row(distance + 1, 0) + filter_row(distance - 1, 0)
        far = filter_row(distance + 1, 1) + filter_row(distance - 1, 1)
        fix[0:1] += signal[0:1] * near
        fix[1:2] += signal[0:1] * far + signal[1:2] * near

    def add_upper(distance, signal, spec, fresh=False):
        re, im = spec[0:length], spec[length:]
        h_re, h_im = wide(spectra[distance, 0:length]), wide(spectra[distance, length:])
        new_re = h_re * re + h_im * im
        new_im = h_re * im - h_im * re
        acc[1, 0:length] = new_re if fresh else acc[1, 0:length] + new_re
        acc[1, length:] = new_im if fresh else acc[1, length:] + new_im
        fix[EDGE + 1 : EDGE + 2] += signal[0:1] * (
            filter_row(distance - 2, length - 1) + filter_row(distance, length - 1)
        )

    copies = []
    for count, tile in enumerate(tiles):
        start = tile * tile_width
        in_half = start // half
        lanes = slice(start, start + tile_width)
        lanes_half = slice(start % half, start % half + tile_width)
        lanes_out = slice(count * tile_width, (count + 1) * tile_width)
        weights = [taps_ref[p, :, lanes] for p in range(3)]
        fix[...] = jnp.zeros(fix.shape, F32)

        add_lower(0, firsts_ref[me, 0, :, lanes], spec_ref[core, :, lanes], True)
        add_upper(0, firsts_ref[me, 1, :, lanes], spec_ref[2 + core, :, lanes], True)

        @pl.when(core == 1)
        def _():
            add_lower(1, firsts_ref[me - 1, 0, :, lanes], spec_ref[0, :, lanes])

        @pl.when(core == 0)
        def _():
            add_upper(1, firsts_ref[me + 1, 1, :, lanes], spec_ref[3, :, lanes])

        for index, unit in enumerate(units):
            other = chip ^ (index + 1)
            for side in range(2):
                first, later = unit[2 * side : 2 * side + 2]
                body_low, body_high = (first, later) if in_half == 0 else (later, first)
                block = 2 * other + (core if side == 0 else 1 - core)

                @pl.when(other < chip)
                def _():
                    signal = firsts_ref[block, 0, :, lanes]
                    spec = spectrum(forward, margin, signal, body_low, 0, lanes_half)
                    add_lower(me - block, signal, spec)

                @pl.when(other > chip)
                def _():
                    signal = firsts_ref[block, 1, :, lanes]
                    spec = spectrum(forward, margin, signal, body_high, 0, lanes_half)
                    add_upper(block - me, signal, spec)

        after_key, after_value, after_incoming = [
            after_ref[p, :, lanes][0:margin] for p in range(3)
        ]
        gated = after_key * after_value
        zero_lag, one_lag = filter_row(0, 0), filter_row(0, 1)
        fix[0:1] += gated[0:1] * zero_lag
        fix[1:2] += gated[1:2] * zero_lag + gated[0:1] * one_lag

        long_conv = table_dot(inverse, acc[0])
        gated_grad = table_dot(inverse, acc[1])
        query_conv, key_conv, value_conv = [
            jnp.concatenate(
                [
                    with_first(margin, conv_first[p, :, lanes], conv_ref[p, 0:HEAD, lanes]),
                    conv_ref[p, HEAD:, lanes],
                ],
                axis=0,
            )
            for p in range(3)
        ]
        incoming = rows_ref[3, :, lanes].astype(F32)
        beyond = slice(length, length + margin)
        grad_edge = gated_grad[beyond] + fix[EDGE : EDGE + margin]
        grads[0, 0:length] = incoming * long_conv[0:length]
        grads[0, beyond] = after_incoming * (long_conv[beyond] + fix[0:margin])
        grads[1, 0:length] = gated_grad[0:length] * value_conv
        grads[1, beyond] = grad_edge * after_value
        grads[2, 0:length] = gated_grad[0:length] * key_conv
        grads[2, beyond] = grad_edge * after_key
        rows_out[0, :, lanes_out] = (query_conv * long_conv[0:length]).astype(BF16)
        for p in range(3):
            total = weights[p][0:1] * grads[p, 0:length]
            for shift in range(1, margin + 1):
                total = total + weights[p][shift : shift + 1] * grads[p, shift : shift + length]
            rows_out[1 + p, :, lanes_out] = total.astype(BF16)
        for p, out in enumerate(outs):
            copy = pltpu.make_async_copy(
                rows_out.at[p, :, lanes_out], out.at[:, lanes], sems.at[4 * count + p]
            )
            copy.start()
            copies.append(copy)
    for copy in copies:
        copy.wait()


def per_device(query_rows, key_rows, value_rows, short_taps, long_filter, cotangent):
    length, width = query_rows.shape
    groups = long_filter.shape[1]
    blocks = lax.axis_size("seq")
    chans = lax.axis_size("chan")
    chips, half = blocks // 2, width // 2
    margin = short_taps.shape[1] - 1
    tile_width = min(half, 256)
    bits = []
    while 2 << len(bits) < blocks:
        bits.append(2 << len(bits))
    bits.reverse()
    forward, inverse = dft_tables(length)
    shape = jax.ShapeDtypeStruct

    def swap(block, bit):
        return lax.ppermute(block, "seq", [(i, i ^ bit) for i in range(blocks)])

    def call(kernel, outs, args, scratch, in_specs=None, out_specs=None, aliases={}, cost=1):
        return list(
            pl.pallas_call(
                kernel,
                out_shape=outs,
                in_specs=in_specs or [VMEM] * len(args),
                out_specs=out_specs or [VMEM] * len(outs),
                scratch_shapes=scratch,
                input_output_aliases=aliases,
                compiler_params=pltpu.CompilerParams(vmem_limit_bytes=40 * 1024 * 1024),
                cost_estimate=pl.CostEstimate(flops=1, bytes_accessed=cost, transcendentals=0),
            )(*args)
        )

    def after(value, *others):
        return lax.optimization_barrier((value, *others))[0]

    rows, marks, short_taps, long_filter, forward, inverse = call(
        fetch_kernel,
        [
            shape((4, length, width), BF16),
            shape((HEAD, width), BF16),
            shape(short_taps.shape, F32),
            shape(long_filter.shape, F32),
            shape(forward.shape, BF16),
            shape(inverse.shape, BF16),
        ],
        [
            pltpu.with_memory_space_constraint(array, pltpu.HBM)
            for array in (
                query_rows,
                key_rows,
                value_rows,
                cotangent,
                short_taps,
                long_filter,
                forward,
                inverse,
            )
        ],
        [pltpu.VMEM((HEAD, width), F32), pltpu.SemaphoreType.DMA((8,))],
        [HBM] * 8,
    )
    all_marks = []
    for bit in bits + [1]:
        all_marks.append(swap(jnp.concatenate([marks] + all_marks, axis=0), bit))
    firsts_true, conv_first, after_rows = call(
        functools.partial(first_kernel, len(all_marks)),
        [
            shape((blocks, 2, EDGE, width), F32),
            shape((3, EDGE, width), F32),
            shape((3, EDGE, width), F32),
        ],
        [short_taps, marks, *all_marks],
        [
            pltpu.VMEM((blocks + 2, HEAD, width), F32),
            pltpu.VMEM((blocks + 1, 3, EDGE, width), F32),
            pltpu.VMEM((2 * EDGE, width), F32),
        ],
    )
    filter_rows = length * groups // width
    pair_shape = shape((4 * length + 2 * filter_rows, width), BF16)
    first_shape = shape((2 * length, half), BF16)
    later_shape = shape((2 * length + 4 * filter_rows, half), BF16)
    pair, conv, *own_units = call(
        functools.partial(own_kernel, bits, tile_width),
        [pair_shape, shape((3, length, width), F32)] + [first_shape, later_shape] * len(bits),
        [rows, short_taps, long_filter],
        [pltpu.VMEM((3, EDGE + length, tile_width), F32)],
        cost=40 * length * width,
    )

    def gather(own):
        units = {}
        for bit, block in zip(bits, own):
            arrived = {bit // 2: swap(block, bit)}
            for index, unit in units.items():
                arrived[index ^ bit // 2] = swap(unit, bit)
            units.update(arrived)
        return [units[index] for index in range(1, chips)]

    firsts = gather([after(unit, all_marks[0]) for unit in own_units[0::2]])
    sibling = swap(after(pair, all_marks[0]), 1)
    spec, near = call(
        functools.partial(chip_kernel, tile_width, groups, margin),
        [shape((4, 2 * length, width), F32), shape((2, 2 * length, groups), F32)],
        [pair, sibling, firsts_true, forward],
        [],
    )
    shares = call(
        functools.partial(filter_grad_kernel, blocks, tile_width, margin),
        [shape((blocks // 4, length, groups), F32)] * 4,
        [spec, near, firsts_true, forward, inverse, *firsts],
        [pltpu.VMEM((blocks + 1, 2 * length, groups), F32)],
    )
    laters = gather([after(unit, near) for unit in own_units[1::2]])
    share, sent = shares[0] + swap(shares[1], 1), shares[2] + swap(shares[3], 1)
    for bit in bits:
        share = after(share, *laters) + swap(sent, bit)
        if bit > 2:
            count = share.shape[0] // 2
            share, sent = share[:count], share[count:]
    units = []
    for first, later in zip(firsts, laters):
        units += [first, later, swap(after(first, share), 1), swap(after(later, share), 1)]
    rows_out = shape((length, width), BF16)
    windows = [
        shape((blocks, 2 * length, groups), F32),
        shape((blocks + 3, length, groups), F32),
    ]

    def results(tiles, extra, outs, out_specs):
        args = [rows, short_taps, long_filter, conv, conv_first, firsts_true, after_rows]
        args += [sibling, spec, forward, inverse, *units]
        count = len(args)
        return call(
            functools.partial(result_kernel, blocks, tile_width, tiles),
            outs,
            args + extra,
            [
                pltpu.VMEM((2, 2 * length, tile_width), F32),
                pltpu.VMEM((2 * EDGE, tile_width), F32),
                pltpu.VMEM((3, length + EDGE, tile_width), F32),
                pltpu.VMEM((4, length, len(tiles) * tile_width), BF16),
                pltpu.SemaphoreType.DMA((4 * len(tiles),)),
            ],
            [VMEM] * count + ([VMEM] * 2 + [HBM] * 4 if extra else []),
            out_specs,
            {count + 2 + index: index for index in range(4)} if extra else {},
            80 * length * len(tiles) * tile_width,
        )

    tiles = width // tile_width
    cuts = [0, max(1, tiles // 4), tiles - tiles // 4, tiles]
    *final, spectra, filter_blocks = results(
        range(cuts[0], cuts[1]), [], [rows_out] * 4 + windows, [HBM] * 4 + [VMEM] * 2
    )
    ready = [final]
    for begin, end in zip(cuts[1:], cuts[2:]):
        if begin < end:
            final = results(
                range(begin, end), [spectra, filter_blocks, *final], [rows_out] * 4, [HBM] * 4
            )
        ready.append(final)

    grad_filter = share[0]
    steps = [1 << index for index in range(chans.bit_length() - 1)]
    for index, step in enumerate(steps):
        arrived = lax.ppermute(grad_filter, "chan", [(i, i ^ step) for i in range(chans)])
        beside = index + len(ready) - len(steps)
        if beside >= 0:
            grad_filter = after(grad_filter, ready[beside][0])
        grad_filter = grad_filter + arrived
    return (*final, grad_filter)


def solution(mesh):
    in_specs = (
        P("seq", "chan"),
        P("seq", "chan"),
        P("seq", "chan"),
        P(None, None, "chan"),
        P("seq", None),
        P("seq", "chan"),
    )
    out_specs = (
        P("seq", "chan"),
        P("seq", "chan"),
        P("seq", "chan"),
        P("seq", "chan"),
        P("seq", None),
    )
    return jax.shard_map(
        per_device, mesh=mesh, in_specs=in_specs, out_specs=out_specs, check_vma=False
    )
```

```python
import functools

import jax
import jax.numpy as jnp
import ml_dtypes
import numpy as np
from jax import lax
from jax.experimental import pallas as pl
from jax.experimental.pallas import tpu as pltpu
from jax.sharding import PartitionSpec as P

F32 = jnp.float32
BF16 = jnp.bfloat16
EDGE = 8
HEAD = 16
VMEM = pl.BlockSpec(memory_space=pltpu.VMEM)
HBM = pl.BlockSpec(memory_space=pltpu.HBM)


def split_table(table):
    high = table.astype(ml_dtypes.bfloat16)
    low = (table - high.astype(np.float64)).astype(ml_dtypes.bfloat16)
    return high, low


def dft_tables(length):
    frequency = np.pi * (2 * np.arange(length) + 1) / (2 * length)
    into = frequency[:, None] * np.arange(length)[None, :]
    high, low = split_table(np.concatenate([np.cos(into), -np.sin(into)], axis=0))
    forward = np.concatenate([high, high, low], axis=1)
    forward = np.pad(forward, ((0, EDGE), (0, 0)))
    back = np.arange(length + EDGE)[:, None] * frequency[None, :]
    high, low = split_table(np.concatenate([np.cos(back), -np.sin(back)], axis=1) / length)
    inverse = np.concatenate([high, high, low], axis=1)
    return jnp.asarray(forward), jnp.asarray(inverse)


def halves(values):
    high = values.astype(BF16)
    return high, (values - high.astype(F32)).astype(BF16)


def table_dot(table, values):
    high, low = halves(values)
    return jnp.dot(
        table, jnp.concatenate([high, low, high], axis=0), preferred_element_type=F32
    )


def tap_sum(rows_ref, first, count, weights):
    total = weights[0:1] * rows_ref[first : first + count]
    for shift in range(1, weights.shape[0]):
        total = total + weights[shift : shift + 1] * rows_ref[first - shift : first - shift + count]
    return total


def put_filter(unit, first, filter_high, filter_low):
    length, groups = filter_high.shape
    width = unit.shape[1]
    rows = length * groups // width
    for tile in range(width // groups):
        lanes = slice(tile * groups, (tile + 1) * groups)
        part = slice(tile * rows, (tile + 1) * rows)
        unit[first : first + rows, lanes] = filter_high[part]
        unit[first + rows : first + 2 * rows, lanes] = filter_low[part]


def get_filter(unit, first, length, groups):
    width = unit.shape[1]
    rows = length * groups // width
    pieces = []
    for tile in range(width // groups):
        lanes = slice(tile * groups, (tile + 1) * groups)
        pieces.append(
            unit[first : first + rows, lanes].astype(F32)
            + unit[first + rows : first + 2 * rows, lanes].astype(F32)
        )
    return jnp.concatenate(pieces, axis=0)


def fetch_kernel(q_hbm, k_hbm, v_hbm, c_hbm, *refs):
    others = refs[:4]
    rows_ref, marks_ref, *other_refs = refs[4:10]
    edge, sems = refs[10:]
    length = q_hbm.shape[0]
    copies = [
        pltpu.make_async_copy(source, rows_ref.at[index], sems.at[index])
        for index, source in enumerate((q_hbm, k_hbm, v_hbm, c_hbm))
    ]
    copies += [
        pltpu.make_async_copy(source, target, sems.at[4 + index])
        for index, (source, target) in enumerate(zip(others, other_refs))
    ]
    for copy in copies:
        copy.start()
    for copy in copies[:4]:
        copy.wait()
    margin = others[0].shape[1] - 1
    edge[...] = jnp.zeros(edge.shape, F32)
    for p in range(4):
        first = rows_ref[p, 0:HEAD].astype(F32)
        edge[(3 + p) * margin : (4 + p) * margin] = first[0:margin]
        if p < 3:
            last = rows_ref[p, length - HEAD :].astype(F32)
            edge[p * margin : (p + 1) * margin] = last[HEAD - margin :]
    marks_ref[...] = edge[...].astype(BF16)
    for copy in copies[4:]:
        copy.wait()


def own_kernel(bits, tile_width, rows_ref, taps_ref, filter_ref, pair_ref, conv_ref, *refs):
    unit_refs, window = refs[:-1], refs[-1]
    length, width = rows_ref.shape[1:]
    half = width // 2
    me = lax.axis_index("seq")
    filter_high, filter_low = halves(filter_ref[...])
    put_filter(pair_ref, 4 * length, filter_high, filter_low)
    for later in unit_refs[1::2]:
        put_filter(later, 2 * length, filter_high, filter_low)
    window[:, 0:EDGE] = jnp.zeros((3, EDGE, tile_width), F32)
    for tile in range(width // tile_width):
        lanes = slice(tile * tile_width, (tile + 1) * tile_width)
        convs = []
        for p in range(3):
            window[p, EDGE:] = rows_ref[p, :, lanes].astype(F32)
            conv = tap_sum(window.at[p], EDGE, length, taps_ref[p, :, lanes])
            conv_ref[p, :, lanes] = conv
            convs.append(conv)
        incoming = rows_ref[3, :, lanes].astype(F32)
        parts = [*halves(convs[1] * convs[2]), *halves(incoming * convs[0])]
        for index, part in enumerate(parts):
            pair_ref[index * length : (index + 1) * length, lanes] = part
        in_half = tile * tile_width // half
        lanes_half = slice(tile * tile_width % half, tile * tile_width % half + tile_width)
        for index, bit in enumerate(bits):
            low_side = (me // bit) % 2 == 0
            first, later = unit_refs[2 * index : 2 * index + 2]
            target_low, target_high = (first, later) if in_half == 0 else (later, first)

            @pl.when(low_side)
            def _():
                target_low[0:length, lanes_half] = parts[0]
                target_low[length : 2 * length, lanes_half] = parts[1]

            @pl.when(jnp.logical_not(low_side))
            def _():
                target_high[0:length, lanes_half] = parts[2]
                target_high[length : 2 * length, lanes_half] = parts[3]


def first_kernel(marks_refs, taps_ref, own_marks, *refs):
    arrived = refs[:marks_refs]
    firsts_ref, conv_ref, after_ref, marks, convs, window = refs[marks_refs:]
    blocks = firsts_ref.shape[0]
    me = lax.axis_index("seq")
    margin = taps_ref.shape[1] - 1
    nothing = jnp.zeros(marks.shape[1:], F32)
    marks[0] = nothing
    marks[blocks + 1] = nothing
    marks[me + 1] = own_marks[...].astype(F32)
    index = 1
    for ref in arrived:
        for place in range(ref.shape[0] // HEAD):
            marks[(me ^ index_of(index, blocks)) + 1] = ref[
                place * HEAD : (place + 1) * HEAD
            ].astype(F32)
            index += 1
    window[...] = jnp.zeros(window.shape, F32)
    convs[blocks] = jnp.zeros(convs.shape[1:], F32)
    for block in range(blocks):
        for p in range(3):
            window[EDGE - margin : EDGE] = marks[block, p * margin : (p + 1) * margin]
            window[EDGE : EDGE + margin] = marks[block + 1, (3 + p) * margin : (4 + p) * margin]
            convs[block, p] = tap_sum(window, EDGE, EDGE, taps_ref[p])
        window[EDGE : EDGE + margin] = marks[block + 1, 6 * margin : 7 * margin]
        firsts_ref[block, 0] = convs[block, 1] * convs[block, 2]
        firsts_ref[block, 1] = window[EDGE:] * convs[block, 0]
    conv_ref[...] = convs[me]
    after_ref[0:2] = convs[me + 1, 1:3]
    window[EDGE : EDGE + margin] = marks[me + 2, 6 * margin : 7 * margin]
    after_ref[2] = window[EDGE:]


def index_of(count, blocks):
    order, bit = [0], blocks // 2
    while bit:
        order += [index ^ bit for index in order]
        bit //= 2
    return order[count]


def with_first(margin, first, rows):
    true = jnp.concatenate([first, jnp.zeros((HEAD - EDGE, first.shape[1]), F32)], axis=0)
    row = lax.broadcasted_iota(jnp.int32, true.shape, 0)
    return jnp.where(row < margin, true, rows)


def spectrum(forward, margin, first, ref, place, lanes):
    length = forward.shape[1] // 3
    parts = []
    for index, part in enumerate(halves(first)):
        begin = place + index * length
        head = with_first(margin, part.astype(F32), ref[begin : begin + HEAD, lanes].astype(F32))
        parts += [head.astype(BF16), ref[begin + HEAD : begin + length, lanes]]
    return jnp.dot(
        forward, jnp.concatenate([*parts, *parts[0:2]], axis=0), preferred_element_type=F32
    )


def cross_add(cross, distance, early, late, groups):
    length = early.shape[0] // 2
    e_re, e_im = early[0:length], early[length:]
    l_re, l_im = late[0:length], late[length:]
    re = e_re * l_re + e_im * l_im
    im = e_re * l_im - e_im * l_re
    parts = range(early.shape[1] // groups)
    cross[distance, 0:length] += sum(re[:, p * groups : (p + 1) * groups] for p in parts)
    cross[distance, length:] += sum(im[:, p * groups : (p + 1) * groups] for p in parts)


def chip_kernel(
    tile_width,
    groups,
    margin,
    own_ref,
    other_ref,
    firsts_ref,
    forward_ref,
    spec_ref,
    cross_ref,
):
    length = forward_ref.shape[1] // 3
    width = own_ref.shape[1]
    me = lax.axis_index("seq")
    core = me % 2
    forward = forward_ref[0 : 2 * length]
    cross_ref[...] = jnp.zeros(cross_ref.shape, F32)

    def one_tile(step, carry):
        lanes = pl.ds(pl.multiple_of(step * tile_width, tile_width), tile_width)
        for ref, slot, block in ((own_ref, core, me), (other_ref, 1 - core, me ^ 1)):
            for kind in range(2):
                first = firsts_ref[block, kind, :, lanes]
                spec_ref[2 * kind + slot, :, lanes] = spectrum(
                    forward, margin, first, ref, 2 * kind * length, lanes
                )
        cross_add(cross_ref, 0, spec_ref[core, :, lanes], spec_ref[2 + core, :, lanes], groups)

        @pl.when(2 * step * tile_width // width == core)
        def _():
            cross_add(cross_ref, 1, spec_ref[0, :, lanes], spec_ref[3, :, lanes], groups)

        return carry

    lax.fori_loop(0, width // tile_width, one_tile, 0)


def filter_grad_kernel(
    blocks,
    tile_width,
    margin,
    spec_ref,
    near_ref,
    firsts_ref,
    forward_ref,
    inverse_ref,
    *refs,
):
    chips = blocks // 2
    units = refs[: chips - 1]
    gf_refs, cross = refs[chips - 1 : -1], refs[-1]
    length = forward_ref.shape[1] // 3
    groups = near_ref.shape[2]
    half = spec_ref.shape[2] // 2
    me = lax.axis_index("seq")
    core, chip = me % 2, me // 2
    forward = forward_ref[0 : 2 * length]
    cross[0:2] = near_ref[...]
    cross[2:] = jnp.zeros((blocks - 1, 2 * length, groups), F32)
    for index, unit in enumerate(units):
        other = chip ^ (index + 1)

        def one_tile(step, carry):
            start = pl.multiple_of(step * tile_width, tile_width)
            lanes = pl.ds(start, tile_width)
            kind = jnp.where(other < chip, 0, 1)
            wide_lanes = pl.ds(pl.multiple_of(kind * half + start, tile_width), tile_width)
            first = firsts_ref[2 * other + core, kind, :, wide_lanes]
            spec = spectrum(forward, margin, first, unit, 0, lanes)

            @pl.when(other < chip)
            def _():
                for slot in range(2):
                    distance = 2 * chip + slot - (2 * other + core)
                    cross_add(cross, distance, spec, spec_ref[2 + slot, :, wide_lanes], groups)

            @pl.when(other > chip)
            def _():
                for slot in range(2):
                    distance = 2 * other + core - (2 * chip + slot)
                    cross_add(cross, distance, spec_ref[slot, :, wide_lanes], spec, groups)

            return carry

        lax.fori_loop(0, half // tile_width, one_tile, 0)

    inverse = inverse_ref[0:length]
    sign = signs(length, groups)
    for place in range(blocks):
        block = me ^ place
        re = cross[block, 0:length] + sign * cross[block + 1, length:]
        im = cross[block, length:] - sign * cross[block + 1, 0:length]
        part = place // chips * 2 + place % 2
        gf_refs[part][place % chips // 2] = table_dot(inverse, jnp.concatenate([re, im], axis=0))


def signs(length, groups):
    row = lax.broadcasted_iota(jnp.int32, (length, groups), 0)
    return jnp.where(row % 2 == 0, 1.0, -1.0)


def result_kernel(blocks, tile_width, tiles, *refs):
    others = blocks // 2 - 1
    (
        rows_ref,
        taps_ref,
        filter_ref,
        conv_ref,
        conv_first,
        firsts_ref,
        after_ref,
        other_ref,
        spec_ref,
        forward_ref,
        inverse_ref,
    ) = refs[:11]
    refs = refs[11:]
    units = [refs[4 * index : 4 * index + 4] for index in range(others)]
    refs = refs[4 * others :]
    if tiles[0] == 0:
        outs, (spectra, filter_rows) = refs[:4], refs[4:6]
        refs = refs[6:]
    else:
        spectra, filter_rows = refs[:2]
        outs = refs[6:10]
        refs = refs[10:]
    acc, fix, grads, rows_out, sems = refs
    length, width = rows_ref.shape[1:]
    groups = filter_ref.shape[1]
    half = width // 2
    margin = taps_ref.shape[1] - 1
    me = lax.axis_index("seq")
    core, chip = me % 2, me // 2
    forward, inverse = forward_ref[0 : 2 * length], inverse_ref[...]

    if tiles[0] == 0:
        sign = signs(length, groups)
        for edge in (0, 1, blocks + 2):
            filter_rows[edge] = jnp.zeros((length, groups), F32)
        filter_rows[me + 2] = filter_ref[...]
        filter_rows[(me ^ 1) + 2] = get_filter(other_ref, 4 * length, length, groups)
        for index, unit in enumerate(units):
            block = me ^ (2 * (index + 1))
            filter_rows[block + 2] = get_filter(unit[1], 2 * length, length, groups)
            filter_rows[(block ^ 1) + 2] = get_filter(unit[3], 2 * length, length, groups)
        previous = None
        for distance in range(blocks):
            own = table_dot(forward, filter_rows[distance + 2])
            if previous is None:
                spectra[distance] = own
            else:
                spectra[distance, 0:length] = own[0:length] - sign * previous[length:]
                spectra[distance, length:] = own[length:] + sign * previous[0:length]
            previous = own

    def wide(values):
        return jnp.concatenate([values] * (tile_width // groups), axis=1)

    def filter_row(block, row):
        return wide(filter_rows[block + 2, pl.ds(row, 1)])

    def add_lower(distance, signal, spec, fresh=False):
        re, im = spec[0:length], spec[length:]
        h_re, h_im = wide(spectra[distance, 0:length]), wide(spectra[distance, length:])
        new_re = h_re * re - h_im * im
        new_im = h_re * im + h_im * re
        acc[0, 0:length] = new_re if fresh else acc[0, 0:length] + new_re
        acc[0, length:] = new_im if fresh else acc[0, length:] + new_im
        near = filter_row(distance + 1, 0) + filter_row(distance - 1, 0)
        far = filter_row(distance + 1, 1) + filter_row(distance - 1, 1)
        fix[0:1] += signal[0:1] * near
        fix[1:2] += signal[0:1] * far + signal[1:2] * near

    def add_upper(distance, signal, spec, fresh=False):
        re, im = spec[0:length], spec[length:]
        h_re, h_im = wide(spectra[distance, 0:length]), wide(spectra[distance, length:])
        new_re = h_re * re + h_im * im
        new_im = h_re * im - h_im * re
        acc[1, 0:length] = new_re if fresh else acc[1, 0:length] + new_re
        acc[1, length:] = new_im if fresh else acc[1, length:] + new_im
        fix[EDGE + 1 : EDGE + 2] += signal[0:1] * (
            filter_row(distance - 2, length - 1) + filter_row(distance, length - 1)
        )

    copies = []
    for count, tile in enumerate(tiles):
        start = tile * tile_width
        in_half = start // half
        lanes = slice(start, start + tile_width)
        lanes_half = slice(start % half, start % half + tile_width)
        lanes_out = slice(count * tile_width, (count + 1) * tile_width)
        weights = [taps_ref[p, :, lanes] for p in range(3)]
        fix[...] = jnp.zeros(fix.shape, F32)

        add_lower(0, firsts_ref[me, 0, :, lanes], spec_ref[core, :, lanes], True)
        add_upper(0, firsts_ref[me, 1, :, lanes], spec_ref[2 + core, :, lanes], True)

        @pl.when(core == 1)
        def _():
            add_lower(1, firsts_ref[me - 1, 0, :, lanes], spec_ref[0, :, lanes])

        @pl.when(core == 0)
        def _():
            add_upper(1, firsts_ref[me + 1, 1, :, lanes], spec_ref[3, :, lanes])

        for index, unit in enumerate(units):
            other = chip ^ (index + 1)
            for side in range(2):
                first, later = unit[2 * side : 2 * side + 2]
                body_low, body_high = (first, later) if in_half == 0 else (later, first)
                block = 2 * other + (core if side == 0 else 1 - core)

                @pl.when(other < chip)
                def _():
                    signal = firsts_ref[block, 0, :, lanes]
                    spec = spectrum(forward, margin, signal, body_low, 0, lanes_half)
                    add_lower(me - block, signal, spec)

                @pl.when(other > chip)
                def _():
                    signal = firsts_ref[block, 1, :, lanes]
                    spec = spectrum(forward, margin, signal, body_high, 0, lanes_half)
                    add_upper(block - me, signal, spec)

        after_key, after_value, after_incoming = [
            after_ref[p, :, lanes][0:margin] for p in range(3)
        ]
        gated = after_key * after_value
        zero_lag, one_lag = filter_row(0, 0), filter_row(0, 1)
        fix[0:1] += gated[0:1] * zero_lag
        fix[1:2] += gated[1:2] * zero_lag + gated[0:1] * one_lag

        long_conv = table_dot(inverse, acc[0])
        gated_grad = table_dot(inverse, acc[1])
        query_conv, key_conv, value_conv = [
            jnp.concatenate(
                [
                    with_first(margin, conv_first[p, :, lanes], conv_ref[p, 0:HEAD, lanes]),
                    conv_ref[p, HEAD:, lanes],
                ],
                axis=0,
            )
            for p in range(3)
        ]
        incoming = rows_ref[3, :, lanes].astype(F32)
        beyond = slice(length, length + margin)
        grad_edge = gated_grad[beyond] + fix[EDGE : EDGE + margin]
        grads[0, 0:length] = incoming * long_conv[0:length]
        grads[0, beyond] = after_incoming * (long_conv[beyond] + fix[0:margin])
        grads[1, 0:length] = gated_grad[0:length] * value_conv
        grads[1, beyond] = grad_edge * after_value
        grads[2, 0:length] = gated_grad[0:length] * key_conv
        grads[2, beyond] = grad_edge * after_key
        rows_out[0, :, lanes_out] = (query_conv * long_conv[0:length]).astype(BF16)
        for p in range(3):
            total = weights[p][0:1] * grads[p, 0:length]
            for shift in range(1, margin + 1):
                total = total + weights[p][shift : shift + 1] * grads[p, shift : shift + length]
            rows_out[1 + p, :, lanes_out] = total.astype(BF16)
        for p, out in enumerate(outs):
            copy = pltpu.make_async_copy(
                rows_out.at[p, :, lanes_out], out.at[:, lanes], sems.at[4 * count + p]
            )
            copy.start()
            copies.append(copy)
    for copy in copies:
        copy.wait()


def per_device(query_rows, key_rows, value_rows, short_taps, long_filter, cotangent):
    length, width = query_rows.shape
    groups = long_filter.shape[1]
    blocks = lax.axis_size("seq")
    chans = lax.axis_size("chan")
    chips, half = blocks // 2, width // 2
    margin = short_taps.shape[1] - 1
    tile_width = min(half, 256)
    bits = []
    while 2 << len(bits) < blocks:
        bits.append(2 << len(bits))
    bits.reverse()
    forward, inverse = dft_tables(length)
    shape = jax.ShapeDtypeStruct

    def swap(block, bit):
        return lax.ppermute(block, "seq", [(i, i ^ bit) for i in range(blocks)])

    def call(kernel, outs, args, scratch, in_specs=None, out_specs=None, aliases={}, cost=1):
        return list(
            pl.pallas_call(
                kernel,
                out_shape=outs,
                in_specs=in_specs or [VMEM] * len(args),
                out_specs=out_specs or [VMEM] * len(outs),
                scratch_shapes=scratch,
                input_output_aliases=aliases,
                compiler_params=pltpu.CompilerParams(vmem_limit_bytes=40 * 1024 * 1024),
                cost_estimate=pl.CostEstimate(flops=1, bytes_accessed=cost, transcendentals=0),
            )(*args)
        )

    def after(value, *others):
        return lax.optimization_barrier((value, *others))[0]

    rows, marks, short_taps, long_filter, forward, inverse = call(
        fetch_kernel,
        [
            shape((4, length, width), BF16),
            shape((HEAD, width), BF16),
            shape(short_taps.shape, F32),
            shape(long_filter.shape, F32),
            shape(forward.shape, BF16),
            shape(inverse.shape, BF16),
        ],
        [
            pltpu.with_memory_space_constraint(array, pltpu.HBM)
            for array in (
                query_rows,
                key_rows,
                value_rows,
                cotangent,
                short_taps,
                long_filter,
                forward,
                inverse,
            )
        ],
        [pltpu.VMEM((HEAD, width), F32), pltpu.SemaphoreType.DMA((8,))],
        [HBM] * 8,
    )
    all_marks = []
    for bit in bits + [1]:
        all_marks.append(swap(jnp.concatenate([marks] + all_marks, axis=0), bit))
    firsts_true, conv_first, after_rows = call(
        functools.partial(first_kernel, len(all_marks)),
        [
            shape((blocks, 2, EDGE, width), F32),
            shape((3, EDGE, width), F32),
            shape((3, EDGE, width), F32),
        ],
        [short_taps, marks, *all_marks],
        [
            pltpu.VMEM((blocks + 2, HEAD, width), F32),
            pltpu.VMEM((blocks + 1, 3, EDGE, width), F32),
            pltpu.VMEM((2 * EDGE, width), F32),
        ],
        cost=32 * length * width,
    )
    filter_rows = length * groups // width
    pair_shape = shape((4 * length + 2 * filter_rows, width), BF16)
    first_shape = shape((2 * length, half), BF16)
    later_shape = shape((2 * length + 4 * filter_rows, half), BF16)
    pair, conv, *own_units = call(
        functools.partial(own_kernel, bits, tile_width),
        [pair_shape, shape((3, length, width), F32)] + [first_shape, later_shape] * len(bits),
        [rows, short_taps, long_filter],
        [pltpu.VMEM((3, EDGE + length, tile_width), F32)],
        cost=40 * length * width,
    )

    def gather(own):
        units = {}
        for bit, block in zip(bits, own):
            arrived = {bit // 2: swap(block, bit)}
            for index, unit in units.items():
                arrived[index ^ bit // 2] = swap(unit, bit)
            units.update(arrived)
        return [units[index] for index in range(1, chips)]

    firsts = gather(own_units[0::2])
    sibling = swap(pair, 1)
    spec, near = call(
        functools.partial(chip_kernel, tile_width, groups, margin),
        [shape((4, 2 * length, width), F32), shape((2, 2 * length, groups), F32)],
        [after(pair, *firsts), sibling, firsts_true, forward],
        [],
    )
    shares = call(
        functools.partial(filter_grad_kernel, blocks, tile_width, margin),
        [shape((blocks // 4, length, groups), F32)] * 4,
        [spec, near, firsts_true, forward, inverse, *firsts],
        [pltpu.VMEM((blocks + 1, 2 * length, groups), F32)],
    )
    laters = gather([after(unit, firsts_true) for unit in own_units[1::2]])
    share, sent = shares[0] + swap(shares[1], 1), shares[2] + swap(shares[3], 1)
    for bit in bits:
        share = after(share, *laters) + swap(sent, bit)
        if bit > 2:
            count = share.shape[0] // 2
            share, sent = share[:count], share[count:]
    units = []
    for first, later in zip(firsts, laters):
        units += [first, later, swap(after(first, share), 1), swap(after(later, share), 1)]
    rows_out = shape((length, width), BF16)
    windows = [
        shape((blocks, 2 * length, groups), F32),
        shape((blocks + 3, length, groups), F32),
    ]

    def results(tiles, extra, outs, out_specs):
        args = [rows, short_taps, long_filter, conv, conv_first, firsts_true, after_rows]
        args += [sibling, spec, forward, inverse, *units]
        count = len(args)
        return call(
            functools.partial(result_kernel, blocks, tile_width, tiles),
            outs,
            args + extra,
            [
                pltpu.VMEM((2, 2 * length, tile_width), F32),
                pltpu.VMEM((2 * EDGE, tile_width), F32),
                pltpu.VMEM((3, length + EDGE, tile_width), F32),
                pltpu.VMEM((4, length, len(tiles) * tile_width), BF16),
                pltpu.SemaphoreType.DMA((4 * len(tiles),)),
            ],
            [VMEM] * count + ([VMEM] * 2 + [HBM] * 4 if extra else []),
            out_specs,
            {count + 2 + index: index for index in range(4)} if extra else {},
            80 * length * len(tiles) * tile_width,
        )

    tiles = width // tile_width
    cuts = [0, max(1, tiles // 4), tiles - tiles // 4, tiles]
    *final, spectra, filter_blocks = results(
        range(cuts[0], cuts[1]), [], [rows_out] * 4 + windows, [HBM] * 4 + [VMEM] * 2
    )
    ready = [final]
    for begin, end in zip(cuts[1:], cuts[2:]):
        if begin < end:
            final = results(
                range(begin, end), [spectra, filter_blocks, *final], [rows_out] * 4, [HBM] * 4
            )
        ready.append(final)

    grad_filter = share[0]
    steps = [1 << index for index in range(chans.bit_length() - 1)]
    for index, step in enumerate(steps):
        arrived = lax.ppermute(grad_filter, "chan", [(i, i ^ step) for i in range(chans)])
        beside = index + len(ready) - len(steps)
        if beside >= 0:
            grad_filter = after(grad_filter, ready[beside][0])
        grad_filter = grad_filter + arrived
    return (*final, grad_filter)


def solution(mesh):
    in_specs = (
        P("seq", "chan"),
        P("seq", "chan"),
        P("seq", "chan"),
        P(None, None, "chan"),
        P("seq", None),
        P("seq", "chan"),
    )
    out_specs = (
        P("seq", "chan"),
        P("seq", "chan"),
        P("seq", "chan"),
        P("seq", "chan"),
        P("seq", None),
    )
    return jax.shard_map(
        per_device, mesh=mesh, in_specs=in_specs, out_specs=out_specs, check_vma=False
    )
```

```python
import functools

import jax
import jax.numpy as jnp
import ml_dtypes
import numpy as np
from jax import lax
from jax.experimental import pallas as pl
from jax.experimental.pallas import tpu as pltpu
from jax.sharding import PartitionSpec as P

F32 = jnp.float32
BF16 = jnp.bfloat16
EDGE = 8
HEAD = 16
VMEM = pl.BlockSpec(memory_space=pltpu.VMEM)
HBM = pl.BlockSpec(memory_space=pltpu.HBM)


def split_table(table):
    high = table.astype(ml_dtypes.bfloat16)
    low = (table - high.astype(np.float64)).astype(ml_dtypes.bfloat16)
    return high, low


def dft_tables(length):
    frequency = np.pi * (2 * np.arange(length) + 1) / (2 * length)
    into = frequency[:, None] * np.arange(length)[None, :]
    high, low = split_table(np.concatenate([np.cos(into), -np.sin(into)], axis=0))
    forward = np.concatenate([high, high, low], axis=1)
    forward = np.pad(forward, ((0, EDGE), (0, 0)))
    back = np.arange(length + EDGE)[:, None] * frequency[None, :]
    high, low = split_table(np.concatenate([np.cos(back), -np.sin(back)], axis=1) / length)
    inverse = np.concatenate([high, high, low], axis=1)
    return jnp.asarray(forward), jnp.asarray(inverse)


def halves(values):
    high = values.astype(BF16)
    return high, (values - high.astype(F32)).astype(BF16)


def table_dot(table, values):
    high, low = halves(values)
    return jnp.dot(
        table, jnp.concatenate([high, low, high], axis=0), preferred_element_type=F32
    )


def tap_sum(rows_ref, first, count, weights):
    total = weights[0:1] * rows_ref[first : first + count]
    for shift in range(1, weights.shape[0]):
        total = total + weights[shift : shift + 1] * rows_ref[first - shift : first - shift + count]
    return total


def put_filter(unit, first, filter_high, filter_low):
    length, groups = filter_high.shape
    width = unit.shape[1]
    rows = length * groups // width
    for tile in range(width // groups):
        lanes = slice(tile * groups, (tile + 1) * groups)
        part = slice(tile * rows, (tile + 1) * rows)
        unit[first : first + rows, lanes] = filter_high[part]
        unit[first + rows : first + 2 * rows, lanes] = filter_low[part]


def get_filter(unit, first, length, groups):
    width = unit.shape[1]
    rows = length * groups // width
    pieces = []
    for tile in range(width // groups):
        lanes = slice(tile * groups, (tile + 1) * groups)
        pieces.append(
            unit[first : first + rows, lanes].astype(F32)
            + unit[first + rows : first + 2 * rows, lanes].astype(F32)
        )
    return jnp.concatenate(pieces, axis=0)


def fetch_kernel(q_hbm, k_hbm, v_hbm, c_hbm, *refs):
    others = refs[:4]
    rows_ref, marks_ref, *other_refs = refs[4:10]
    edge, sems = refs[10:]
    length = q_hbm.shape[0]
    copies = [
        pltpu.make_async_copy(source, rows_ref.at[index], sems.at[index])
        for index, source in enumerate((q_hbm, k_hbm, v_hbm, c_hbm))
    ]
    copies += [
        pltpu.make_async_copy(source, target, sems.at[4 + index])
        for index, (source, target) in enumerate(zip(others, other_refs))
    ]
    for copy in copies:
        copy.start()
    for copy in copies[:4]:
        copy.wait()
    margin = others[0].shape[1] - 1
    edge[...] = jnp.zeros(edge.shape, F32)
    for p in range(4):
        first = rows_ref[p, 0:HEAD].astype(F32)
        edge[(3 + p) * margin : (4 + p) * margin] = first[0:margin]
        if p < 3:
            last = rows_ref[p, length - HEAD :].astype(F32)
            edge[p * margin : (p + 1) * margin] = last[HEAD - margin :]
    marks_ref[...] = edge[...].astype(BF16)
    for copy in copies[4:]:
        copy.wait()


def own_kernel(bits, tile_width, rows_ref, taps_ref, filter_ref, pair_ref, conv_ref, *refs):
    unit_refs, window = refs[:-1], refs[-1]
    length, width = rows_ref.shape[1:]
    half = width // 2
    me = lax.axis_index("seq")
    filter_high, filter_low = halves(filter_ref[...])
    put_filter(pair_ref, 4 * length, filter_high, filter_low)
    for later in unit_refs[1::2]:
        put_filter(later, 2 * length, filter_high, filter_low)
    window[:, 0:EDGE] = jnp.zeros((3, EDGE, tile_width), F32)
    for tile in range(width // tile_width):
        lanes = slice(tile * tile_width, (tile + 1) * tile_width)
        convs = []
        for p in range(3):
            window[p, EDGE:] = rows_ref[p, :, lanes].astype(F32)
            conv = tap_sum(window.at[p], EDGE, length, taps_ref[p, :, lanes])
            conv_ref[p, :, lanes] = conv
            convs.append(conv)
        incoming = rows_ref[3, :, lanes].astype(F32)
        parts = [*halves(convs[1] * convs[2]), *halves(incoming * convs[0])]
        for index, part in enumerate(parts):
            pair_ref[index * length : (index + 1) * length, lanes] = part
        in_half = tile * tile_width // half
        lanes_half = slice(tile * tile_width % half, tile * tile_width % half + tile_width)
        for index, bit in enumerate(bits):
            low_side = (me // bit) % 2 == 0
            first, later = unit_refs[2 * index : 2 * index + 2]
            target_low, target_high = (first, later) if in_half == 0 else (later, first)

            @pl.when(low_side)
            def _():
                target_low[0:length, lanes_half] = parts[0]
                target_low[length : 2 * length, lanes_half] = parts[1]

            @pl.when(jnp.logical_not(low_side))
            def _():
                target_high[0:length, lanes_half] = parts[2]
                target_high[length : 2 * length, lanes_half] = parts[3]


def first_kernel(marks_refs, taps_ref, own_marks, *refs):
    arrived = refs[:marks_refs]
    firsts_ref, conv_ref, after_ref, marks, convs, window = refs[marks_refs:]
    blocks = firsts_ref.shape[0]
    me = lax.axis_index("seq")
    margin = taps_ref.shape[1] - 1
    nothing = jnp.zeros(marks.shape[1:], F32)
    marks[0] = nothing
    marks[blocks + 1] = nothing
    marks[me + 1] = own_marks[...].astype(F32)
    index = 1
    for ref in arrived:
        for place in range(ref.shape[0] // HEAD):
            marks[(me ^ index_of(index, blocks)) + 1] = ref[
                place * HEAD : (place + 1) * HEAD
            ].astype(F32)
            index += 1
    window[...] = jnp.zeros(window.shape, F32)
    convs[blocks] = jnp.zeros(convs.shape[1:], F32)
    for block in range(blocks):
        for p in range(3):
            window[EDGE - margin : EDGE] = marks[block, p * margin : (p + 1) * margin]
            window[EDGE : EDGE + margin] = marks[block + 1, (3 + p) * margin : (4 + p) * margin]
            convs[block, p] = tap_sum(window, EDGE, EDGE, taps_ref[p])
        window[EDGE : EDGE + margin] = marks[block + 1, 6 * margin : 7 * margin]
        firsts_ref[block, 0] = convs[block, 1] * convs[block, 2]
        firsts_ref[block, 1] = window[EDGE:] * convs[block, 0]
    conv_ref[...] = convs[me]
    after_ref[0:2] = convs[me + 1, 1:3]
    window[EDGE : EDGE + margin] = marks[me + 2, 6 * margin : 7 * margin]
    after_ref[2] = window[EDGE:]


def index_of(count, blocks):
    order, bit = [0], blocks // 2
    while bit:
        order += [index ^ bit for index in order]
        bit //= 2
    return order[count]


def with_first(margin, first, rows):
    true = jnp.concatenate([first, jnp.zeros((HEAD - EDGE, first.shape[1]), F32)], axis=0)
    row = lax.broadcasted_iota(jnp.int32, true.shape, 0)
    return jnp.where(row < margin, true, rows)


def spectrum(forward, margin, first, ref, place, lanes):
    length = forward.shape[1] // 3
    parts = []
    for index, part in enumerate(halves(first)):
        begin = place + index * length
        head = with_first(margin, part.astype(F32), ref[begin : begin + HEAD, lanes].astype(F32))
        parts += [head.astype(BF16), ref[begin + HEAD : begin + length, lanes]]
    return jnp.dot(
        forward, jnp.concatenate([*parts, *parts[0:2]], axis=0), preferred_element_type=F32
    )


def cross_add(cross, distance, early, late, groups):
    length = early.shape[0] // 2
    e_re, e_im = early[0:length], early[length:]
    l_re, l_im = late[0:length], late[length:]
    re = e_re * l_re + e_im * l_im
    im = e_re * l_im - e_im * l_re
    parts = range(early.shape[1] // groups)
    cross[distance, 0:length] += sum(re[:, p * groups : (p + 1) * groups] for p in parts)
    cross[distance, length:] += sum(im[:, p * groups : (p + 1) * groups] for p in parts)


def chip_kernel(
    tile_width,
    groups,
    margin,
    own_ref,
    other_ref,
    firsts_ref,
    forward_ref,
    spec_ref,
    cross_ref,
):
    length = forward_ref.shape[1] // 3
    width = own_ref.shape[1]
    me = lax.axis_index("seq")
    core = me % 2
    forward = forward_ref[0 : 2 * length]
    cross_ref[...] = jnp.zeros(cross_ref.shape, F32)

    def one_tile(step, carry):
        lanes = pl.ds(pl.multiple_of(step * tile_width, tile_width), tile_width)
        for ref, slot, block in ((own_ref, core, me), (other_ref, 1 - core, me ^ 1)):
            for kind in range(2):
                first = firsts_ref[block, kind, :, lanes]
                spec_ref[2 * kind + slot, :, lanes] = spectrum(
                    forward, margin, first, ref, 2 * kind * length, lanes
                )
        cross_add(cross_ref, 0, spec_ref[core, :, lanes], spec_ref[2 + core, :, lanes], groups)

        @pl.when(2 * step * tile_width // width == core)
        def _():
            cross_add(cross_ref, 1, spec_ref[0, :, lanes], spec_ref[3, :, lanes], groups)

        return carry

    lax.fori_loop(0, width // tile_width, one_tile, 0)


def unit_kernel(tile_width, margin, firsts_ref, forward_ref, *refs):
    others = len(refs) // 2
    length = forward_ref.shape[1] // 3
    half = refs[0].shape[1]
    me = lax.axis_index("seq")
    core, chip = me % 2, me // 2
    forward = forward_ref[0 : 2 * length]
    for index, (unit, spec_ref) in enumerate(zip(refs[:others], refs[others:])):
        other = chip ^ (index + 1)
        kind = jnp.where(other < chip, 0, 1)
        for tile in range(half // tile_width):
            start = tile * tile_width
            lanes = slice(start, start + tile_width)
            wide_lanes = pl.ds(pl.multiple_of(kind * half + start, tile_width), tile_width)
            first = firsts_ref[2 * other + core, kind, :, wide_lanes]
            spec_ref[:, lanes] = spectrum(forward, margin, first, unit, 0, lanes)


def filter_grad_kernel(
    blocks,
    tile_width,
    spec_ref,
    near_ref,
    forward_ref,
    inverse_ref,
    *refs,
):
    chips = blocks // 2
    units = refs[: chips - 1]
    gf_refs, cross = refs[chips - 1 : -1], refs[-1]
    length = forward_ref.shape[1] // 3
    groups = near_ref.shape[2]
    half = spec_ref.shape[2] // 2
    me = lax.axis_index("seq")
    core, chip = me % 2, me // 2
    cross[0:2] = near_ref[...]
    cross[2:] = jnp.zeros((blocks - 1, 2 * length, groups), F32)
    for index, unit in enumerate(units):
        other = chip ^ (index + 1)

        def one_tile(step, carry):
            start = pl.multiple_of(step * tile_width, tile_width)
            lanes = pl.ds(start, tile_width)
            kind = jnp.where(other < chip, 0, 1)
            wide_lanes = pl.ds(pl.multiple_of(kind * half + start, tile_width), tile_width)
            spec = unit[:, lanes]

            @pl.when(other < chip)
            def _():
                for slot in range(2):
                    distance = 2 * chip + slot - (2 * other + core)
                    cross_add(cross, distance, spec, spec_ref[2 + slot, :, wide_lanes], groups)

            @pl.when(other > chip)
            def _():
                for slot in range(2):
                    distance = 2 * other + core - (2 * chip + slot)
                    cross_add(cross, distance, spec_ref[slot, :, wide_lanes], spec, groups)

            return carry

        lax.fori_loop(0, half // tile_width, one_tile, 0)

    inverse = inverse_ref[0:length]
    sign = signs(length, groups)
    for place in range(blocks):
        block = me ^ place
        re = cross[block, 0:length] + sign * cross[block + 1, length:]
        im = cross[block, length:] - sign * cross[block + 1, 0:length]
        part = place // chips * 2 + place % 2
        gf_refs[part][place % chips // 2] = table_dot(inverse, jnp.concatenate([re, im], axis=0))


def signs(length, groups):
    row = lax.broadcasted_iota(jnp.int32, (length, groups), 0)
    return jnp.where(row % 2 == 0, 1.0, -1.0)


def result_kernel(blocks, tile_width, tiles, *refs):
    others = blocks // 2 - 1
    (
        rows_ref,
        taps_ref,
        filter_ref,
        conv_ref,
        conv_first,
        firsts_ref,
        after_ref,
        other_ref,
        spec_ref,
        forward_ref,
        inverse_ref,
    ) = refs[:11]
    refs = refs[11:]
    units = [refs[4 * index : 4 * index + 4] for index in range(others)]
    refs = refs[4 * others :]
    if tiles[0] == 0:
        outs, (spectra, filter_rows) = refs[:4], refs[4:6]
        refs = refs[6:]
    else:
        spectra, filter_rows = refs[:2]
        outs = refs[6:10]
        refs = refs[10:]
    acc, fix, grads, rows_out, sems = refs
    length, width = rows_ref.shape[1:]
    groups = filter_ref.shape[1]
    half = width // 2
    margin = taps_ref.shape[1] - 1
    me = lax.axis_index("seq")
    core, chip = me % 2, me // 2
    forward, inverse = forward_ref[0 : 2 * length], inverse_ref[...]

    if tiles[0] == 0:
        sign = signs(length, groups)
        for edge in (0, 1, blocks + 2):
            filter_rows[edge] = jnp.zeros((length, groups), F32)
        filter_rows[me + 2] = filter_ref[...]
        filter_rows[(me ^ 1) + 2] = get_filter(other_ref, 4 * length, length, groups)
        for index, unit in enumerate(units):
            block = me ^ (2 * (index + 1))
            filter_rows[block + 2] = get_filter(unit[1], 2 * length, length, groups)
            filter_rows[(block ^ 1) + 2] = get_filter(unit[3], 2 * length, length, groups)
        previous = None
        for distance in range(blocks):
            own = table_dot(forward, filter_rows[distance + 2])
            if previous is None:
                spectra[distance] = own
            else:
                spectra[distance, 0:length] = own[0:length] - sign * previous[length:]
                spectra[distance, length:] = own[length:] + sign * previous[0:length]
            previous = own

    def wide(values):
        return jnp.concatenate([values] * (tile_width // groups), axis=1)

    def filter_row(block, row):
        return wide(filter_rows[block + 2, pl.ds(row, 1)])

    def add_lower(distance, signal, spec, fresh=False):
        re, im = spec[0:length], spec[length:]
        h_re, h_im = wide(spectra[distance, 0:length]), wide(spectra[distance, length:])
        new_re = h_re * re - h_im * im
        new_im = h_re * im + h_im * re
        acc[0, 0:length] = new_re if fresh else acc[0, 0:length] + new_re
        acc[0, length:] = new_im if fresh else acc[0, length:] + new_im
        near = filter_row(distance + 1, 0) + filter_row(distance - 1, 0)
        far = filter_row(distance + 1, 1) + filter_row(distance - 1, 1)
        fix[0:1] += signal[0:1] * near
        fix[1:2] += signal[0:1] * far + signal[1:2] * near

    def add_upper(distance, signal, spec, fresh=False):
        re, im = spec[0:length], spec[length:]
        h_re, h_im = wide(spectra[distance, 0:length]), wide(spectra[distance, length:])
        new_re = h_re * re + h_im * im
        new_im = h_re * im - h_im * re
        acc[1, 0:length] = new_re if fresh else acc[1, 0:length] + new_re
        acc[1, length:] = new_im if fresh else acc[1, length:] + new_im
        fix[EDGE + 1 : EDGE + 2] += signal[0:1] * (
            filter_row(distance - 2, length - 1) + filter_row(distance, length - 1)
        )

    copies = []
    for count, tile in enumerate(tiles):
        start = tile * tile_width
        in_half = start // half
        lanes = slice(start, start + tile_width)
        lanes_half = slice(start % half, start % half + tile_width)
        lanes_out = slice(count * tile_width, (count + 1) * tile_width)
        weights = [taps_ref[p, :, lanes] for p in range(3)]
        fix[...] = jnp.zeros(fix.shape, F32)

        add_lower(0, firsts_ref[me, 0, :, lanes], spec_ref[core, :, lanes], True)
        add_upper(0, firsts_ref[me, 1, :, lanes], spec_ref[2 + core, :, lanes], True)

        @pl.when(core == 1)
        def _():
            add_lower(1, firsts_ref[me - 1, 0, :, lanes], spec_ref[0, :, lanes])

        @pl.when(core == 0)
        def _():
            add_upper(1, firsts_ref[me + 1, 1, :, lanes], spec_ref[3, :, lanes])

        for index, unit in enumerate(units):
            other = chip ^ (index + 1)
            for side in range(2):
                first, later = unit[2 * side : 2 * side + 2]
                body_low, body_high = (first, later) if in_half == 0 else (later, first)
                block = 2 * other + (core if side == 0 else 1 - core)

                @pl.when(other < chip)
                def _():
                    signal = firsts_ref[block, 0, :, lanes]
                    spec = spectrum(forward, margin, signal, body_low, 0, lanes_half)
                    add_lower(me - block, signal, spec)

                @pl.when(other > chip)
                def _():
                    signal = firsts_ref[block, 1, :, lanes]
                    spec = spectrum(forward, margin, signal, body_high, 0, lanes_half)
                    add_upper(block - me, signal, spec)

        after_key, after_value, after_incoming = [
            after_ref[p, :, lanes][0:margin] for p in range(3)
        ]
        gated = after_key * after_value
        zero_lag, one_lag = filter_row(0, 0), filter_row(0, 1)
        fix[0:1] += gated[0:1] * zero_lag
        fix[1:2] += gated[1:2] * zero_lag + gated[0:1] * one_lag

        long_conv = table_dot(inverse, acc[0])
        gated_grad = table_dot(inverse, acc[1])
        query_conv, key_conv, value_conv = [
            jnp.concatenate(
                [
                    with_first(margin, conv_first[p, :, lanes], conv_ref[p, 0:HEAD, lanes]),
                    conv_ref[p, HEAD:, lanes],
                ],
                axis=0,
            )
            for p in range(3)
        ]
        incoming = rows_ref[3, :, lanes].astype(F32)
        beyond = slice(length, length + margin)
        grad_edge = gated_grad[beyond] + fix[EDGE : EDGE + margin]
        grads[0, 0:length] = incoming * long_conv[0:length]
        grads[0, beyond] = after_incoming * (long_conv[beyond] + fix[0:margin])
        grads[1, 0:length] = gated_grad[0:length] * value_conv
        grads[1, beyond] = grad_edge * after_value
        grads[2, 0:length] = gated_grad[0:length] * key_conv
        grads[2, beyond] = grad_edge * after_key
        rows_out[0, :, lanes_out] = (query_conv * long_conv[0:length]).astype(BF16)
        for p in range(3):
            total = weights[p][0:1] * grads[p, 0:length]
            for shift in range(1, margin + 1):
                total = total + weights[p][shift : shift + 1] * grads[p, shift : shift + length]
            rows_out[1 + p, :, lanes_out] = total.astype(BF16)
        for p, out in enumerate(outs):
            copy = pltpu.make_async_copy(
                rows_out.at[p, :, lanes_out], out.at[:, lanes], sems.at[4 * count + p]
            )
            copy.start()
            copies.append(copy)
    for copy in copies:
        copy.wait()


def per_device(query_rows, key_rows, value_rows, short_taps, long_filter, cotangent):
    length, width = query_rows.shape
    groups = long_filter.shape[1]
    blocks = lax.axis_size("seq")
    chans = lax.axis_size("chan")
    chips, half = blocks // 2, width // 2
    margin = short_taps.shape[1] - 1
    tile_width = min(half, 256)
    bits = []
    while 2 << len(bits) < blocks:
        bits.append(2 << len(bits))
    bits.reverse()
    forward, inverse = dft_tables(length)
    shape = jax.ShapeDtypeStruct

    def swap(block, bit):
        return lax.ppermute(block, "seq", [(i, i ^ bit) for i in range(blocks)])

    def call(kernel, outs, args, scratch, in_specs=None, out_specs=None, aliases={}, cost=1):
        return list(
            pl.pallas_call(
                kernel,
                out_shape=outs,
                in_specs=in_specs or [VMEM] * len(args),
                out_specs=out_specs or [VMEM] * len(outs),
                scratch_shapes=scratch,
                input_output_aliases=aliases,
                compiler_params=pltpu.CompilerParams(vmem_limit_bytes=40 * 1024 * 1024),
                cost_estimate=pl.CostEstimate(flops=1, bytes_accessed=cost, transcendentals=0),
            )(*args)
        )

    def after(value, *others):
        return lax.optimization_barrier((value, *others))[0]

    rows, marks, short_taps, long_filter, forward, inverse = call(
        fetch_kernel,
        [
            shape((4, length, width), BF16),
            shape((HEAD, width), BF16),
            shape(short_taps.shape, F32),
            shape(long_filter.shape, F32),
            shape(forward.shape, BF16),
            shape(inverse.shape, BF16),
        ],
        [
            pltpu.with_memory_space_constraint(array, pltpu.HBM)
            for array in (
                query_rows,
                key_rows,
                value_rows,
                cotangent,
                short_taps,
                long_filter,
                forward,
                inverse,
            )
        ],
        [pltpu.VMEM((HEAD, width), F32), pltpu.SemaphoreType.DMA((8,))],
        [HBM] * 8,
    )
    all_marks = []
    for bit in bits + [1]:
        all_marks.append(swap(jnp.concatenate([marks] + all_marks, axis=0), bit))
    firsts_true, conv_first, after_rows = call(
        functools.partial(first_kernel, len(all_marks)),
        [
            shape((blocks, 2, EDGE, width), F32),
            shape((3, EDGE, width), F32),
            shape((3, EDGE, width), F32),
        ],
        [short_taps, marks, *all_marks],
        [
            pltpu.VMEM((blocks + 2, HEAD, width), F32),
            pltpu.VMEM((blocks + 1, 3, EDGE, width), F32),
            pltpu.VMEM((2 * EDGE, width), F32),
        ],
        cost=32 * length * width,
    )
    filter_rows = length * groups // width
    pair_shape = shape((4 * length + 2 * filter_rows, width), BF16)
    first_shape = shape((2 * length, half), BF16)
    later_shape = shape((2 * length + 4 * filter_rows, half), BF16)
    pair, conv, *own_units = call(
        functools.partial(own_kernel, bits, tile_width),
        [pair_shape, shape((3, length, width), F32)] + [first_shape, later_shape] * len(bits),
        [rows, short_taps, long_filter],
        [pltpu.VMEM((3, EDGE + length, tile_width), F32)],
        cost=40 * length * width,
    )

    def gather(own):
        units = {}
        for bit, block in zip(bits, own):
            arrived = {bit // 2: swap(block, bit)}
            for index, unit in units.items():
                arrived[index ^ bit // 2] = swap(unit, bit)
            units.update(arrived)
        return [units[index] for index in range(1, chips)]

    firsts = gather(own_units[0::2])
    sibling = swap(pair, 1)
    spec, near = call(
        functools.partial(chip_kernel, tile_width, groups, margin),
        [shape((4, 2 * length, width), F32), shape((2, 2 * length, groups), F32)],
        [pair, sibling, firsts_true, forward],
        [],
    )
    unit_specs = call(
        functools.partial(unit_kernel, tile_width, margin),
        [shape((2 * length, half), F32)] * (chips - 1),
        [after(firsts_true, near), forward, *firsts],
        [],
        cost=80 * length * width,
    )
    shares = call(
        functools.partial(filter_grad_kernel, blocks, tile_width),
        [shape((blocks // 4, length, groups), F32)] * 4,
        [spec, near, forward, inverse, *unit_specs],
        [pltpu.VMEM((blocks + 1, 2 * length, groups), F32)],
    )
    laters = gather([after(unit, firsts_true) for unit in own_units[1::2]])
    share, sent = shares[0] + swap(shares[1], 1), shares[2] + swap(shares[3], 1)
    for bit in bits:
        share = after(share, *laters) + swap(sent, bit)
        if bit > 2:
            count = share.shape[0] // 2
            share, sent = share[:count], share[count:]
    units = []
    for first, later in zip(firsts, laters):
        units += [first, later, swap(after(first, share), 1), swap(after(later, share), 1)]
    rows_out = shape((length, width), BF16)
    windows = [
        shape((blocks, 2 * length, groups), F32),
        shape((blocks + 3, length, groups), F32),
    ]

    def results(tiles, extra, outs, out_specs):
        args = [rows, short_taps, long_filter, conv, conv_first, firsts_true, after_rows]
        args += [sibling, spec, forward, inverse, *units]
        count = len(args)
        return call(
            functools.partial(result_kernel, blocks, tile_width, tiles),
            outs,
            args + extra,
            [
                pltpu.VMEM((2, 2 * length, tile_width), F32),
                pltpu.VMEM((2 * EDGE, tile_width), F32),
                pltpu.VMEM((3, length + EDGE, tile_width), F32),
                pltpu.VMEM((4, length, len(tiles) * tile_width), BF16),
                pltpu.SemaphoreType.DMA((4 * len(tiles),)),
            ],
            [VMEM] * count + ([VMEM] * 2 + [HBM] * 4 if extra else []),
            out_specs,
            {count + 2 + index: index for index in range(4)} if extra else {},
            80 * length * len(tiles) * tile_width,
        )

    tiles = width // tile_width
    cuts = [0, max(1, tiles // 4), tiles - tiles // 4, tiles]
    *final, spectra, filter_blocks = results(
        range(cuts[0], cuts[1]), [], [rows_out] * 4 + windows, [HBM] * 4 + [VMEM] * 2
    )
    ready = [final]
    for begin, end in zip(cuts[1:], cuts[2:]):
        if begin < end:
            final = results(
                range(begin, end), [spectra, filter_blocks, *final], [rows_out] * 4, [HBM] * 4
            )
        ready.append(final)

    grad_filter = share[0]
    steps = [1 << index for index in range(chans.bit_length() - 1)]
    for index, step in enumerate(steps):
        arrived = lax.ppermute(grad_filter, "chan", [(i, i ^ step) for i in range(chans)])
        beside = index + len(ready) - len(steps)
        if beside >= 0:
            grad_filter = after(grad_filter, ready[beside][0])
        grad_filter = grad_filter + arrived
    return (*final, grad_filter)


def solution(mesh):
    in_specs = (
        P("seq", "chan"),
        P("seq", "chan"),
        P("seq", "chan"),
        P(None, None, "chan"),
        P("seq", None),
        P("seq", "chan"),
    )
    out_specs = (
        P("seq", "chan"),
        P("seq", "chan"),
        P("seq", "chan"),
        P("seq", "chan"),
        P("seq", None),
    )
    return jax.shard_map(
        per_device, mesh=mesh, in_specs=in_specs, out_specs=out_specs, check_vma=False
    )
```

```python
import functools

import jax
import jax.numpy as jnp
import ml_dtypes
import numpy as np
from jax import lax
from jax.experimental import pallas as pl
from jax.experimental.pallas import tpu as pltpu
from jax.sharding import PartitionSpec as P

F32 = jnp.float32
BF16 = jnp.bfloat16
EDGE = 8
HEAD = 16
VMEM = pl.BlockSpec(memory_space=pltpu.VMEM)
HBM = pl.BlockSpec(memory_space=pltpu.HBM)


def split_table(table):
    high = table.astype(ml_dtypes.bfloat16)
    low = (table - high.astype(np.float64)).astype(ml_dtypes.bfloat16)
    return high, low


def dft_tables(length):
    frequency = np.pi * (2 * np.arange(length) + 1) / (2 * length)
    into = frequency[:, None] * np.arange(length)[None, :]
    high, low = split_table(np.concatenate([np.cos(into), -np.sin(into)], axis=0))
    forward = np.concatenate([high, high, low], axis=1)
    forward = np.pad(forward, ((0, EDGE), (0, 0)))
    back = np.arange(length + EDGE)[:, None] * frequency[None, :]
    high, low = split_table(np.concatenate([np.cos(back), -np.sin(back)], axis=1) / length)
    inverse = np.concatenate([high, high, low], axis=1)
    return jnp.asarray(forward), jnp.asarray(inverse)


def halves(values):
    high = values.astype(BF16)
    return high, (values - high.astype(F32)).astype(BF16)


def table_dot(table, values):
    high, low = halves(values)
    return jnp.dot(
        table, jnp.concatenate([high, low, high], axis=0), preferred_element_type=F32
    )


def tap_sum(rows_ref, first, count, weights):
    total = weights[0:1] * rows_ref[first : first + count]
    for shift in range(1, weights.shape[0]):
        total = total + weights[shift : shift + 1] * rows_ref[first - shift : first - shift + count]
    return total


def put_filter(unit, first, filter_high, filter_low):
    length, groups = filter_high.shape
    width = unit.shape[1]
    rows = length * groups // width
    for tile in range(width // groups):
        lanes = slice(tile * groups, (tile + 1) * groups)
        part = slice(tile * rows, (tile + 1) * rows)
        unit[first : first + rows, lanes] = filter_high[part]
        unit[first + rows : first + 2 * rows, lanes] = filter_low[part]


def get_filter(unit, first, length, groups):
    width = unit.shape[1]
    rows = length * groups // width
    pieces = []
    for tile in range(width // groups):
        lanes = slice(tile * groups, (tile + 1) * groups)
        pieces.append(
            unit[first : first + rows, lanes].astype(F32)
            + unit[first + rows : first + 2 * rows, lanes].astype(F32)
        )
    return jnp.concatenate(pieces, axis=0)


def fetch_kernel(q_hbm, k_hbm, v_hbm, c_hbm, *refs):
    others = refs[:4]
    rows_ref, marks_ref, *other_refs = refs[4:10]
    edge, sems = refs[10:]
    length = q_hbm.shape[0]
    copies = [
        pltpu.make_async_copy(source, rows_ref.at[index], sems.at[index])
        for index, source in enumerate((q_hbm, k_hbm, v_hbm, c_hbm))
    ]
    copies += [
        pltpu.make_async_copy(source, target, sems.at[4 + index])
        for index, (source, target) in enumerate(zip(others, other_refs))
    ]
    for copy in copies:
        copy.start()
    for copy in copies[:4]:
        copy.wait()
    margin = others[0].shape[1] - 1
    edge[...] = jnp.zeros(edge.shape, F32)
    for p in range(4):
        first = rows_ref[p, 0:HEAD].astype(F32)
        edge[(3 + p) * margin : (4 + p) * margin] = first[0:margin]
        if p < 3:
            last = rows_ref[p, length - HEAD :].astype(F32)
            edge[p * margin : (p + 1) * margin] = last[HEAD - margin :]
    marks_ref[...] = edge[...].astype(BF16)
    for copy in copies[4:]:
        copy.wait()


def own_kernel(bits, tile_width, rows_ref, taps_ref, filter_ref, pair_ref, conv_ref, *refs):
    unit_refs, window = refs[:-1], refs[-1]
    parts_out = len(unit_refs) // len(bits)
    length, width = rows_ref.shape[1:]
    half = width // 2
    me = lax.axis_index("seq")
    filter_high, filter_low = halves(filter_ref[...])
    put_filter(pair_ref, 4 * length, filter_high, filter_low)
    for later in unit_refs[1::parts_out]:
        put_filter(later, 2 * length, filter_high, filter_low)
    window[:, 0:EDGE] = jnp.zeros((3, EDGE, tile_width), F32)
    for tile in range(width // tile_width):
        lanes = slice(tile * tile_width, (tile + 1) * tile_width)
        convs = []
        for p in range(3):
            window[p, EDGE:] = rows_ref[p, :, lanes].astype(F32)
            conv = tap_sum(window.at[p], EDGE, length, taps_ref[p, :, lanes])
            conv_ref[p, :, lanes] = conv
            convs.append(conv)
        incoming = rows_ref[3, :, lanes].astype(F32)
        parts = [*halves(convs[1] * convs[2]), *halves(incoming * convs[0])]
        for index, part in enumerate(parts):
            pair_ref[index * length : (index + 1) * length, lanes] = part
        in_half = tile * tile_width // half
        lanes_half = slice(tile * tile_width % half, tile * tile_width % half + tile_width)
        for index, bit in enumerate(bits):
            low_side = (me // bit) % 2 == 0
            first, *laters = unit_refs[parts_out * index : parts_out * (index + 1)]
            cut = laters[0].shape[1]
            later = laters[lanes_half.start // cut]
            lanes_later = slice(lanes_half.start % cut, lanes_half.start % cut + tile_width)
            targets = [(first, lanes_half), (later, lanes_later)]
            (low, lanes_low), (high, lanes_high) = targets if in_half == 0 else targets[::-1]

            @pl.when(low_side)
            def _():
                low[0:length, lanes_low] = parts[0]
                low[length : 2 * length, lanes_low] = parts[1]

            @pl.when(jnp.logical_not(low_side))
            def _():
                high[0:length, lanes_high] = parts[2]
                high[length : 2 * length, lanes_high] = parts[3]


def first_kernel(marks_refs, taps_ref, own_marks, *refs):
    arrived = refs[:marks_refs]
    firsts_ref, conv_ref, after_ref, marks, convs, window = refs[marks_refs:]
    blocks = firsts_ref.shape[0]
    me = lax.axis_index("seq")
    margin = taps_ref.shape[1] - 1
    nothing = jnp.zeros(marks.shape[1:], F32)
    marks[0] = nothing
    marks[blocks + 1] = nothing
    marks[me + 1] = own_marks[...].astype(F32)
    index = 1
    for ref in arrived:
        for place in range(ref.shape[0] // HEAD):
            marks[(me ^ index_of(index, blocks)) + 1] = ref[
                place * HEAD : (place + 1) * HEAD
            ].astype(F32)
            index += 1
    window[...] = jnp.zeros(window.shape, F32)
    convs[blocks] = jnp.zeros(convs.shape[1:], F32)
    for block in range(blocks):
        for p in range(3):
            window[EDGE - margin : EDGE] = marks[block, p * margin : (p + 1) * margin]
            window[EDGE : EDGE + margin] = marks[block + 1, (3 + p) * margin : (4 + p) * margin]
            convs[block, p] = tap_sum(window, EDGE, EDGE, taps_ref[p])
        window[EDGE : EDGE + margin] = marks[block + 1, 6 * margin : 7 * margin]
        firsts_ref[block, 0] = convs[block, 1] * convs[block, 2]
        firsts_ref[block, 1] = window[EDGE:] * convs[block, 0]
    conv_ref[...] = convs[me]
    after_ref[0:2] = convs[me + 1, 1:3]
    window[EDGE : EDGE + margin] = marks[me + 2, 6 * margin : 7 * margin]
    after_ref[2] = window[EDGE:]


def index_of(count, blocks):
    order, bit = [0], blocks // 2
    while bit:
        order += [index ^ bit for index in order]
        bit //= 2
    return order[count]


def with_first(margin, first, rows):
    true = jnp.concatenate([first, jnp.zeros((HEAD - EDGE, first.shape[1]), F32)], axis=0)
    row = lax.broadcasted_iota(jnp.int32, true.shape, 0)
    return jnp.where(row < margin, true, rows)


def spectrum(forward, margin, first, ref, place, lanes):
    length = forward.shape[1] // 3
    parts = []
    for index, part in enumerate(halves(first)):
        begin = place + index * length
        head = with_first(margin, part.astype(F32), ref[begin : begin + HEAD, lanes].astype(F32))
        parts += [head.astype(BF16), ref[begin + HEAD : begin + length, lanes]]
    return jnp.dot(
        forward, jnp.concatenate([*parts, *parts[0:2]], axis=0), preferred_element_type=F32
    )


def cross_add(cross, distance, early, late, groups):
    length = early.shape[0] // 2
    e_re, e_im = early[0:length], early[length:]
    l_re, l_im = late[0:length], late[length:]
    re = e_re * l_re + e_im * l_im
    im = e_re * l_im - e_im * l_re
    parts = range(early.shape[1] // groups)
    cross[distance, 0:length] += sum(re[:, p * groups : (p + 1) * groups] for p in parts)
    cross[distance, length:] += sum(im[:, p * groups : (p + 1) * groups] for p in parts)


def chip_kernel(
    tile_width,
    groups,
    margin,
    own_ref,
    other_ref,
    firsts_ref,
    forward_ref,
    spec_ref,
    cross_ref,
):
    length = forward_ref.shape[1] // 3
    width = own_ref.shape[1]
    me = lax.axis_index("seq")
    core = me % 2
    forward = forward_ref[0 : 2 * length]
    cross_ref[...] = jnp.zeros(cross_ref.shape, F32)

    def one_tile(step, carry):
        lanes = pl.ds(pl.multiple_of(step * tile_width, tile_width), tile_width)
        for ref, slot, block in ((own_ref, core, me), (other_ref, 1 - core, me ^ 1)):
            for kind in range(2):
                first = firsts_ref[block, kind, :, lanes]
                spec_ref[2 * kind + slot, :, lanes] = spectrum(
                    forward, margin, first, ref, 2 * kind * length, lanes
                )
        cross_add(cross_ref, 0, spec_ref[core, :, lanes], spec_ref[2 + core, :, lanes], groups)

        @pl.when(2 * step * tile_width // width == core)
        def _():
            cross_add(cross_ref, 1, spec_ref[0, :, lanes], spec_ref[3, :, lanes], groups)

        return carry

    lax.fori_loop(0, width // tile_width, one_tile, 0)


def unit_kernel(tile_width, margin, firsts_ref, forward_ref, *refs):
    others = len(refs) // 2
    length = forward_ref.shape[1] // 3
    half = refs[0].shape[1]
    me = lax.axis_index("seq")
    core, chip = me % 2, me // 2
    forward = forward_ref[0 : 2 * length]
    for index, (unit, spec_ref) in enumerate(zip(refs[:others], refs[others:])):
        other = chip ^ (index + 1)
        kind = jnp.where(other < chip, 0, 1)
        for tile in range(half // tile_width):
            start = tile * tile_width
            lanes = slice(start, start + tile_width)
            wide_lanes = pl.ds(pl.multiple_of(kind * half + start, tile_width), tile_width)
            first = firsts_ref[2 * other + core, kind, :, wide_lanes]
            spec_ref[:, lanes] = spectrum(forward, margin, first, unit, 0, lanes)


def filter_grad_kernel(
    blocks,
    tile_width,
    spec_ref,
    near_ref,
    forward_ref,
    inverse_ref,
    *refs,
):
    chips = blocks // 2
    units = refs[: chips - 1]
    gf_refs, cross = refs[chips - 1 : -1], refs[-1]
    length = forward_ref.shape[1] // 3
    groups = near_ref.shape[2]
    half = spec_ref.shape[2] // 2
    me = lax.axis_index("seq")
    core, chip = me % 2, me // 2
    cross[0:2] = near_ref[...]
    cross[2:] = jnp.zeros((blocks - 1, 2 * length, groups), F32)
    for index, unit in enumerate(units):
        other = chip ^ (index + 1)

        def one_tile(step, carry):
            start = pl.multiple_of(step * tile_width, tile_width)
            lanes = pl.ds(start, tile_width)
            kind = jnp.where(other < chip, 0, 1)
            wide_lanes = pl.ds(pl.multiple_of(kind * half + start, tile_width), tile_width)
            spec = unit[:, lanes]

            @pl.when(other < chip)
            def _():
                for slot in range(2):
                    distance = 2 * chip + slot - (2 * other + core)
                    cross_add(cross, distance, spec, spec_ref[2 + slot, :, wide_lanes], groups)

            @pl.when(other > chip)
            def _():
                for slot in range(2):
                    distance = 2 * other + core - (2 * chip + slot)
                    cross_add(cross, distance, spec_ref[slot, :, wide_lanes], spec, groups)

            return carry

        lax.fori_loop(0, half // tile_width, one_tile, 0)

    inverse = inverse_ref[0:length]
    sign = signs(length, groups)
    for place in range(blocks):
        block = me ^ place
        re = cross[block, 0:length] + sign * cross[block + 1, length:]
        im = cross[block, length:] - sign * cross[block + 1, 0:length]
        part = place // chips * 2 + place % 2
        gf_refs[part][place % chips // 2] = table_dot(inverse, jnp.concatenate([re, im], axis=0))


def signs(length, groups):
    row = lax.broadcasted_iota(jnp.int32, (length, groups), 0)
    return jnp.where(row % 2 == 0, 1.0, -1.0)


def result_kernel(blocks, tile_width, tiles, fresh_windows, *refs):
    others = blocks // 2 - 1
    (
        rows_ref,
        taps_ref,
        filter_ref,
        conv_ref,
        conv_first,
        firsts_ref,
        after_ref,
        other_ref,
        spec_ref,
        forward_ref,
        inverse_ref,
    ) = refs[:11]
    refs = refs[11:]
    units = [refs[4 * index : 4 * index + 4] for index in range(others)]
    refs = refs[4 * others :]
    if fresh_windows:
        outs, (spectra, filter_rows) = refs[:4], refs[4:6]
        refs = refs[6:]
    else:
        spectra, filter_rows = refs[:2]
        outs = refs[6:10]
        refs = refs[10:]
    acc, fix, grads, rows_out, sems = refs
    length, width = rows_ref.shape[1:]
    groups = filter_ref.shape[1]
    half = width // 2
    margin = taps_ref.shape[1] - 1
    me = lax.axis_index("seq")
    core, chip = me % 2, me // 2
    forward, inverse = forward_ref[0 : 2 * length], inverse_ref[...]

    if fresh_windows:
        sign = signs(length, groups)
        for edge in (0, 1, blocks + 2):
            filter_rows[edge] = jnp.zeros((length, groups), F32)
        filter_rows[me + 2] = filter_ref[...]
        filter_rows[(me ^ 1) + 2] = get_filter(other_ref, 4 * length, length, groups)
        for index, unit in enumerate(units):
            block = me ^ (2 * (index + 1))
            filter_rows[block + 2] = get_filter(unit[1], 2 * length, length, groups)
            filter_rows[(block ^ 1) + 2] = get_filter(unit[3], 2 * length, length, groups)
        previous = None
        for distance in range(blocks):
            own = table_dot(forward, filter_rows[distance + 2])
            if previous is None:
                spectra[distance] = own
            else:
                spectra[distance, 0:length] = own[0:length] - sign * previous[length:]
                spectra[distance, length:] = own[length:] + sign * previous[0:length]
            previous = own

    def wide(values):
        return jnp.concatenate([values] * (tile_width // groups), axis=1)

    def filter_row(block, row):
        return wide(filter_rows[block + 2, pl.ds(row, 1)])

    def add_lower(distance, signal, spec, fresh=False):
        re, im = spec[0:length], spec[length:]
        h_re, h_im = wide(spectra[distance, 0:length]), wide(spectra[distance, length:])
        new_re = h_re * re - h_im * im
        new_im = h_re * im + h_im * re
        acc[0, 0:length] = new_re if fresh else acc[0, 0:length] + new_re
        acc[0, length:] = new_im if fresh else acc[0, length:] + new_im
        near = filter_row(distance + 1, 0) + filter_row(distance - 1, 0)
        far = filter_row(distance + 1, 1) + filter_row(distance - 1, 1)
        fix[0:1] += signal[0:1] * near
        fix[1:2] += signal[0:1] * far + signal[1:2] * near

    def add_upper(distance, signal, spec, fresh=False):
        re, im = spec[0:length], spec[length:]
        h_re, h_im = wide(spectra[distance, 0:length]), wide(spectra[distance, length:])
        new_re = h_re * re + h_im * im
        new_im = h_re * im - h_im * re
        acc[1, 0:length] = new_re if fresh else acc[1, 0:length] + new_re
        acc[1, length:] = new_im if fresh else acc[1, length:] + new_im
        fix[EDGE + 1 : EDGE + 2] += signal[0:1] * (
            filter_row(distance - 2, length - 1) + filter_row(distance, length - 1)
        )

    copies = []
    for count, tile in enumerate(tiles):
        start = tile * tile_width
        in_half = start // half
        lanes = slice(start, start + tile_width)
        lanes_half = slice(start % half, start % half + tile_width)
        place = start % half % units[0][1].shape[1]
        lanes_later = slice(place, place + tile_width)
        lanes_out = slice(count * tile_width, (count + 1) * tile_width)
        weights = [taps_ref[p, :, lanes] for p in range(3)]
        fix[...] = jnp.zeros(fix.shape, F32)

        add_lower(0, firsts_ref[me, 0, :, lanes], spec_ref[core, :, lanes], True)
        add_upper(0, firsts_ref[me, 1, :, lanes], spec_ref[2 + core, :, lanes], True)

        @pl.when(core == 1)
        def _():
            add_lower(1, firsts_ref[me - 1, 0, :, lanes], spec_ref[0, :, lanes])

        @pl.when(core == 0)
        def _():
            add_upper(1, firsts_ref[me + 1, 1, :, lanes], spec_ref[3, :, lanes])

        for index, unit in enumerate(units):
            other = chip ^ (index + 1)
            for side in range(2):
                first, later = unit[2 * side : 2 * side + 2]
                bodies = [(first, lanes_half), (later, lanes_later)]
                (body_low, lanes_low), (body_high, lanes_high) = (
                    bodies if in_half == 0 else bodies[::-1]
                )
                block = 2 * other + (core if side == 0 else 1 - core)

                @pl.when(other < chip)
                def _():
                    signal = firsts_ref[block, 0, :, lanes]
                    spec = spectrum(forward, margin, signal, body_low, 0, lanes_low)
                    add_lower(me - block, signal, spec)

                @pl.when(other > chip)
                def _():
                    signal = firsts_ref[block, 1, :, lanes]
                    spec = spectrum(forward, margin, signal, body_high, 0, lanes_high)
                    add_upper(block - me, signal, spec)

        after_key, after_value, after_incoming = [
            after_ref[p, :, lanes][0:margin] for p in range(3)
        ]
        gated = after_key * after_value
        zero_lag, one_lag = filter_row(0, 0), filter_row(0, 1)
        fix[0:1] += gated[0:1] * zero_lag
        fix[1:2] += gated[1:2] * zero_lag + gated[0:1] * one_lag

        long_conv = table_dot(inverse, acc[0])
        gated_grad = table_dot(inverse, acc[1])
        query_conv, key_conv, value_conv = [
            jnp.concatenate(
                [
                    with_first(margin, conv_first[p, :, lanes], conv_ref[p, 0:HEAD, lanes]),
                    conv_ref[p, HEAD:, lanes],
                ],
                axis=0,
            )
            for p in range(3)
        ]
        incoming = rows_ref[3, :, lanes].astype(F32)
        beyond = slice(length, length + margin)
        grad_edge = gated_grad[beyond] + fix[EDGE : EDGE + margin]
        grads[0, 0:length] = incoming * long_conv[0:length]
        grads[0, beyond] = after_incoming * (long_conv[beyond] + fix[0:margin])
        grads[1, 0:length] = gated_grad[0:length] * value_conv
        grads[1, beyond] = grad_edge * after_value
        grads[2, 0:length] = gated_grad[0:length] * key_conv
        grads[2, beyond] = grad_edge * after_key
        rows_out[0, :, lanes_out] = (query_conv * long_conv[0:length]).astype(BF16)
        for p in range(3):
            total = weights[p][0:1] * grads[p, 0:length]
            for shift in range(1, margin + 1):
                total = total + weights[p][shift : shift + 1] * grads[p, shift : shift + length]
            rows_out[1 + p, :, lanes_out] = total.astype(BF16)
        for p, out in enumerate(outs):
            copy = pltpu.make_async_copy(
                rows_out.at[p, :, lanes_out], out.at[:, lanes], sems.at[4 * count + p]
            )
            copy.start()
            copies.append(copy)
    for copy in copies:
        copy.wait()


def per_device(query_rows, key_rows, value_rows, short_taps, long_filter, cotangent):
    length, width = query_rows.shape
    groups = long_filter.shape[1]
    blocks = lax.axis_size("seq")
    chans = lax.axis_size("chan")
    chips, half = blocks // 2, width // 2
    margin = short_taps.shape[1] - 1
    tile_width = min(half, 256)
    bits = []
    while 2 << len(bits) < blocks:
        bits.append(2 << len(bits))
    bits.reverse()
    forward, inverse = dft_tables(length)
    shape = jax.ShapeDtypeStruct

    def swap(block, bit):
        return lax.ppermute(block, "seq", [(i, i ^ bit) for i in range(blocks)])

    def call(kernel, outs, args, scratch, in_specs=None, out_specs=None, aliases={}, cost=1):
        return list(
            pl.pallas_call(
                kernel,
                out_shape=outs,
                in_specs=in_specs or [VMEM] * len(args),
                out_specs=out_specs or [VMEM] * len(outs),
                scratch_shapes=scratch,
                input_output_aliases=aliases,
                compiler_params=pltpu.CompilerParams(vmem_limit_bytes=40 * 1024 * 1024),
                cost_estimate=pl.CostEstimate(flops=1, bytes_accessed=cost, transcendentals=0),
            )(*args)
        )

    def after(value, *others):
        return lax.optimization_barrier((value, *others))[0]

    rows, marks, short_taps, long_filter, forward, inverse = call(
        fetch_kernel,
        [
            shape((4, length, width), BF16),
            shape((HEAD, width), BF16),
            shape(short_taps.shape, F32),
            shape(long_filter.shape, F32),
            shape(forward.shape, BF16),
            shape(inverse.shape, BF16),
        ],
        [
            pltpu.with_memory_space_constraint(array, pltpu.HBM)
            for array in (
                query_rows,
                key_rows,
                value_rows,
                cotangent,
                short_taps,
                long_filter,
                forward,
                inverse,
            )
        ],
        [pltpu.VMEM((HEAD, width), F32), pltpu.SemaphoreType.DMA((8,))],
        [HBM] * 8,
    )
    all_marks = []
    for bit in bits + [1]:
        all_marks.append(swap(jnp.concatenate([marks] + all_marks, axis=0), bit))
    firsts_true, conv_first, after_rows = call(
        functools.partial(first_kernel, len(all_marks)),
        [
            shape((blocks, 2, EDGE, width), F32),
            shape((3, EDGE, width), F32),
            shape((3, EDGE, width), F32),
        ],
        [short_taps, marks, *all_marks],
        [
            pltpu.VMEM((blocks + 2, HEAD, width), F32),
            pltpu.VMEM((blocks + 1, 3, EDGE, width), F32),
            pltpu.VMEM((2 * EDGE, width), F32),
        ],
        cost=32 * length * width,
    )
    filter_rows = length * groups // width
    pair_shape = shape((4 * length + 2 * filter_rows, width), BF16)
    first_shape = shape((2 * length, half), BF16)
    half_tiles = half // tile_width
    cut_tiles = (half_tiles + 1) // 2
    cut = cut_tiles * tile_width
    later_shapes = [shape((2 * length + 2 * length * groups // cut, cut), BF16)]
    if cut < half:
        later_shapes.append(shape((2 * length, half - cut), BF16))
    pair, conv, *own_units = call(
        functools.partial(own_kernel, bits, tile_width),
        [pair_shape, shape((3, length, width), F32)] + [first_shape, *later_shapes] * len(bits),
        [rows, short_taps, long_filter],
        [pltpu.VMEM((3, EDGE + length, tile_width), F32)],
        cost=40 * length * width,
    )

    def gather(own):
        units = {}
        for bit, block in zip(bits, own):
            arrived = {bit // 2: swap(block, bit)}
            for index, unit in units.items():
                arrived[index ^ bit // 2] = swap(unit, bit)
            units.update(arrived)
        return [units[index] for index in range(1, chips)]

    parts_out = 1 + len(later_shapes)
    firsts = gather(own_units[0::parts_out])
    sibling = swap(pair, 1)
    spec, near = call(
        functools.partial(chip_kernel, tile_width, groups, margin),
        [shape((4, 2 * length, width), F32), shape((2, 2 * length, groups), F32)],
        [pair, sibling, firsts_true, forward],
        [],
    )
    unit_specs = call(
        functools.partial(unit_kernel, tile_width, margin),
        [shape((2 * length, half), F32)] * (chips - 1),
        [after(firsts_true, near), forward, *firsts],
        [],
        cost=80 * length * width,
    )
    shares = call(
        functools.partial(filter_grad_kernel, blocks, tile_width),
        [shape((blocks // 4, length, groups), F32)] * 4,
        [spec, near, forward, inverse, *unit_specs],
        [pltpu.VMEM((blocks + 1, 2 * length, groups), F32)],
    )
    laters = [gather([after(unit, firsts_true) for unit in own_units[1::parts_out]])]
    share = after(shares[0], *laters[0]) + swap(shares[1], 1)
    sent = shares[2] + swap(shares[3], 1)
    for bit in bits:
        share = share + swap(sent, bit)
        if bit > 2:
            count = share.shape[0] // 2
            share, sent = share[:count], share[count:]
    if len(later_shapes) > 1:
        laters.append(gather([after(unit, share) for unit in own_units[2::parts_out]]))
    firsts_forwarded = [swap(after(first, share), 1) for first in firsts]

    def units_of(part, behind):
        units = []
        for first, later, forwarded in zip(firsts, laters[part], firsts_forwarded):
            units += [first, later, forwarded, swap(after(later, behind), 1)]
        return units

    rows_out = shape((length, width), BF16)
    windows = [
        shape((blocks, 2 * length, groups), F32),
        shape((blocks + 3, length, groups), F32),
    ]

    def results(tiles, units, extra, outs, out_specs):
        args = [rows, short_taps, long_filter, conv, conv_first, firsts_true, after_rows]
        args += [sibling, spec, forward, inverse, *units]
        count = len(args)
        return call(
            functools.partial(result_kernel, blocks, tile_width, tiles, not extra),
            outs,
            args + extra,
            [
                pltpu.VMEM((2, 2 * length, tile_width), F32),
                pltpu.VMEM((2 * EDGE, tile_width), F32),
                pltpu.VMEM((3, length + EDGE, tile_width), F32),
                pltpu.VMEM((4, length, len(tiles) * tile_width), BF16),
                pltpu.SemaphoreType.DMA((4 * len(tiles),)),
            ],
            [VMEM] * count + ([VMEM] * 2 + [HBM] * 4 if extra else []),
            out_specs,
            {count + 2 + index: index for index in range(4)} if extra else {},
            80 * length * len(tiles) * tile_width,
        )

    units = units_of(0, share)
    *final, spectra, filter_blocks = results(
        range(cut_tiles), units, [], [rows_out] * 4 + windows, [HBM] * 4 + [VMEM] * 2
    )

    def more_results(final, tiles, units):
        extra = [spectra, filter_blocks, *final]
        return results(tiles, units, extra, [rows_out] * 4, [HBM] * 4)

    later_tiles = [
        in_half * half_tiles + tile for in_half in range(2) for tile in range(cut_tiles, half_tiles)
    ]
    grad_filter = share[0]
    ready = [final, more_results(final, range(half_tiles, half_tiles + cut_tiles), units)]

    steps = [1 << index for index in range(chans.bit_length() - 1)]
    if len(laters) > 1 and len(steps) < 2:
        ready.append(more_results(ready[1], later_tiles, units_of(1, grad_filter)))
    for index, step in enumerate(steps):
        beside = index + 3 - len(steps)
        arrived = lax.ppermute(grad_filter, "chan", [(i, i ^ step) for i in range(chans)])
        if beside == 1 and len(laters) > 1:
            ready.append(more_results(ready[1], later_tiles, units_of(1, grad_filter)))
        if 0 <= beside < len(ready):
            grad_filter = after(grad_filter, ready[beside][0])
        grad_filter = grad_filter + arrived
    final = ready[-1]
    return (*final, grad_filter)


def solution(mesh):
    in_specs = (
        P("seq", "chan"),
        P("seq", "chan"),
        P("seq", "chan"),
        P(None, None, "chan"),
        P("seq", None),
        P("seq", "chan"),
    )
    out_specs = (
        P("seq", "chan"),
        P("seq", "chan"),
        P("seq", "chan"),
        P("seq", "chan"),
        P("seq", None),
    )
    return jax.shard_map(
        per_device, mesh=mesh, in_specs=in_specs, out_specs=out_specs, check_vma=False
    )
```
